32 devices in a mesh: batch: 4 (over z), seq: 8 (over y, x, core).
Axes of the slice: x: 2, y: 2, z: 4, core: 2. Of those that a mesh axis runs over, the one named last changes fastest.
Arguments:
- latents: bfloat16 [8, 512, 1024], P('batch', 'seq'), may hold values from -6 to 6
- pixels: bfloat16 [8, 12544, 261], P('batch', 'seq'), may hold values from -6 to 6
- keep_mask: int32 [8, 12544], P('batch', 'seq'), may hold values from 0 to 1, as said below
- gain_attn: float32 [1024], replicated, may hold values from 0.5 to 1.5
- shift_attn: float32 [1024], replicated, may hold values from -2 to 2
- w_query: bfloat16 [1024, 1024], replicated, may hold values from -0.375 to 0.375
- w_key: bfloat16 [261, 1024], replicated, may hold values from -0.375 to 0.375
- w_value: bfloat16 [261, 1024], replicated, may hold values from -0.375 to 0.375
- w_out: bfloat16 [1024, 1024], replicated, may hold values from -2 to 2
- gain_mlp: float32 [1024], replicated, may hold values from 0.5 to 1.5
- shift_mlp: float32 [1024], replicated, may hold values from -2 to 2
- w_up: bfloat16 [1024, 1024], replicated, may hold values from -0.1875 to 0.1875
- bias_up: float32 [1024], replicated, may hold values from -2 to 2
- w_down: bfloat16 [1024, 1024], replicated, may hold values from -0.1875 to 0.1875
- bias_down: float32 [1024], replicated, may hold values from -2 to 2
- cotangent: bfloat16 [8, 512, 1024], P('batch', 'seq'), may hold values from -6 to 6
Outputs:
- new_latents: bfloat16 [8, 512, 1024], P('batch', 'seq')
- latent_grad: float32 [8, 512, 1024], P('batch', 'seq')
- pixel_grad: float32 [8, 12544, 261], P('batch', 'seq')
- grad_gain_attn: float32 [1024], replicated
- grad_shift_attn: float32 [1024], replicated
- grad_w_query: float32 [1024, 1024], replicated
- grad_w_key: float32 [261, 1024], replicated
- grad_w_value: float32 [261, 1024], replicated
- grad_w_out: float32 [1024, 1024], replicated
- grad_gain_mlp: float32 [1024], replicated
- grad_shift_mlp: float32 [1024], replicated
- grad_w_up: float32 [1024, 1024], replicated
- grad_bias_up: float32 [1024], replicated
- grad_w_down: float32 [1024, 1024], replicated
- grad_bias_down: float32 [1024], replicated
The draws below stay inside these ranges and needn't reach their ends.
Inputs may be any that keep to these rules, and one draw needn't show every extreme that they name: `keep_mask`: every image keeps its first pixel; the share of kept pixels differs from one aligned block of 1568 pixels to the next.
All inputs are finite; a program needn't handle non-finite values.
Results may differ from the reference program's by a relative error of at most 0.0169.
Values may be sent and summed in bfloat16 or wider, within the bound.
No kernel may reach another device: no remote copies, remote signals or barrier semaphores. Data moves between devices by JAX's collectives and lax.ppermute only.
A program may use at most 128 MiB of HBM per device.

```python
import jax
import jax.numpy as jnp
from jax import lax

D = 1024
FF = 1024
CIN = 261
LAT = 512
PIX_DEV = 1568
PIX = 12544
IMAGES = 8


def draw_keep_mask(key, part):
    key = jax.random.fold_in(key, 7)
    share_key, roll_key = jax.random.split(key)
    blocks = PIX // PIX_DEV
    percent = jax.random.randint(share_key, (IMAGES, blocks, 1), 20, 96)
    rolled = jax.random.randint(roll_key, (IMAGES, blocks, PIX_DEV), 0, 100)
    kept = (rolled < percent).astype(jnp.int32).reshape(IMAGES, PIX)
    return kept.at[:, 0].set(1)


def block_levels(own_key, dims, shards, smallest, high):
    loudness, own = 1.0, jax.random.fold_in(own_key, 6)
    for axis_at, parts in shards:
        heights = jnp.exp(jax.random.uniform(jax.random.fold_in(own, axis_at), (parts,), jnp.float32, smallest / len(shards), high / len(shards)))
        loudness = loudness * jnp.repeat(heights, dims[axis_at] // parts).reshape([-1 if axis == axis_at else 1 for axis in range(len(dims))])
    return loudness


def bell_draw(rng, shape, scale, limit, shards=(), held_as=jnp.bfloat16):
    level = block_levels(rng, shape, shards, -0.22, 0.18) if shards else 1.0
    drawn = jax.random.normal(rng, shape, jnp.float32) * scale * level
    return jnp.minimum(jnp.maximum(drawn, -limit), limit).astype(held_as)


def setup_inputs(seed: int = 0) -> dict:
    splits = jax.random.split(jax.random.key(seed), 17)
    return {
        "latents": bell_draw(splits[0], (IMAGES, LAT, D), 1.0, 6.0, ((0, 4), (1, 8))),
        "pixels": bell_draw(splits[1], (IMAGES, PIX, CIN), 1.0, 6.0, ((0, 4), (1, 8))),
        "keep_mask": draw_keep_mask(jax.random.fold_in(splits[16], 71), 0),
        "gain_attn": jnp.clip(1.0 + 0.1 * jax.random.normal(splits[3], (D,), jnp.float32), 0.5, 1.5),
        "shift_attn": bell_draw(splits[4], (D,), 0.3, 2.0, (), jnp.float32),
        "w_query": bell_draw(splits[5], (D, D), (D // 4) ** -0.5, 0.375),
        "w_key": bell_draw(splits[6], (CIN, D), CIN ** -0.5, 0.375),
        "w_value": bell_draw(splits[7], (CIN, D), CIN ** -0.5, 0.375),
        "w_out": bell_draw(splits[8], (D, D), (max(1, 128 * D // PIX)) ** -0.5, 2.0),
        "gain_mlp": jnp.clip(1.0 + 0.1 * jax.random.normal(splits[9], (D,), jnp.float32), 0.5, 1.5),
        "shift_mlp": bell_draw(splits[10], (D,), 0.3, 2.0, (), jnp.float32),
        "w_up": bell_draw(splits[11], (D, FF), D ** -0.5, 0.1875),
        "bias_up": bell_draw(splits[12], (FF,), 0.3, 2.0, (), jnp.float32),
        "w_down": bell_draw(splits[13], (FF, D), FF ** -0.5, 0.1875),
        "bias_down": bell_draw(splits[14], (D,), 0.3, 2.0, (), jnp.float32),
        "cotangent": bell_draw(splits[15], (IMAGES, LAT, D), 1.0, 6.0, ((0, 4), (1, 8))),
    }


@jax.custom_vjp
def low(v):
    return lax.optimization_barrier(v.astype(jnp.bfloat16)).astype(jnp.float32)

@jax.custom_vjp
def low_back(v):
    return v

def low_keep(v):
    return (low(v), None)

def low_pass(kept, grad):
    return (grad,)

def back_keep(v):
    return (v, None)

def back_low(kept, grad):
    return (low(grad),)
low.defvjp(low_keep, low_pass)
low_back.defvjp(back_keep, back_low)

def layer_norm(values, gain, shift):
    mean = lax.optimization_barrier(jnp.mean(values, axis=-1, keepdims=True))
    centered = values - mean
    spread = lax.optimization_barrier(jnp.mean(centered * centered, axis=-1, keepdims=True))
    return centered * lax.rsqrt(spread + 1e-05) * gain + shift

def matmul(left, right):
    return jnp.dot(left, right, precision=lax.Precision.HIGHEST)

def one_image(params, latent_rows, pixel_rows, keep_rows):
    gain_attn, shift_attn, w_query, w_key, w_value, w_out, gain_mlp, shift_mlp, w_up, bias_up, w_down, bias_down = params
    normed = low(layer_norm(latent_rows, gain_attn, shift_attn))
    query = low_back(low(matmul(normed, w_query) * D ** (-0.5)))
    keys = low_back(low(matmul(pixel_rows, w_key)))
    values = low_back(low(matmul(pixel_rows, w_value)))
    scores = low_back(matmul(query, keys.T))
    masked = jnp.where(keep_rows[None, :] > 0, scores, -jnp.inf)
    lse = jax.nn.logsumexp(masked, axis=-1, keepdims=True)
    weights = low(jnp.exp(masked - lse))
    attended = low_back(low(matmul(weights, values)))
    resid = latent_rows + low_back(matmul(attended, w_out))
    normed_mlp = low(layer_norm(resid, gain_mlp, shift_mlp))
    pre = low_back(matmul(normed_mlp, w_up) + bias_up)
    act = low(jax.nn.gelu(pre, approximate=False))
    return resid + matmul(act, w_down) + bias_down

def reference(latents, pixels, keep_mask, gain_attn, shift_attn, w_query, w_key, w_value, w_out, gain_mlp, shift_mlp, w_up, bias_up, w_down, bias_down, cotangent):
    params = tuple((p.astype(jnp.float32) for p in (gain_attn, shift_attn, w_query, w_key, w_value, w_out, gain_mlp, shift_mlp, w_up, bias_up, w_down, bias_down)))
    step_fn = jax.checkpoint(one_image)

    def forward(weights_all, latent_all, pixel_all):
        return lax.map(lambda items: step_fn(weights_all, items[0], items[1], items[2]), (latent_all, pixel_all, keep_mask))
    result, pullback = jax.vjp(forward, params, latents.astype(jnp.float32), pixels.astype(jnp.float32))
    param_grads, latent_grad, pixel_grad = pullback(cotangent.astype(jnp.float32))
    return (result.astype(jnp.bfloat16), latent_grad, pixel_grad, param_grads[0], param_grads[1], param_grads[2], param_grads[3], param_grads[4], param_grads[5], param_grads[6], param_grads[7], param_grads[8], param_grads[9], param_grads[10], param_grads[11])
```

```python
import functools

import jax
import jax.numpy as jnp
from jax import lax
from jax.sharding import PartitionSpec as P

f32 = jnp.float32
bf16 = jnp.bfloat16
EPS = 1e-05
DROP = -1e30
ROW_ONE = 0
ROW_LSE = 3
ROW_MASK = 6
ROW_TOP = 7


def dot(a, b, ca, cb):
    return lax.dot_general(a, b, (((ca,), (cb,)), ((), ())), preferred_element_type=f32)


def split3(v):
    hi = lax.reduce_precision(v, 8, 7)
    mid = lax.reduce_precision(v - hi, 8, 7)
    low = v - hi - mid
    return hi.astype(bf16), mid.astype(bf16), low.astype(bf16)


def norm_parts(v):
    mean = jnp.mean(v, axis=-1, keepdims=True)
    centered = v - mean
    spread = jnp.mean(centered * centered, axis=-1, keepdims=True)
    scale = lax.rsqrt(spread + EPS)
    return centered * scale, scale


def norm_back(d_out, hat, scale, gain):
    d_hat = d_out * gain
    mean = jnp.mean(d_hat, axis=-1, keepdims=True)
    along = jnp.mean(d_hat * hat, axis=-1, keepdims=True)
    return scale * (d_hat - mean - hat * along)


def gelu_and_slope(v):
    cdf = 0.5 * (1.0 + lax.erf(v * (0.5**0.5)))
    pdf = jnp.exp(-0.5 * v * v) * (1.0 / (2.0 * jnp.pi) ** 0.5)
    return v * cdf, cdf + v * pdf


def seq_send(v, mask, n):
    return lax.ppermute(v, "seq", [(i, i ^ mask) for i in range(n)])


def batch_send(v, mask, n):
    return lax.ppermute(v, "batch", [(i, i ^ mask) for i in range(n)])


class Comm:
    def __init__(self, n_seq, n_batch):
        self.n_seq, self.n_batch = n_seq, n_batch
        self.chips = n_seq // 2
        self.s = lax.axis_index("seq")
        self.core = lax.rem(self.s, 2)
        self.chip = lax.div(self.s, 2)
        self.z = lax.axis_index("batch")

    def place(self, axis):
        if axis == "chip":
            return self.chip, self.chips, lambda v, m: seq_send(v, 2 * m, self.n_seq)
        return self.z, self.n_batch, lambda v, m: batch_send(v, m, self.n_batch)

    def scatter_sum(self, v, axis, dim=0):
        me, n, send = self.place(axis)
        size = v.shape[dim] // n
        own = lax.dynamic_slice_in_dim(v, me * size, size, dim).astype(f32)
        got = [
            send(lax.dynamic_slice_in_dim(v, (me ^ m) * size, size, dim), m) for m in range(1, n)
        ]
        for piece in got:
            own = own + piece.astype(f32)
        return own.astype(v.dtype)

    def gather(self, v, axis, dim=0):
        me, n, send = self.place(axis)
        size = v.shape[dim]
        shape = list(v.shape)
        shape[dim] = size * n
        out = jnp.zeros(shape, v.dtype)
        got = [v] + [send(v, m) for m in range(1, n)]
        for m, piece in enumerate(got):
            out = lax.dynamic_update_slice_in_dim(out, piece, (me ^ m) * size, dim)
        return out

    def sum_all(self, v, axis):
        _, n, send = self.place(axis)
        got = [send(v, m) for m in range(1, n)]
        total = v.astype(f32)
        for piece in got:
            total = total + piece.astype(f32)
        return total.astype(v.dtype)

    def twin(self, v):
        return seq_send(v, 1, self.n_seq)

    def half(self, v, core, dim):
        size = v.shape[dim] // 2
        return lax.dynamic_slice_in_dim(v, core * size, size, dim)

    def join(self, v, dim):
        other = self.twin(v)
        first = jnp.where(self.core == 0, v, other)
        second = jnp.where(self.core == 0, other, v)
        return jnp.concatenate([first, second], axis=dim)


def shards(
    n_seq,
    n_batch,
    latents,
    pixels,
    keep_mask,
    gain_attn,
    shift_attn,
    w_query,
    w_key,
    w_value,
    w_out,
    gain_mlp,
    shift_mlp,
    w_up,
    bias_up,
    w_down,
    bias_down,
    cotangent,
):
    images, rows, width = latents.shape
    pix, feats = pixels.shape[1:]
    wide = -(-(feats + 8) // 16) * 16
    lanes = images * rows
    scale = width ** (-0.5)
    comm = Comm(n_seq, n_batch)
    x = latents.reshape(lanes, width).astype(f32)
    g = cotangent.reshape(lanes, width)
    g_f = g.astype(f32)

    hat1, scale1 = norm_parts(x)
    normed = (hat1 * gain_attn + shift_attn).astype(bf16)
    query = (dot(normed, w_query, 1, 0) * scale).astype(bf16)
    qk = dot(w_key, query, 1, 1).astype(bf16)
    tail = jnp.zeros((wide - feats, lanes), bf16).at[ROW_MASK].set(1.0)
    qk = jnp.concatenate([qk, tail], axis=0)

    def lay(v):
        return v.reshape(n_seq, wide, images, rows).transpose(2, 1, 0, 3).reshape(images, wide, -1)

    qk_all = lay(lax.all_gather(qk, "seq"))
    bias = jnp.where(keep_mask > 0, 0.0, DROP).astype(bf16)[..., None]
    one = jnp.ones((images, pix, 3), bf16)
    zero = jnp.zeros((images, pix, 3), bf16)
    rest = jnp.zeros((images, pix, wide - feats - 7), bf16)
    pix_x = jnp.concatenate([pixels, one, zero, bias, rest], axis=-1)

    scores = jnp.einsum("ipc,icl->ipl", pix_x, qk_all, preferred_element_type=f32)
    top = jnp.max(scores, axis=1)
    probs = jnp.exp(scores - top[:, None, :]).astype(bf16)
    part = jnp.einsum("ipc,ipl->icl", pix_x, probs, preferred_element_type=f32)

    def unlay(v):
        return v.reshape(images, wide, n_seq, rows).transpose(2, 1, 0, 3).reshape(n_seq, wide, lanes)

    sent = unlay(part.at[:, feats + ROW_TOP].set(top))
    got = lax.all_to_all(sent, "seq", 0, 0)
    tops = got[:, feats + ROW_TOP]
    peak = jnp.max(tops, axis=0)
    share = jnp.exp(tops - peak)
    total = jnp.sum(share * got[:, feats + ROW_ONE], axis=0)
    ctx_t = jnp.sum(share[:, None, :] * got[:, :feats], axis=0) / total
    lse = peak + jnp.log(total)
    ctx = ctx_t.T

    w_vo = dot(w_value, w_out, 1, 0)
    vo_hi = lax.reduce_precision(w_vo, 8, 7)
    vo_lo = (w_vo - vo_hi).astype(bf16)
    vo_hi = vo_hi.astype(bf16)
    ctx_b = ctx.astype(bf16)
    resid = x + dot(ctx_b, vo_hi, 1, 0) + dot(ctx_b, vo_lo, 1, 0)
    hat2, scale2 = norm_parts(resid)
    normed2 = (hat2 * gain_mlp + shift_mlp).astype(bf16)
    pre = dot(normed2, w_up, 1, 0) + bias_up
    act_f, slope = gelu_and_slope(pre)
    act = act_f.astype(bf16)
    new_latents = (resid + dot(act, w_down, 1, 0) + bias_down).astype(bf16)
    d_pre_f = dot(g, w_down, 1, 1) * slope
    d_pre = d_pre_f.astype(bf16)
    d_normed2 = dot(d_pre, w_up, 1, 1)
    d_resid = g_f + norm_back(d_normed2, hat2, scale2, gain_mlp)
    d_resid_b = d_resid.astype(bf16)
    d_ctx = (dot(vo_hi, d_resid_b, 1, 1) + dot(vo_lo, d_resid_b, 1, 1)).astype(bf16)
    delta = jnp.sum(ctx_t * d_ctx.astype(f32), axis=0)
    tail = jnp.stack(list(split3(-delta)) + list(split3(lse)))
    tail = jnp.concatenate([tail, jnp.zeros((wide - feats - 6, lanes), bf16)])
    back = lay(lax.all_gather(jnp.concatenate([d_ctx, tail]), "seq"))

    lse_all = jnp.sum(back[:, feats + ROW_LSE : feats + ROW_LSE + 3].astype(f32), axis=1)
    ratio = jnp.exp(top - lse_all)
    d_probs = jnp.einsum("ipc,icl->ipl", pix_x, back, preferred_element_type=f32)
    d_scores = (probs.astype(f32) * ratio[:, None, :] * d_probs).astype(bf16)
    dq_part = jnp.einsum("ipc,ipl->icl", pix_x, d_scores, preferred_element_type=f32)
    d_ctx_all = (back.astype(f32) * ratio[:, None, :]).astype(bf16)
    pixel_grad = jnp.einsum(
        "ipl,icl->ipc", d_scores, qk_all[:, :feats], preferred_element_type=f32
    ) + jnp.einsum("ipl,icl->ipc", probs, d_ctx_all[:, :feats], preferred_element_type=f32)

    dq_got = lax.all_to_all(unlay(dq_part.astype(bf16)), "seq", 0, 0)
    dq_t = jnp.sum(dq_got.astype(f32), axis=0)
    dq_t = dq_t[:feats] - dq_t[feats + ROW_ONE] * ctx_t
    dqk_b = dq_t.astype(bf16)
    d_query = dot(dqk_b, w_key, 0, 0).astype(bf16)
    d_normed = dot(d_query, w_query, 1, 1) * scale
    latent_grad = d_resid + norm_back(d_normed, hat1, scale1, gain_attn)

    pad = jnp.zeros((wide - feats, lanes), bf16)
    m_part = dot(jnp.concatenate([dqk_b, pad]), normed, 1, 0)
    c_part = dot(jnp.concatenate([ctx_b.T, pad]), d_resid_b, 1, 0)

    def pair(v, dim=0):
        return comm.join(v, dim)

    act2, g2, normed22, d_pre2 = pair(act), pair(g), pair(normed2), pair(d_pre)
    down = dot(comm.half(act2, comm.core, 1), g2, 0, 0).astype(bf16)
    up = dot(normed22, comm.half(d_pre2, comm.core, 1), 0, 0).astype(bf16)
    down = comm.scatter_sum(down, "chip")
    up = comm.scatter_sum(up, "z")
    down = comm.scatter_sum(down, "z")
    up = comm.scatter_sum(up, "chip")
    down = comm.gather(down, "z")
    up = comm.gather(up, "chip")
    down = comm.gather(down, "chip")
    up = comm.gather(up, "z")
    grad_down = comm.join(down, 0).astype(f32)
    grad_up = comm.join(up, 1).astype(f32)

    def small_sum(v):
        mine = comm.half(v, comm.core, 1)
        other = comm.half(v, 1 - comm.core, 1).astype(bf16)
        v = (mine + comm.twin(other).astype(f32)).astype(bf16)
        v = comm.scatter_sum(v, "chip", 1)
        v = comm.sum_all(v, "z")
        v = comm.gather(v, "chip", 1)
        return comm.join(v, 1)[:feats]

    c_sum = small_sum(c_part)
    m_sum = small_sum(m_part)
    grad_value = dot(c_sum, w_out, 1, 1)
    grad_out = dot(w_value, c_sum, 0, 0)
    grad_key = dot(m_sum, w_query, 1, 0) * scale
    grad_query = dot(m_sum, w_key, 0, 0) * scale

    vectors = jnp.stack(
        [
            jnp.sum(d_normed * hat1, axis=0),
            jnp.sum(d_normed, axis=0),
            jnp.sum(d_normed2 * hat2, axis=0),
            jnp.sum(d_normed2, axis=0),
            jnp.sum(d_pre_f.astype(bf16).astype(f32), axis=0),
            jnp.sum(g_f, axis=0),
        ]
    )
    vectors = lax.psum(vectors, ("batch", "seq"))
    shape = (images, rows, width)
    return (
        new_latents.reshape(shape),
        latent_grad.reshape(shape),
        pixel_grad,
        vectors[0],
        vectors[1],
        grad_query,
        grad_key,
        grad_value,
        grad_out,
        vectors[2],
        vectors[3],
        grad_up,
        vectors[4],
        grad_down,
        vectors[5],
    )


def solution(mesh):
    split = P("batch", "seq", None)
    placed = (split, split, P("batch", "seq")) + (P(),) * 12 + (split,)
    return jax.shard_map(
        functools.partial(shards, mesh.shape["seq"], mesh.shape["batch"]),
        mesh=mesh,
        in_specs=placed,
        out_specs=(split, split, split) + (P(),) * 12,
        check_vma=False,
    )
```

```python
import functools

import jax
import jax.numpy as jnp
from jax import lax
from jax.experimental import pallas as pl
from jax.experimental.pallas import tpu as pltpu
from jax.sharding import PartitionSpec as P

f32 = jnp.float32
bf16 = jnp.bfloat16
EPS = 1e-05
DROP = -1e30
ONE, TOP, MASK = 0, 3, 6
VMEM_LIMIT = 56 << 20


def dot(a, b, ca, cb):
    return lax.dot_general(a, b, (((ca,), (cb,)), ((), ())), preferred_element_type=f32)


def shape(dims, dtype):
    return jax.ShapeDtypeStruct(dims, dtype)


def call(body, out, grid=(), ins=None, outs=None, scratch=()):
    kwargs = {}
    if grid:
        kwargs = dict(grid=grid, in_specs=ins, out_specs=outs)
    return pl.pallas_call(
        body,
        out_shape=out,
        scratch_shapes=list(scratch),
        compiler_params=pltpu.CompilerParams(vmem_limit_bytes=VMEM_LIMIT),
        **kwargs,
    )


def whole(dims):
    return pl.BlockSpec(dims, lambda *_: (0,) * len(dims))


def one_of(dims):
    return pl.BlockSpec((1,) + dims, lambda i, *_: (i,) + (0,) * len(dims))


def split3(v):
    hi = v.astype(bf16).astype(f32)
    mid = (v - hi).astype(bf16).astype(f32)
    return hi, mid, v - hi - mid


def position():
    s = lax.axis_index("seq")
    return lax.rem(s, 2), lax.div(s, 2), lax.axis_index("batch")


def slot(start, size):
    return pl.ds(pl.multiple_of(start, size), size)


def tail_rows(rows, lanes):
    at = lax.broadcasted_iota(jnp.int32, (8, lanes), 0)
    tile = jnp.zeros((8, lanes), f32)
    for k, v in rows.items():
        tile = jnp.where(at == k, v, tile)
    return tile


def norm_parts(v):
    mean = jnp.mean(v, axis=-1, keepdims=True)
    centered = v - mean
    spread = jnp.mean(centered * centered, axis=-1, keepdims=True)
    scale = lax.rsqrt(spread + EPS)
    return centered * scale, scale


def norm_back(d_out, hat, scale, gain):
    d_hat = d_out * gain
    mean = jnp.mean(d_hat, axis=-1, keepdims=True)
    along = jnp.mean(d_hat * hat, axis=-1, keepdims=True)
    return scale * (d_hat - mean - hat * along)


def gelu_and_slope(v):
    cdf = 0.5 * (1.0 + lax.erf(v * (0.5**0.5)))
    pdf = jnp.exp(-0.5 * v * v) * (1.0 / (2.0 * 3.141592653589793) ** 0.5)
    return v * cdf, cdf + v * pdf


def chunks(n, size=256):
    return [(a, min(size, n - a)) for a in range(0, n, size)]


def query_kernel(scale, x_ref, gain_ref, shift_ref, wq_ref, wk_ref, qk_ref, hat_ref, pad_ref):
    feats = wk_ref.shape[0]
    wide, lanes = qk_ref.shape
    hat, _ = norm_parts(x_ref[...].astype(f32))
    normed = (hat * gain_ref[...] + shift_ref[...]).astype(bf16)
    hat_ref[...] = hat.astype(bf16)
    query = (dot(normed, wq_ref[...], 1, 0) * scale).astype(bf16)
    pad_ref[...] = jnp.zeros((wide, lanes), f32)
    pad_ref[:feats] = dot(wk_ref[...], query, 1, 1)
    pad_ref[wide - 8 :] = tail_rows({MASK: 1.0}, lanes)
    qk_ref[...] = pad_ref[...].astype(bf16)


def pixel_kernel(pix_ref, keep_ref, x_ref, t_ref, pad_ref):
    feats, n = pix_ref.shape[1:]
    wide = t_ref.shape[1]
    keep = keep_ref[pl.ds(pl.program_id(0), 1), :]
    bias = jnp.where(keep > 0, 0.0, DROP).astype(f32)
    pad_ref[wide - 16 :] = jnp.zeros((16, n), f32)
    pad_ref[:feats] = pix_ref[0].astype(f32)
    pad_ref[wide - 8 :] = tail_rows({ONE: 1.0, ONE + 1: 1.0, ONE + 2: 1.0, MASK: bias}, n)
    t_ref[0] = pad_ref[...].astype(bf16)
    x_ref[0] = pad_ref[...].T.astype(bf16)


def weight_kernel(wv_ref, wo_ref, g_ref, wd_ref, hi_ref, lo_ref, dact_ref, pad_ref):
    feats = wv_ref.shape[0]
    pad_ref[...] = jnp.zeros(pad_ref.shape, f32)
    pad_ref[:feats] = dot(wv_ref[...], wo_ref[...], 1, 0)
    v = pad_ref[...]
    hi = v.astype(bf16)
    hi_ref[...] = hi
    lo_ref[...] = (v - hi.astype(f32)).astype(bf16)
    dact_ref[...] = dot(g_ref[...], wd_ref[...], 1, 1)


def lay_lanes(i, rows, refs, out_ref):
    for k in range(2):

        @pl.when(i == k)
        def _():
            parts = [ref[:, k * rows : (k + 1) * rows] for ref in refs]
            out_ref[...] = jnp.concatenate(parts, axis=1)


def unlay_lanes(i, rows, v, mine_ref, twin_ref):
    blocks = mine_ref.shape[0]
    for k in range(2):

        @pl.when(i == k)
        def _():
            for b in range(2 * blocks):
                ref = (mine_ref, twin_ref)[b // blocks]
                piece = v[:, b * rows : (b + 1) * rows].astype(ref.dtype)
                ref[b % blocks, :, k * rows : (k + 1) * rows] = piece


def attend_kernel(rows, x_ref, t_ref, *refs):
    *sides, p_ref, q_ref, top_ref, pm_ref, pt_ref, s_ref = refs
    i = pl.program_id(0)
    n = x_ref.shape[1]
    wide, lanes = q_ref.shape[1:]
    lay_lanes(i, rows, sides, q_ref.at[0])
    q = q_ref[0]
    top = jnp.full((1, lanes), -jnp.inf, f32)
    for a, size in chunks(n):
        s = dot(x_ref[0, a : a + size], q, 1, 0)
        s_ref[a : a + size] = s
        top = jnp.maximum(top, jnp.max(s, axis=0, keepdims=True))
    total = jnp.zeros((wide, lanes), f32)
    for a, size in chunks(n):
        p = jnp.exp(s_ref[a : a + size] - top).astype(bf16)
        p_ref[0, a : a + size] = p
        total = total + dot(t_ref[0, :, a : a + size], p, 1, 0)
    top_ref[0] = top
    tile = total[wide - 8 :]
    at = lax.broadcasted_iota(jnp.int32, tile.shape, 0)
    tile = jnp.where(at == TOP, top, jnp.where(at == ONE, tile, 0.0))
    unlay_lanes(i, rows, jnp.concatenate([total[: wide - 8], tile], axis=0), pm_ref, pt_ref)


def merge_kernel(a_ref, b_ref, *out_refs):
    blocks, wide, lanes = a_ref.shape
    base = wide - 8
    for k, ref in enumerate(out_refs):
        ta, tb = a_ref[k, pl.ds(base + TOP, 1)], b_ref[k, pl.ds(base + TOP, 1)]
        top = jnp.maximum(ta, tb)
        wa, wb = jnp.exp(ta - top), jnp.exp(tb - top)
        total = a_ref[k, pl.ds(base + ONE, 1)] * wa + b_ref[k, pl.ds(base + ONE, 1)] * wb
        ref[:base] = a_ref[k, :base] * wa + b_ref[k, :base] * wb
        ref[base:] = tail_rows({ONE: total, TOP: top}, lanes)


def mlp_kernel(feats, n_got, keep_ref, *refs):
    got_refs, refs = refs[:n_got], refs[n_got:]
    x_ref, g_ref, hi_ref, lo_ref, gain_ref, shift_ref, wu_ref, bu_ref, wd_ref, bd_ref, dact_ref, *outs = refs
    new_ref, dres_ref, trio_ref, ctx_ref, back_ref, csum_ref = outs
    wide, lanes = keep_ref.shape
    base = wide - 8
    part_refs = (keep_ref, *got_refs)
    parts = [ref[...] for ref in part_refs]
    tops = [ref[pl.ds(base + TOP, 1)] for ref in part_refs]
    sums = [ref[pl.ds(base + ONE, 1)] for ref in part_refs]
    peak = functools.reduce(jnp.maximum, tops)
    total = jnp.zeros((1, lanes), f32)
    ctx = jnp.zeros((wide, lanes), f32)
    for v, top, part in zip(parts, tops, sums):
        share = jnp.exp(top - peak)
        total = total + part * share
        ctx = ctx + v * share
    ctx = ctx / total
    lse = peak + jnp.log(total)
    row = lax.broadcasted_iota(jnp.int32, (wide, lanes), 0)
    ctx = jnp.where(row < feats, ctx, 0.0)
    ctx_ref[...] = ctx
    ctx_b = ctx.astype(bf16)
    resid = x_ref[...].astype(f32) + dot(ctx_b, hi_ref[...], 0, 0) + dot(ctx_b, lo_ref[...], 0, 0)
    hat, scale = norm_parts(resid)
    normed = (hat * gain_ref[...] + shift_ref[...]).astype(bf16)
    trio_ref[0] = normed
    pre = dot(normed, wu_ref[...], 1, 0) + bu_ref[...]
    act_f, slope = gelu_and_slope(pre)
    act = act_f.astype(bf16)
    trio_ref[1] = act
    d_pre = (dact_ref[...] * slope).astype(bf16)
    trio_ref[2] = d_pre
    d_normed = dot(d_pre, wu_ref[...], 1, 1)
    g = g_ref[...].astype(f32)
    d_resid = g + norm_back(d_normed, hat, scale, gain_ref[...])
    dres_ref[...] = d_resid
    d_resid_b = d_resid.astype(bf16)
    d_ctx = (dot(hi_ref[...], d_resid_b, 1, 1) + dot(lo_ref[...], d_resid_b, 1, 1)).astype(bf16)
    delta = jnp.sum(ctx * d_ctx.astype(f32), axis=0, keepdims=True)
    rows = {ONE + k: -v for k, v in enumerate(split3(delta))}
    rows.update({TOP + k: v for k, v in enumerate(split3(lse))})
    back_ref[...] = jnp.concatenate([d_ctx[:base], tail_rows(rows, lanes).astype(bf16)], axis=0)
    new_ref[...] = (resid + dot(act, wd_ref[...], 1, 0) + bd_ref[...]).astype(bf16)
    c = dot(ctx_b, d_resid_b, 1, 0)
    vectors = {
        0: jnp.sum(d_normed * hat, axis=0, keepdims=True),
        1: jnp.sum(d_normed, axis=0, keepdims=True),
        2: jnp.sum(d_pre.astype(f32), axis=0, keepdims=True),
        3: jnp.sum(g, axis=0, keepdims=True),
    }
    csum_ref[...] = jnp.concatenate([c[:base], tail_rows(vectors, c.shape[1])], axis=0)


def back_kernel(rows, n, cut, _, x_ref, t_ref, p_ref, top_ref, c_ref, *refs):
    sides, hats, outs = refs[: 2 * n], refs[2 * n : 4 * n], refs[4 * n :]
    ds_ref, dc_ref, dm_ref, dt_ref, *outs = outs
    both_ref, b_ref, hat_ref = outs[-3:]
    i = pl.program_id(0)
    pix = x_ref.shape[1]
    wide, lanes = b_ref.shape
    base = wide - 8
    lay_lanes(i, rows, sides, b_ref)
    for k in range(2):

        @pl.when(i == k)
        def _():
            for b, ref in enumerate(hats):
                hat_ref[b * rows : (b + 1) * rows] = ref[k * rows : (k + 1) * rows]

    b = b_ref[...]
    tail = b[wide - 16 :].astype(f32)[8:]
    at = lax.broadcasted_iota(jnp.int32, tail.shape, 0)
    lse = jnp.sum(jnp.where((at >= TOP) & (at < TOP + 3), tail, 0.0), axis=0, keepdims=True)
    ratio = jnp.exp(top_ref[0] - lse)
    dc_ref[0] = (b.astype(f32) * ratio).astype(bf16)
    total = jnp.zeros((wide, lanes), f32)
    for a, size in chunks(pix):
        d = dot(x_ref[0, a : a + size], b, 1, 0)
        ds = (p_ref[0, a : a + size].astype(f32) * (d * ratio)).astype(bf16)
        ds_ref[0, a : a + size] = ds
        total = total + dot(t_ref[0, :, a : a + size], ds, 1, 0)
    total_b = total.astype(bf16)
    m = dot(total_b, hat_ref[...], 1, 0)
    sums = dot(jnp.ones((8, lanes), bf16), total_b, 1, 1)
    sums = jnp.concatenate([sums, jnp.zeros((8, m.shape[1] - wide), f32)], axis=1)
    at = lax.broadcasted_iota(jnp.int32, sums.shape, 0)
    sums = jnp.where(at == 0, sums, 0.0)

    @pl.when(i == 0)
    def _():
        both_ref[:base] = m[:base]
        both_ref[base:wide] = sums
        both_ref[wide:] = c_ref[...]

    @pl.when(i > 0)
    def _():
        both_ref[:base] += m[:base]
        both_ref[base:wide] += sums

    unlay_lanes(i, rows, total, dm_ref.at[:, :wide], dt_ref.at[:, :wide])
    if cut:

        @pl.when(i == pl.num_programs(0) - 1)
        def _():
            core, chip, _ = position()
            part = dm_ref.shape[2]
            for b in range(n):
                at = (chip ^ b) * part
                dm_ref[b, wide:] = both_ref[:, slot(core * n * part + at, part)]
                dt_ref[b, wide:] = both_ref[:, slot((1 - core) * n * part + at, part)].astype(bf16)


def pixel_grad_kernel(feats, ds_ref, p_ref, q_ref, dc_ref, out_ref):
    for i in range(ds_ref.shape[0]):
        v = dot(q_ref[i], ds_ref[i], 1, 1) + dot(dc_ref[i], p_ref[i], 1, 1)
        out_ref[:, i, :] = v[:feats]


def latent_kernel(scale, dq_ref, ctx_ref, x_ref, gain_ref, wk_ref, wq_ref, dres_ref, lat_ref):
    feats = wk_ref.shape[0]
    wide, lanes = dq_ref.shape
    d = dq_ref[...] - dq_ref[pl.ds(wide - 8 + ONE, 1)] * ctx_ref[...]
    d = d[:feats].astype(bf16)
    d_query = dot(d, wk_ref[...], 0, 0).astype(bf16)
    d_normed = dot(d_query, wq_ref[...], 1, 1) * scale
    hat, spread = norm_parts(x_ref[...].astype(f32))
    lat_ref[...] = dres_ref[...] + norm_back(d_normed, hat, spread, gain_ref[...])


def weight_grad_kernel(n_batch, trio_ref, twin_ref, g_ref, g2_ref, token_ref, *refs):
    token_ref[...] = jnp.zeros(token_ref.shape, f32)
    core, chip, _ = position()
    tall, half = refs[0].shape
    tall, size = tall // 2, tall // 2 // n_batch
    cols = slot(core * half, half)
    d_pre = jnp.concatenate([trio_ref[2, :, cols], twin_ref[2, :, cols]], axis=0)
    g = jnp.concatenate([g_ref[:, cols], g2_ref[:, cols]], axis=0)
    for m, ref in enumerate(refs):
        rows = slot((chip ^ m) * tall, tall)
        for h, (a, right) in enumerate(((0, d_pre), (1, g))):
            left = jnp.concatenate([trio_ref[a, :, rows], twin_ref[a, :, rows]], axis=0)
            v = dot(left, right, 0, 0).astype(ref.dtype)
            for z in range(n_batch):
                at = (2 * z + h) * size
                ref[at : at + size] = v[z * size : (z + 1) * size]


def total(refs):
    v = refs[0][...].astype(f32)
    for ref in refs[1:]:
        v = v + ref[...].astype(f32)
    return v


def split_kernel(n, *refs):
    z = position()[2]
    out_refs, sum_ref = refs[n:-1], refs[-1]
    sum_ref[...] = total(refs[:n])
    size = out_refs[0].shape[0]
    for j, ref in enumerate(out_refs):
        ref[...] = sum_ref[slot(lax.rem(z + j, len(out_refs)) * size, size)].astype(ref.dtype)


def fold_kernel(n, mine_ref, twin_ref, keep_ref, *out_refs):
    keep_ref[...] = mine_ref[0] + twin_ref[0].astype(f32)
    for m, ref in enumerate(out_refs, 1):
        ref[...] = (mine_ref[m] + twin_ref[m].astype(f32)).astype(bf16)


def join_kernel(n, keep_ref, *refs):
    x_refs, u_refs, (dq_ref, out_ref) = refs[: n - 1], refs[n - 1 : -2], refs[-2:]
    wide, part = dq_ref.shape
    base = keep_ref.shape[0] - wide
    v = keep_ref[...]
    for ref in x_refs:
        v = v + ref[...].astype(f32)
    dq_ref[...] = v[:wide]
    out_ref[:base] = v[wide:].astype(bf16)
    v = total(u_refs).astype(bf16)
    for q in range(n):
        at = base + q * v.shape[0]
        out_ref[at : at + v.shape[0]] = v[:, q * part : (q + 1) * part]


def stack_kernel(z_count, *refs):
    z_refs, (sum_ref, own_ref) = refs[:z_count], refs[z_count:]
    rows = sum_ref.shape[0]
    v = z_refs[0][:rows].astype(f32)
    for ref in z_refs[1:]:
        v = v + ref[:rows].astype(f32)
    sum_ref[...] = v.astype(bf16)
    for j, ref in enumerate(z_refs):
        own_ref[j] = ref[rows:]


def place_kernel(n, *refs):
    core, chip, z = position()
    out_refs = refs[-2:]
    n_batch, tall, part = refs[0].shape
    pieces = out_refs[0].shape[1] // 2 // part
    size = tall // pieces // 2
    for side, col in enumerate((core, 1 - core)):
        for m, ref in enumerate(refs[side * n : (side + 1) * n]):
            for j in range(n_batch):
                rows = slot(((chip ^ m) * n_batch + lax.rem(z + n_batch - j, n_batch)) * size, size)
                for q in range(pieces):
                    cols = slot((col * pieces + q) * part, part)
                    for h, out_ref in enumerate(out_refs):
                        at = (2 * q + h) * size
                        out_ref[rows, cols] = ref[j, at : at + size].astype(f32)


def final_kernel(scale, n, *refs):
    pieces, refs = refs[: max(2 * n, 1)], refs[max(2 * n, 1) :]
    wq_ref, wk_ref, wv_ref, wo_ref, gain_ref, shift_ref, *refs = refs
    gq_ref, gk_ref, gv_ref, go_ref, gg_ref, gs_ref, *refs = refs
    vector_refs, (both_ref, m_ref) = refs[:4], refs[4:]
    j = pl.program_id(0)
    feats, width = wk_ref.shape
    wide = m_ref.shape[0]
    tall = gq_ref.shape[0]
    row = lax.broadcasted_iota(jnp.int32, (wide, 1), 0)

    @pl.when(j == 0)
    def _():
        if n == 0:
            both_ref[...] = pieces[0][...].astype(bf16)
        else:
            core, chip, _ = position()
            for side, col in enumerate((core, 1 - core)):
                for b, ref in enumerate(pieces[side * n : (side + 1) * n]):
                    part = ref.shape[1]
                    both_ref[:, slot(col * n * part + (chip ^ b) * part, part)] = ref[...]
        tile = both_ref[2 * wide - 16 :].astype(f32)
        for k, ref in enumerate(vector_refs):
            ref[...] = tile[8 + k : 9 + k]
        a = both_ref[wide - 16 : wide].astype(f32)[8:][:, :wide].astype(bf16)
        at = lax.broadcasted_iota(jnp.int32, (8, width), 0)
        shift = shift_ref[...]
        high = shift.astype(bf16)
        low = (shift - high.astype(f32)).astype(bf16)
        a = jnp.concatenate([a[:1], a[:1], jnp.zeros((6, wide), bf16)], axis=0)
        two = jnp.where(at == 0, high.astype(f32), jnp.where(at == 1, low.astype(f32), 0.0)).astype(bf16)
        m = both_ref[:wide].astype(f32) * gain_ref[...] + dot(a, two, 0, 0)
        m_ref[...] = jnp.where(row < feats, m, 0.0).astype(bf16)
        t = dot(a[:, :feats], wk_ref[...], 1, 0) * scale
        gs_ref[...] = dot(t.astype(bf16), wq_ref[...], 1, 1)[:1]

    cols = slot(j * tall, tall)
    gk_ref[...] = (dot(m_ref[...], wq_ref[:, cols], 1, 0) * scale)[:feats]
    gq_ref[...] = dot(m_ref[:, cols][:feats], wk_ref[...], 0, 0) * scale
    gh = dot(both_ref[:wide, cols][:feats], wk_ref[...], 0, 0) * wq_ref[cols].astype(f32)
    ones = jnp.ones((8, width), bf16)
    high = gh.astype(bf16)
    low = (gh - high.astype(f32)).astype(bf16)
    gg_ref[...] = ((dot(ones, high, 1, 1) + dot(ones, low, 1, 1)) * scale)[:1]
    c = both_ref[wide:]
    gv_ref[...] = dot(c, wo_ref[...], 1, 1)[:feats]
    go_ref[...] = dot(wv_ref[...], c[:feats], 0, 0)


def seq_send(v, mask, n):
    return lax.ppermute(v, "seq", [(i, i ^ mask) for i in range(n)])


def batch_send(v, shift, n):
    return lax.ppermute(v, "batch", [(i, (i + shift) % n) for i in range(n)])


class Comm:
    def __init__(self, n_seq, n_batch):
        self.n_seq, self.n_batch = n_seq, n_batch
        self.chips = n_seq // 2

    def twin(self, v):
        return seq_send(v, 1, self.n_seq)

    def to_chips(self, pieces):
        return [seq_send(v, 2 * m, self.n_seq) for m, v in enumerate(pieces, 1)]

    def to_z(self, pieces):
        n = self.n_batch
        order = sorted(range(1, n), key=lambda j: min(j, n - j))
        got = {j: batch_send(pieces[j - 1], j, n) for j in order}
        return [got[j] for j in range(1, n)]

    def all_z(self, v):
        return [v] + self.to_z([v] * (self.n_batch - 1))

    def all_chips(self, v):
        return [v] + self.to_chips([v] * (self.chips - 1))

    def spread(self, v, *after):
        mine, after = tie(self.all_chips(v), after)
        return mine + [self.twin(piece) for piece in mine], *after


def tie(first, second):
    out = lax.optimization_barrier((*first, *second))
    return list(out[: len(first)]), list(out[len(first) :])


def add_all(first, rest):
    for v in rest:
        first = first + v.astype(f32)
    return first


def shards(
    n_seq,
    n_batch,
    latents,
    pixels,
    keep_mask,
    gain_attn,
    shift_attn,
    w_query,
    w_key,
    w_value,
    w_out,
    gain_mlp,
    shift_mlp,
    w_up,
    bias_up,
    w_down,
    bias_down,
    cotangent,
):
    images, rows, width = latents.shape
    pix, feats = pixels.shape[1:]
    hidden = w_up.shape[1]
    wide = -(-(feats + 8) // 16) * 16
    lanes = images * rows
    scale = width ** (-0.5)
    comm = Comm(n_seq, n_batch)
    blocks = comm.chips
    every = n_seq * rows
    x = latents.reshape(lanes, width)
    g = cotangent.reshape(lanes, width)
    gain1, shift1, gain2, shift2, b_up, b_down = (
        v.reshape(1, -1) for v in (gain_attn, shift_attn, gain_mlp, shift_mlp, bias_up, bias_down)
    )
    small = (blocks, wide, lanes)

    qk, hat = call(
        functools.partial(query_kernel, scale),
        [shape((wide, lanes), bf16), shape((lanes, width), bf16)],
        scratch=[pltpu.VMEM((wide, lanes), f32)],
    )(x, gain1, shift1, w_query, w_key)

    pix_x, pix_t = call(
        pixel_kernel,
        [shape((images, pix, wide), bf16), shape((images, wide, pix), bf16)],
        grid=(images,),
        ins=[one_of((feats, pix)), whole((images, pix))],
        outs=[one_of((pix, wide)), one_of((wide, pix))],
        scratch=[pltpu.VMEM((wide, pix), f32)],
    )(pixels.transpose(0, 2, 1), keep_mask)
    q_sides, pix_x, hat = comm.spread(qk, pix_x, hat)
    hats = comm.all_chips(hat)
    vo_hi, vo_lo, d_act = call(
        weight_kernel,
        [shape((wide, width), bf16)] * 2 + [shape((lanes, hidden), f32)],
        scratch=[pltpu.VMEM((wide, width), f32)],
    )(w_value, w_out, g, w_down)

    probs, q_all, top, part_mine, part_twin = call(
        functools.partial(attend_kernel, rows),
        [
            shape((images, pix, every), bf16),
            shape((images, wide, every), bf16),
            shape((images, 1, every), f32),
            shape(small, f32),
            shape(small, f32),
        ],
        grid=(images,),
        ins=[one_of((pix, wide)), one_of((wide, pix))] + [whole((wide, lanes))] * n_seq,
        outs=[one_of((pix, every)), one_of((wide, every)), one_of((1, every)), whole(small), whole(small)],
        scratch=[pltpu.VMEM((pix, every), f32)],
    )(pix_x, pix_t, *q_sides)
    (part_twin,), hats = tie([part_twin], hats)
    keep, *send = call(merge_kernel, [shape((wide, lanes), f32)] * blocks)(
        part_mine, comm.twin(part_twin)
    )
    got = comm.to_chips(send)
    hats = hats + [comm.twin(v) for v in hats]

    new_latents, d_resid, trio, ctx, back, c_part = call(
        functools.partial(mlp_kernel, feats, blocks - 1),
        [
            shape((lanes, width), bf16),
            shape((lanes, width), f32),
            shape((3, lanes, width), bf16),
            shape((wide, lanes), f32),
            shape((wide, lanes), bf16),
            shape((wide, width), f32),
        ],
    )(keep, *got, x, g, vo_hi, vo_lo, gain2, shift2, w_up, b_up, w_down, b_down, d_act)

    half = width // 2
    part = half // blocks
    quarter, tall, size = width // blocks, width // n_batch, width // blocks // n_batch
    cut = part == lanes and part % 128 == 0 and size % 16 == 0
    twin_trio, g2 = comm.twin(trio), comm.twin(g)
    made = jnp.zeros((8, 128), f32)
    if cut:
        made, *own = call(
            functools.partial(weight_grad_kernel, n_batch),
            [shape((8, 128), f32), shape((2 * quarter, half), f32)]
            + [shape((2 * quarter, half), bf16)] * (blocks - 1),
        )(trio, twin_trio, g, g2)
        back_sides, made, *own = comm.spread(back, made, *own)
        own[1:] = comm.to_chips(own[1:])
    else:
        back_sides, made = comm.spread(back, made)
    deep = wide * 3 if cut else wide
    d_scores, d_ctx_all, dq_mine, dq_twin, *both = call(
        functools.partial(back_kernel, rows, blocks, cut),
        [
            shape((images, pix, every), bf16),
            shape((images, wide, every), bf16),
            shape((blocks, deep, lanes), f32),
            shape((blocks, deep, lanes), bf16),
        ]
        + [shape((2 * wide, width), f32)] * (not cut),
        grid=(images,),
        ins=[
            whole((8, 128)),
            one_of((pix, wide)),
            one_of((wide, pix)),
            one_of((pix, every)),
            one_of((1, every)),
            whole((wide, width)),
        ]
        + [whole((wide, lanes))] * n_seq
        + [whole((lanes, width))] * n_seq,
        outs=[one_of((pix, every)), one_of((wide, every))]
        + [whole((blocks, deep, lanes))] * 2
        + [whole((2 * wide, width))] * (not cut),
        scratch=[pltpu.VMEM((2 * wide, width), f32)] * cut
        + [pltpu.VMEM((wide, every), bf16), pltpu.VMEM((every, width), bf16)],
    )(made, pix_x, pix_t, probs, top, c_part, *back_sides, *hats)

    step = 256
    pixel_grad = call(
        functools.partial(pixel_grad_kernel, feats),
        shape((feats, images, pix), f32),
        grid=(-(-pix // step),),
        ins=[pl.BlockSpec((images, step, every), lambda j: (0, j, 0))] * 2 + [whole((images, wide, every))] * 2,
        outs=pl.BlockSpec((feats, images, step), lambda j: (0, 0, j)),
    )(d_scores, probs, q_all, d_ctx_all)

    def latent_part(dq):
        return call(functools.partial(latent_kernel, scale), shape((lanes, width), f32))(
            dq, ctx, x, gain1, w_key, w_query, d_resid
        )

    if cut:
        (dq_twin,), own = tie([dq_twin], own)
        x_keep, *sends = call(
            functools.partial(fold_kernel, blocks),
            [shape((deep, part), f32)] + [shape((deep, part), bf16)] * (blocks - 1),
        )(dq_mine, comm.twin(dq_twin))
        x_got = comm.to_chips(sends)
        first, *rest = call(
            functools.partial(split_kernel, blocks),
            [shape((2 * size, half), f32)] + [shape((2 * size, half), bf16)] * (n_batch - 1),
            scratch=[pltpu.VMEM((2 * quarter, half), f32)],
        )(*own)
        own = [first] + comm.to_z(rest)
        x_got, (pixel_grad, *own) = tie(x_got, [pixel_grad, *own])
        packed = 2 * wide + 2 * blocks * size
        dq, z_own = call(
            functools.partial(join_kernel, blocks),
            [shape((wide, part), f32), shape((packed, part), bf16)],
        )(x_keep, *x_got, *own)
        latent_grad = latent_part(dq)
        z_got, (latent_grad,) = tie(comm.all_z(z_own), [latent_grad])
        sums, own = call(
            functools.partial(stack_kernel, n_batch),
            [shape((2 * wide, part), bf16), shape((n_batch, 2 * blocks * size, part), bf16)],
        )(*z_got)
        pieces = comm.all_chips(sums)
        all_own = [own] + [seq_send(own, 2 * m, n_seq) for m in range(1, blocks - 1)]
        pieces, (own,) = tie(pieces, [own])
        all_own.append(seq_send(own, 2 * (blocks - 1), n_seq))
        own = all_own
        pieces = pieces + [comm.twin(v) for v in pieces]
    else:
        dq = dq_mine + comm.twin(dq_twin).astype(f32)
        dq = add_all(dq[0], comm.to_chips([dq[m].astype(bf16) for m in range(1, blocks)]))
        latent_grad = latent_part(dq)
        pieces = [lax.psum(both[0], ("batch", "seq"))]
    quart = width // 4
    by_rows = pl.BlockSpec((quart, width), lambda j: (j, 0))
    by_columns = pl.BlockSpec((feats, quart), lambda j: (0, j))
    row = whole((1, width))
    grad_query, grad_key, grad_value, grad_out, *vectors = call(
        functools.partial(final_kernel, scale, blocks if cut else 0),
        [
            shape((width, width), f32),
            shape((feats, width), f32),
            shape((feats, width), f32),
            shape((width, width), f32),
        ]
        + [shape((1, width), f32)] * 6,
        grid=(4,),
        ins=[whole(v.shape) for v in pieces]
        + [whole((width, width)), whole((feats, width)), by_columns, by_rows, row, row],
        outs=[by_rows, by_columns, by_columns, by_rows, pl.BlockSpec((1, quart), lambda j: (0, j))] + [row] * 5,
        scratch=[pltpu.VMEM((2 * wide, width), bf16), pltpu.VMEM((wide, width), bf16)],
    )(*pieces, w_query, w_key, w_value, w_out, gain1, shift1)
    vectors = [v.reshape(width) for v in vectors]
    if cut:
        own, (vectors[0],) = tie(own, [vectors[0]])
        grad_up, grad_down = call(
            functools.partial(place_kernel, blocks), [shape((width, width), f32)] * 2
        )(*own, *(comm.twin(v) for v in own))
    else:
        grad_up = lax.psum(dot(trio[0], trio[2], 0, 0), ("batch", "seq"))
        grad_down = lax.psum(dot(trio[1], g, 0, 0), ("batch", "seq"))
    dims = (images, rows, width)
    return (
        new_latents.reshape(dims),
        latent_grad.reshape(dims),
        pixel_grad.transpose(1, 2, 0),
        vectors[0],
        vectors[1],
        grad_query,
        grad_key,
        grad_value,
        grad_out,
        vectors[2],
        vectors[3],
        grad_up,
        vectors[4],
        grad_down,
        vectors[5],
    )


def solution(mesh):
    split = P("batch", "seq", None)
    placed = (split, split, P("batch", "seq")) + (P(),) * 12 + (split,)
    return jax.shard_map(
        functools.partial(shards, mesh.shape["seq"], mesh.shape["batch"]),
        mesh=mesh,
        in_specs=placed,
        out_specs=(split, split, split) + (P(),) * 12,
        check_vma=False,
    )
```

```python
import functools

import jax
import jax.numpy as jnp
from jax import lax
from jax.experimental import pallas as pl
from jax.experimental.pallas import tpu as pltpu
from jax.sharding import PartitionSpec as P

f32 = jnp.float32
bf16 = jnp.bfloat16
EPS = 1e-05
DROP = -1e30
ONE, TOP, MASK = 0, 3, 6
VMEM_LIMIT = 20 << 20


def dot(a, b, ca, cb):
    return lax.dot_general(a, b, (((ca,), (cb,)), ((), ())), preferred_element_type=f32)


def shape(dims, dtype):
    return jax.ShapeDtypeStruct(dims, dtype)


def call(body, out, grid=(), ins=None, outs=None, scratch=(), limit=VMEM_LIMIT):
    kwargs = {}
    if grid:
        kwargs = dict(grid=grid, in_specs=ins, out_specs=outs)
    elif ins:
        kwargs = dict(in_specs=ins)
    return pl.pallas_call(
        body,
        out_shape=out,
        scratch_shapes=list(scratch),
        compiler_params=pltpu.CompilerParams(vmem_limit_bytes=limit),
        **kwargs,
    )


def whole(dims):
    return pl.BlockSpec(dims, lambda *_: (0,) * len(dims))


def one_of(dims):
    return pl.BlockSpec((1,) + dims, lambda i, *_: (i,) + (0,) * len(dims))


def split3(v):
    hi = v.astype(bf16).astype(f32)
    mid = (v - hi).astype(bf16).astype(f32)
    return hi, mid, v - hi - mid


def position():
    s = lax.axis_index("seq")
    return lax.rem(s, 2), lax.div(s, 2), lax.axis_index("batch")


def slot(start, size):
    return pl.ds(pl.multiple_of(start, size), size)


def tail_rows(rows, lanes):
    at = lax.broadcasted_iota(jnp.int32, (8, lanes), 0)
    tile = jnp.zeros((8, lanes), f32)
    for k, v in rows.items():
        tile = jnp.where(at == k, v, tile)
    return tile


def norm_parts(v):
    mean = jnp.mean(v, axis=-1, keepdims=True)
    centered = v - mean
    spread = jnp.mean(centered * centered, axis=-1, keepdims=True)
    scale = lax.rsqrt(spread + EPS)
    return centered * scale, scale


def norm_back(d_out, hat, scale, gain):
    d_hat = d_out * gain
    mean = jnp.mean(d_hat, axis=-1, keepdims=True)
    along = jnp.mean(d_hat * hat, axis=-1, keepdims=True)
    return scale * (d_hat - mean - hat * along)


def gelu_and_slope(v):
    cdf = 0.5 * (1.0 + lax.erf(v * (0.5**0.5)))
    pdf = jnp.exp(-0.5 * v * v) * (1.0 / (2.0 * 3.141592653589793) ** 0.5)
    return v * cdf, cdf + v * pdf


def chunks(n, size=256):
    return [(a, min(size, n - a)) for a in range(0, n, size)]


def query_kernel(scale, *refs):
    sources, (qk_ref, normed_ref), refs = refs[:5], refs[5:7], refs[7:]
    held, (pad_ref, sems) = refs[:5], refs[5:]
    copies = [pltpu.make_async_copy(a, b, sems.at[k]) for k, (a, b) in enumerate(zip(sources, held))]
    for copy in copies:
        copy.start()
    x_ref, gain_ref, shift_ref, wq_ref, wk_ref = held
    feats = wk_ref.shape[0]
    wide, lanes = qk_ref.shape
    for copy in copies[:3]:
        copy.wait()
    hat, _ = norm_parts(x_ref[...].astype(f32))
    normed = (hat * gain_ref[...] + shift_ref[...]).astype(bf16)
    normed_ref[...] = normed
    copies[3].wait()
    query = (dot(normed, wq_ref[...], 1, 0) * scale).astype(bf16)
    pad_ref[...] = jnp.zeros((wide, lanes), f32)
    copies[4].wait()
    pad_ref[:feats] = dot(wk_ref[...], query, 1, 1)
    pad_ref[wide - 8 :] = tail_rows({MASK: 1.0}, lanes)
    qk_ref[...] = pad_ref[...].astype(bf16)


def pixel_kernel(pix_ref, keep_ref, x_ref, t_ref, pad_ref):
    feats, n = pix_ref.shape[1:]
    wide = t_ref.shape[1]
    keep = keep_ref[pl.ds(pl.program_id(0), 1), :]
    bias = jnp.where(keep > 0, 0.0, DROP).astype(f32)
    pad_ref[wide - 16 :] = jnp.zeros((16, n), f32)
    pad_ref[:feats] = pix_ref[0].astype(f32)
    pad_ref[wide - 8 :] = tail_rows({ONE: 1.0, ONE + 1: 1.0, ONE + 2: 1.0, MASK: bias}, n)
    t_ref[0] = pad_ref[...].astype(bf16)
    x_ref[0] = pad_ref[...].T.astype(bf16)


def weight_kernel(wv_ref, wo_ref, g_ref, wd_ref, hi_ref, lo_ref, dact_ref, pad_ref):
    feats = wv_ref.shape[0]
    pad_ref[...] = jnp.zeros(pad_ref.shape, f32)
    pad_ref[:feats] = dot(wv_ref[...], wo_ref[...], 1, 0)
    v = pad_ref[...]
    hi = v.astype(bf16)
    hi_ref[...] = hi
    lo_ref[...] = (v - hi.astype(f32)).astype(bf16)
    dact_ref[...] = dot(g_ref[...], wd_ref[...], 1, 1)


def lay_lanes(i, rows, refs, out_ref):
    for k in range(2):

        @pl.when(i == k)
        def _():
            parts = [ref[b, :, k * rows : (k + 1) * rows] for ref in refs for b in range(ref.shape[0])]
            out_ref[...] = jnp.concatenate(parts, axis=1)


def unlay_lanes(i, rows, v, mine_ref, twin_ref):
    blocks = mine_ref.shape[0]
    for k in range(2):

        @pl.when(i == k)
        def _():
            for b in range(2 * blocks):
                ref = (mine_ref, twin_ref)[b // blocks]
                piece = v[:, b * rows : (b + 1) * rows].astype(ref.dtype)
                ref[b % blocks, :, k * rows : (k + 1) * rows] = piece


def attend_kernel(rows, x_ref, t_ref, *refs):
    *sides, p_ref, q_ref, top_ref, pm_ref, pt_ref, s_ref = refs
    i = pl.program_id(0)
    n = x_ref.shape[1]
    wide, lanes = q_ref.shape[1:]
    lay_lanes(i, rows, sides, q_ref.at[0])
    q = q_ref[0]
    top = jnp.full((1, lanes), -jnp.inf, f32)
    for a, size in chunks(n):
        s = dot(x_ref[0, a : a + size], q, 1, 0)
        s_ref[a : a + size] = s
        top = jnp.maximum(top, jnp.max(s, axis=0, keepdims=True))
    total = jnp.zeros((wide, lanes), f32)
    for a, size in chunks(n):
        p = jnp.exp(s_ref[a : a + size] - top).astype(bf16)
        p_ref[0, a : a + size] = p
        total = total + dot(t_ref[0, :, a : a + size], p, 1, 0)
    top_ref[0] = top
    tile = total[wide - 8 :]
    at = lax.broadcasted_iota(jnp.int32, tile.shape, 0)
    tile = jnp.where(at == TOP, top, jnp.where(at == ONE, tile, 0.0))
    unlay_lanes(i, rows, jnp.concatenate([total[: wide - 8], tile], axis=0), pm_ref, pt_ref)


def merge_kernel(a_ref, b_ref, *out_refs):
    blocks, wide, lanes = a_ref.shape
    base = wide - 8
    for k, ref in enumerate(out_refs):
        ta, tb = a_ref[k, pl.ds(base + TOP, 1)], b_ref[k, pl.ds(base + TOP, 1)]
        top = jnp.maximum(ta, tb)
        wa, wb = jnp.exp(ta - top), jnp.exp(tb - top)
        total = a_ref[k, pl.ds(base + ONE, 1)] * wa + b_ref[k, pl.ds(base + ONE, 1)] * wb
        ref[:base] = a_ref[k, :base] * wa + b_ref[k, :base] * wb
        ref[base:] = tail_rows({ONE: total, TOP: top}, lanes)


def mlp_kernel(feats, n_got, keep_ref, *refs):
    got_refs, refs = refs[:n_got], refs[n_got:]
    x_ref, g_ref, hi_ref, lo_ref, gain_ref, shift_ref, wu_ref, bu_ref, wd_ref, bd_ref, dact_ref, *outs = refs
    new_ref, dres_ref, trio_ref, ctx_ref, back_ref, csum_ref = outs
    wide, lanes = keep_ref.shape
    base = wide - 8
    part_refs = (keep_ref, *got_refs)
    parts = [ref[...] for ref in part_refs]
    tops = [ref[pl.ds(base + TOP, 1)] for ref in part_refs]
    sums = [ref[pl.ds(base + ONE, 1)] for ref in part_refs]
    peak = functools.reduce(jnp.maximum, tops)
    total = jnp.zeros((1, lanes), f32)
    ctx = jnp.zeros((wide, lanes), f32)
    for v, top, part in zip(parts, tops, sums):
        share = jnp.exp(top - peak)
        total = total + part * share
        ctx = ctx + v * share
    ctx = ctx / total
    lse = peak + jnp.log(total)
    row = lax.broadcasted_iota(jnp.int32, (wide, lanes), 0)
    ctx = jnp.where(row < feats, ctx, 0.0)
    ctx_ref[...] = ctx
    ctx_b = ctx.astype(bf16)
    resid = x_ref[...].astype(f32) + dot(ctx_b, hi_ref[...], 0, 0) + dot(ctx_b, lo_ref[...], 0, 0)
    hat, scale = norm_parts(resid)
    normed = (hat * gain_ref[...] + shift_ref[...]).astype(bf16)
    trio_ref[0] = normed
    pre = dot(normed, wu_ref[...], 1, 0) + bu_ref[...]
    act_f, slope = gelu_and_slope(pre)
    act = act_f.astype(bf16)
    trio_ref[1] = act
    d_pre = (dact_ref[...] * slope).astype(bf16)
    trio_ref[2] = d_pre
    d_normed = dot(d_pre, wu_ref[...], 1, 1)
    g = g_ref[...].astype(f32)
    d_resid = g + norm_back(d_normed, hat, scale, gain_ref[...])
    dres_ref[...] = d_resid
    d_resid_b = d_resid.astype(bf16)
    d_ctx = (dot(hi_ref[...], d_resid_b, 1, 1) + dot(lo_ref[...], d_resid_b, 1, 1)).astype(bf16)
    delta = jnp.sum(ctx * d_ctx.astype(f32), axis=0, keepdims=True)
    rows = {ONE + k: -v for k, v in enumerate(split3(delta))}
    rows.update({TOP + k: v for k, v in enumerate(split3(lse))})
    back_ref[...] = jnp.concatenate([d_ctx[:base], tail_rows(rows, lanes).astype(bf16)], axis=0)
    new_ref[...] = (resid + dot(act, wd_ref[...], 1, 0) + bd_ref[...]).astype(bf16)
    c = dot(ctx_b, d_resid_b, 1, 0)
    vectors = {
        0: jnp.sum(d_normed * hat, axis=0, keepdims=True),
        1: jnp.sum(d_normed, axis=0, keepdims=True),
        2: jnp.sum(d_pre.astype(f32), axis=0, keepdims=True),
        3: jnp.sum(g, axis=0, keepdims=True),
    }
    csum_ref[...] = jnp.concatenate([c[:base], tail_rows(vectors, c.shape[1])], axis=0)


def back_kernel(rows, x_ref, t_ref, p_ref, top_ref, *refs):
    sides, (ds_ref, dc_ref, dm_ref, dt_ref, b_ref) = refs[:2], refs[2:]
    i = pl.program_id(0)
    pix = x_ref.shape[1]
    wide, lanes = b_ref.shape
    lay_lanes(i, rows, sides, b_ref)
    b = b_ref[...]
    tail = b[wide - 16 :].astype(f32)[8:]
    at = lax.broadcasted_iota(jnp.int32, tail.shape, 0)
    lse = jnp.sum(jnp.where((at >= TOP) & (at < TOP + 3), tail, 0.0), axis=0, keepdims=True)
    ratio = jnp.exp(top_ref[0] - lse)
    dc_ref[0] = (b.astype(f32) * ratio).astype(bf16)
    sums = jnp.zeros((wide, lanes), f32)
    for a, size in chunks(pix):
        d = dot(x_ref[0, a : a + size], b, 1, 0)
        ds = (p_ref[0, a : a + size].astype(f32) * (d * ratio)).astype(bf16)
        ds_ref[0, a : a + size] = ds
        sums = sums + dot(t_ref[0, :, a : a + size], ds, 1, 0)
    unlay_lanes(i, rows, sums, dm_ref, dt_ref)


def pixel_grad_kernel(feats, ds_ref, p_ref, q_ref, dc_ref, out_ref):
    for i in range(ds_ref.shape[0]):
        v = dot(q_ref[i], ds_ref[i], 1, 1) + dot(dc_ref[i], p_ref[i], 1, 1)
        out_ref[:, i, :] = v[:feats]


def latent_kernel(scale, n_got, cut, *refs):
    dq_refs, refs = refs[: n_got + 1], refs[n_got + 1 :]
    ctx_ref, x_ref, normed_ref, gain_ref, wk_ref, wq_ref, dres_ref, c_ref, *outs = refs
    lat_ref, *outs, dq_ref = outs
    feats = wk_ref.shape[0]
    wide, lanes = dq_ref.shape
    base = wide - 8
    dq_ref[...] = dq_refs[0][...]
    for ref in dq_refs[1:]:
        dq_ref[...] += ref[:wide].astype(f32)
    d = dq_ref[...] - dq_ref[pl.ds(base + ONE, 1)] * ctx_ref[...]
    row = lax.broadcasted_iota(jnp.int32, (wide, lanes), 0)
    d = jnp.where(row < feats, d, 0.0).astype(bf16)
    d_query = dot(d[:feats], wk_ref[...], 0, 0).astype(bf16)
    d_normed = dot(d_query, wq_ref[...], 1, 1) * scale
    hat, spread = norm_parts(x_ref[...].astype(f32))
    vectors = {
        0: jnp.sum(d_normed * hat, axis=0, keepdims=True),
        1: jnp.sum(d_normed, axis=0, keepdims=True),
    }
    both_ref = outs[-1]
    both_ref[:base] = dot(d, normed_ref[...], 1, 0)[:base]
    both_ref[base:wide] = tail_rows(vectors, both_ref.shape[1])
    both_ref[wide:] = c_ref[...]
    if cut:
        mine_ref, twin_ref = outs[:2]
        core, chip, _ = position()
        n, _, part = mine_ref.shape
        for b in range(n):
            at = (chip ^ b) * part
            mine_ref[b] = both_ref[:, slot(core * n * part + at, part)]
            twin_ref[b] = both_ref[:, slot((1 - core) * n * part + at, part)].astype(bf16)
    lat_ref[...] = dres_ref[...] + norm_back(d_normed, hat, spread, gain_ref[...])


def halves_kernel(*refs):
    mine_ref, other_ref = refs[-2:]
    core, half = position()[0], mine_ref.shape[2]
    for j, ref in enumerate(refs[:-2]):
        mine_ref[j] = ref[:, slot(core * half, half)]
        other_ref[j] = ref[:, slot((1 - core) * half, half)]


def up_kernel(n, trio_ref, twin_ref, *refs):
    core, chip, z = position()
    up_refs, act_refs = refs[:n], refs[n:]
    tall, half = up_refs[0].shape
    cols = slot(core * half, half)
    slab = act_refs[0].shape[1]
    for j, ref in enumerate(act_refs):
        rows = slot(lax.rem(z + j, len(act_refs)) * slab, slab)
        ref[...] = jnp.concatenate([trio_ref[1, :, rows], twin_ref[1, :, rows]], axis=0)
    d_pre = jnp.concatenate([trio_ref[2, :, cols], twin_ref[2, :, cols]], axis=0)
    for m, ref in enumerate(up_refs):
        rows = slot((chip ^ m) * tall, tall)
        normed = jnp.concatenate([trio_ref[0, :, rows], twin_ref[0, :, rows]], axis=0)
        ref[...] = dot(normed, d_pre, 0, 0).astype(ref.dtype)


def total(refs):
    v = refs[0][...].astype(f32)
    for ref in refs[1:]:
        v = v + ref[...].astype(f32)
    return v


def halve_kernel(bit, *refs):
    keep_ref, send_ref, sum_ref = refs[-3:]
    sum_ref[...] = total(refs[:-3])
    size = keep_ref.shape[0]
    mine = lax.rem(lax.div(position()[2], bit), 2)
    keep_ref[...] = sum_ref[slot(mine * size, size)]
    send_ref[...] = sum_ref[slot((1 - mine) * size, size)].astype(bf16)


def fold_kernel(n, mine_ref, twin_ref, keep_ref, *out_refs):
    keep_ref[...] = mine_ref[0] + twin_ref[0].astype(f32)
    for m, ref in enumerate(out_refs, 1):
        ref[...] = (mine_ref[m] + twin_ref[m].astype(f32)).astype(bf16)


def fold_down_kernel(n_batch, mine_ref, twin_ref, g_ref, g2_ref, *refs):
    act_refs, refs = refs[:n_batch], refs[n_batch:]
    keep_ref, own_ref, *send_refs, sum_ref = refs
    chip = position()[1]
    base, part = keep_ref.shape
    size = own_ref.shape[0]
    act = jnp.concatenate([ref[...] for ref in act_refs], axis=0)
    g = jnp.concatenate([ref[j] for j in range(n_batch) for ref in (g_ref, g2_ref)], axis=0)
    sum_ref[...] = dot(act, g, 0, 0)
    keep_ref[...] = mine_ref[0] + twin_ref[0].astype(f32)
    own_ref[...] = sum_ref[slot(chip * size, size)]
    for m, ref in enumerate(send_refs, 1):
        ref[:base] = (mine_ref[m] + twin_ref[m].astype(f32)).astype(bf16)
        v = sum_ref[slot((chip ^ m) * size, size)].astype(bf16)
        for q in range(v.shape[1] // part):
            ref[base + q * size : base + (q + 1) * size] = v[:, q * part : (q + 1) * part]


def unfold_kernel(own_ref, *refs):
    got_refs, out_ref = refs[:-1], refs[-1]
    size, half = own_ref.shape
    part = got_refs[0].shape[1]
    base = got_refs[0].shape[0] - size * (half // part)
    for q in range(half // part):
        cols = slice(q * part, (q + 1) * part)
        v = own_ref[:, cols]
        for ref in got_refs:
            v = v + ref[base + q * size : base + (q + 1) * size].astype(f32)
        out_ref[:, cols] = v.astype(bf16)


def add_kernel(*refs):
    refs[-1][...] = total(refs[:-1]).astype(refs[-1].dtype)


def stack_kernel(*refs):
    for j, ref in enumerate(refs[:-1]):
        refs[-1][j] = ref[...]


def place_kernel(n, *refs):
    core, chip, z = position()
    out_refs = refs[-2:]
    half = out_refs[0].shape[1] // 2
    n_batch, _, size = refs[0].shape[:3]
    for side, col in enumerate((core, 1 - core)):
        for m, ref in enumerate(refs[side * n : (side + 1) * n]):
            for j, mask in enumerate(z_masks(n_batch)):
                k, z_at = chip ^ m, z ^ mask
                for h, row in enumerate((k * n_batch + z_at, z_at * n + k)):
                    v = ref[j, h].astype(f32)
                    out_refs[h][slot(row * size, size), slot(col * half, half)] = v


def final_kernel(scale, n, *refs):
    pieces, refs = refs[: 1 + (n > 0)], refs[1 + (n > 0) :]
    wq_ref, wk_ref, wv_ref, wo_ref, gq_ref, gk_ref, gv_ref, go_ref, *vector_refs, both_ref = refs
    j = pl.program_id(0)
    feats = wk_ref.shape[0]
    wide = both_ref.shape[0] // 2
    tall = gq_ref.shape[0]

    @pl.when(j == 0)
    def _():
        if n == 0:
            both_ref[...] = pieces[0][...].astype(bf16)
        else:
            core, chip, _ = position()
            for side, col in enumerate((core, 1 - core)):
                part = pieces[side].shape[2]
                for b in range(n):
                    both_ref[:, slot(col * n * part + (chip ^ b) * part, part)] = pieces[side][b]
        for k, ref in enumerate(vector_refs):
            base, at = (wide, k) if k < 2 else (2 * wide, k - 2)
            ref[...] = both_ref[base - 16 : base].astype(f32)[8 + at : 9 + at]

    m, c = both_ref[:wide], both_ref[wide:]
    gk_ref[...] = (dot(m, wq_ref[...], 1, 0) * scale)[:feats]
    gq_ref[...] = dot(both_ref[:wide, slot(j * tall, tall)][:feats], wk_ref[...], 0, 0) * scale
    gv_ref[...] = dot(c, wo_ref[...], 1, 1)[:feats]
    go_ref[...] = dot(wv_ref[...], c[:feats], 0, 0)


def seq_send(v, mask, n):
    return lax.ppermute(v, "seq", [(i, i ^ mask) for i in range(n)])


def batch_send(v, shift, n):
    return lax.ppermute(v, "batch", [(i, (i + shift) % n) for i in range(n)])


def z_masks(n):
    masks = [0]
    while len(masks) < n:
        masks = masks + [m ^ (2 * len(masks) - 1) for m in masks]
    return masks


class Comm:
    def __init__(self, n_seq, n_batch):
        self.n_seq, self.n_batch = n_seq, n_batch
        self.chips = n_seq // 2

    def twin(self, v):
        return seq_send(v, 1, self.n_seq)

    def to_chips(self, pieces):
        return [seq_send(v, 2 * m, self.n_seq) for m, v in enumerate(pieces, 1)]

    def to_z(self, pieces):
        n = self.n_batch
        order = sorted(range(1, n), key=lambda j: min(j, n - j))
        got = {j: batch_send(pieces[j - 1], j, n) for j in order}
        return [got[j] for j in range(1, n)]

    def next_z(self, v):
        return batch_send(v, 1, self.n_batch)

    def sum_scatter_z(self, pieces, mask, end):
        while mask > end:
            size, half = pieces[0].shape[0] // 2, pieces[0].shape[1]
            keep, send = call(
                functools.partial(halve_kernel, mask // 2),
                [shape((size, half), f32), shape((size, half), bf16)],
                scratch=[pltpu.VMEM((2 * size, half), f32)],
            )(*pieces)
            pairs = [(i, i ^ (mask - 1)) for i in range(self.n_batch)]
            pieces = [keep, lax.ppermute(send, "batch", pairs)]
            mask //= 2
        return pieces

    def sum_z(self, v):
        mask = 1
        while mask < self.n_batch:
            pairs = [(i, i ^ (2 * mask - 1)) for i in range(self.n_batch)]
            other = lax.ppermute(v, "batch", pairs)
            v = call(add_kernel, shape(v.shape, v.dtype))(v, other)
            mask *= 2
        return v

    def all_z(self, v):
        got = [v]
        while len(got) < self.n_batch:
            pairs = [(i, i ^ (2 * len(got) - 1)) for i in range(self.n_batch)]
            got = got + [lax.ppermute(piece, "batch", pairs) for piece in got]
        return got

    def all_chips(self, v):
        return [v] + self.to_chips([v] * (self.chips - 1))

    def spread(self, v, beside):
        mine, beside = tie(self.all_chips(v), beside)
        mine = call(stack_kernel, shape((self.chips, *v.shape), v.dtype))(*mine)
        return [mine, self.twin(mine)], beside


def tie(first, second):
    out = lax.optimization_barrier((*first, *second))
    return list(out[: len(first)]), list(out[len(first) :])


def add_all(first, rest):
    for v in rest:
        first = first + v.astype(f32)
    return first


def shards(
    n_seq,
    n_batch,
    latents,
    pixels,
    keep_mask,
    gain_attn,
    shift_attn,
    w_query,
    w_key,
    w_value,
    w_out,
    gain_mlp,
    shift_mlp,
    w_up,
    bias_up,
    w_down,
    bias_down,
    cotangent,
):
    images, rows, width = latents.shape
    pix, feats = pixels.shape[1:]
    hidden = w_up.shape[1]
    wide = -(-(feats + 8) // 16) * 16
    lanes = images * rows
    scale = width ** (-0.5)
    comm = Comm(n_seq, n_batch)
    blocks = comm.chips
    every = n_seq * rows
    x = latents.reshape(lanes, width)
    g = cotangent.reshape(lanes, width)
    gain1, shift1, gain2, shift2, b_up, b_down = (
        v.reshape(1, -1) for v in (gain_attn, shift_attn, gain_mlp, shift_mlp, bias_up, bias_down)
    )
    small = (blocks, wide, lanes)

    operands = (x, gain1, shift1, w_query, w_key)
    qk, normed = call(
        functools.partial(query_kernel, scale),
        [shape((wide, lanes), bf16), shape((lanes, width), bf16)],
        ins=[pl.BlockSpec(memory_space=pltpu.HBM)] * 5,
        scratch=[pltpu.VMEM(v.shape, v.dtype) for v in operands]
        + [pltpu.VMEM((wide, lanes), f32), pltpu.SemaphoreType.DMA((5,))],
        limit=60 << 20,
    )(*operands)

    pix_x, pix_t = call(
        pixel_kernel,
        [shape((images, pix, wide), bf16), shape((images, wide, pix), bf16)],
        grid=(images,),
        ins=[one_of((feats, pix)), whole((images, pix))],
        outs=[one_of((pix, wide)), one_of((wide, pix))],
        scratch=[pltpu.VMEM((wide, pix), f32)],
    )(pixels.transpose(0, 2, 1), keep_mask)
    g_all = [g, comm.next_z(g)]
    q_sides, (pix_x, g_all[1]) = comm.spread(qk, [pix_x, g_all[1]])
    vo_hi, vo_lo, d_act = call(
        weight_kernel,
        [shape((wide, width), bf16)] * 2 + [shape((lanes, hidden), f32)],
        scratch=[pltpu.VMEM((wide, width), f32)],
    )(w_value, w_out, g, w_down)

    probs, q_all, top, part_mine, part_twin = call(
        functools.partial(attend_kernel, rows),
        [
            shape((images, pix, every), bf16),
            shape((images, wide, every), bf16),
            shape((images, 1, every), f32),
            shape(small, f32),
            shape(small, f32),
        ],
        grid=(images,),
        ins=[one_of((pix, wide)), one_of((wide, pix))] + [whole(small)] * 2,
        outs=[one_of((pix, every)), one_of((wide, every)), one_of((1, every)), whole(small), whole(small)],
        scratch=[pltpu.VMEM((pix, every), f32)],
    )(pix_x, pix_t, *q_sides)
    keep, *send = call(merge_kernel, [shape((wide, lanes), f32)] * blocks)(
        part_mine, comm.twin(part_twin)
    )
    g_next = comm.next_z(g_all[-1])
    got, (g_next,) = tie(comm.to_chips(send), [g_next])
    g_all.append(g_next)

    new_latents, d_resid, trio, ctx, back, c_part = call(
        functools.partial(mlp_kernel, feats, blocks - 1),
        [
            shape((lanes, width), bf16),
            shape((lanes, width), f32),
            shape((3, lanes, width), bf16),
            shape((wide, lanes), f32),
            shape((wide, lanes), bf16),
            shape((wide, width), f32),
        ],
    )(keep, *got, x, g, vo_hi, vo_lo, gain2, shift2, w_up, b_up, w_down, b_down, d_act)

    half = width // 2
    part = half // blocks
    quarter, tall, size = width // blocks, width // n_batch, width // blocks // n_batch
    cut = part == lanes and part % 128 == 0 and size % 16 == 0
    tall = hidden // n_batch
    if cut:
        up = call(
            functools.partial(up_kernel, blocks),
            [shape((quarter, half), f32)]
            + [shape((quarter, half), bf16)] * (blocks - 1)
            + [shape((2 * lanes, tall), bf16)] * n_batch,
        )(trio, comm.twin(trio))
        up, act = up[:blocks], up[blocks:]
        g_next = [comm.next_z(g_all[-1]) for _ in range(3, n_batch)]
        back_sides, rest = comm.spread(back, [*up, *g_next])
        up, g_all = rest[:blocks], g_all + rest[blocks:]
        up[1:] = comm.to_chips(up[1:])
        act = list(act)
        act_near = [j for j in range(1, n_batch) if min(j, n_batch - j) == 1]
        for j in act_near:
            act[j] = batch_send(act[j], j, n_batch)
        g_mine, g_twin = call(halves_kernel, [shape((n_batch, lanes, half), bf16)] * 2)(*g_all)
        g_twin = comm.twin(g_twin)
    else:
        back_sides, _ = comm.spread(back, [])
    d_scores, d_ctx_all, dq_mine, dq_twin = call(
        functools.partial(back_kernel, rows),
        [
            shape((images, pix, every), bf16),
            shape((images, wide, every), bf16),
            shape(small, f32),
            shape(small, bf16),
        ],
        grid=(images,),
        ins=[one_of((pix, wide)), one_of((wide, pix)), one_of((pix, every)), one_of((1, every))]
        + [whole(small)] * 2,
        outs=[one_of((pix, every)), one_of((wide, every)), whole(small), whole(small)],
        scratch=[pltpu.VMEM((wide, every), bf16)],
    )(pix_x, pix_t, probs, top, *back_sides)

    step = 256
    pixel_grad = call(
        functools.partial(pixel_grad_kernel, feats),
        shape((feats, images, pix), f32),
        grid=(-(-pix // step),),
        ins=[pl.BlockSpec((images, step, every), lambda j: (0, j, 0))] * 2 + [whole((images, wide, every))] * 2,
        outs=pl.BlockSpec((feats, images, step), lambda j: (0, 0, j)),
    )(d_scores, probs, q_all, d_ctx_all)

    def folded(mine, twin):
        return call(
            functools.partial(fold_kernel, blocks),
            [shape(mine.shape[1:], f32)] + [shape(mine.shape[1:], bf16)] * (blocks - 1),
        )(mine, comm.twin(twin))

    if cut:
        act_far = [j for j in range(1, n_batch) if j not in act_near]
        (dq_mine,), far = tie([dq_mine], [act[j] for j in act_far])
        for j, v in zip(act_far, far):
            act[j] = batch_send(v, j, n_batch)
        (dq_twin,), rest = tie([dq_twin], [pixel_grad, *up, *act])
        pixel_grad, up, act = rest[0], rest[1 : 1 + blocks], rest[1 + blocks :]
        first, down, *rest = call(
            functools.partial(fold_down_kernel, n_batch),
            [shape((wide, lanes), f32), shape((size, half), f32)]
            + [shape((wide + blocks * size, lanes), bf16)] * (blocks - 1),
            scratch=[pltpu.VMEM((tall, half), f32)],
        )(dq_mine, comm.twin(dq_twin), g_mine, g_twin, *act)
        dq, up = tie([first] + comm.to_chips(rest), comm.sum_scatter_z(up, n_batch, 2))
    else:
        first, *rest = folded(dq_mine, dq_twin)
        dq = [first] + comm.to_chips(rest)
    latent_grad, *both = call(
        functools.partial(latent_kernel, scale, blocks - 1, cut),
        [shape((lanes, width), f32)]
        + [shape((blocks, 2 * wide, part), f32), shape((blocks, 2 * wide, part), bf16)] * cut
        + [shape((2 * wide, width), f32)] * (not cut),
        scratch=[pltpu.VMEM((2 * wide, width), f32)] * cut + [pltpu.VMEM((wide, lanes), f32)],
    )(*dq, ctx, x, normed, gain1, w_key, w_query, d_resid, c_part)
    if cut:
        up = comm.sum_scatter_z(up, 2, 1)
        first, *rest = folded(*both)
        (first, *rest), up = tie([first, *rest], up)
        up = call(add_kernel, shape((size, half), bf16))(*up)
        down = call(unfold_kernel, shape((size, half), bf16))(down, *dq[1:])
        own = call(stack_kernel, shape((2, size, half), bf16))(up, down)
        sums, own = tie([first] + comm.to_chips(rest), comm.all_z(own))
        own = call(stack_kernel, shape((n_batch, 2, size, half), bf16))(*own)
        sums = call(add_kernel, shape((2 * wide, part), bf16))(*sums)
        (sums,), own = tie([comm.sum_z(sums)], comm.all_chips(own))
        pieces = comm.all_chips(sums)
        grad_up, grad_down = call(functools.partial(place_kernel, blocks), [shape((width, width), f32)] * 2)(
            *own, *map(comm.twin, own)
        )
        pieces, (grad_up, grad_down) = tie(pieces, [grad_up, grad_down])
        pieces = call(stack_kernel, shape((blocks, 2 * wide, part), bf16))(*pieces)
        pieces = [pieces, comm.twin(pieces)]
    else:
        pieces = [lax.psum(both[0], ("batch", "seq"))]
    quart = width // 4
    by_rows = pl.BlockSpec((quart, width), lambda j: (j, 0))
    by_columns = pl.BlockSpec((feats, quart), lambda j: (0, j))
    row = whole((1, width))
    grad_query, grad_key, grad_value, grad_out, *vectors = call(
        functools.partial(final_kernel, scale, blocks if cut else 0),
        [
            shape((width, width), f32),
            shape((feats, width), f32),
            shape((feats, width), f32),
            shape((width, width), f32),
        ]
        + [shape((1, width), f32)] * 6,
        grid=(4,),
        ins=[whole(v.shape) for v in pieces]
        + [pl.BlockSpec((width, quart), lambda j: (0, j)), whole((feats, width)), by_columns, by_rows],
        outs=[by_rows, by_columns, by_columns, by_rows] + [row] * 6,
        scratch=[pltpu.VMEM((2 * wide, width), bf16)],
    )(*pieces, w_query, w_key, w_value, w_out)
    vectors = [v.reshape(width) for v in vectors]
    if not cut:
        grad_up = lax.psum(dot(trio[0], trio[2], 0, 0), ("batch", "seq"))
        grad_down = lax.psum(dot(trio[1], g, 0, 0), ("batch", "seq"))
    dims = (images, rows, width)
    return (
        new_latents.reshape(dims),
        latent_grad.reshape(dims),
        pixel_grad.transpose(1, 2, 0),
        vectors[0],
        vectors[1],
        grad_query,
        grad_key,
        grad_value,
        grad_out,
        vectors[2],
        vectors[3],
        grad_up,
        vectors[4],
        grad_down,
        vectors[5],
    )


def solution(mesh):
    split = P("batch", "seq", None)
    placed = (split, split, P("batch", "seq")) + (P(),) * 12 + (split,)
    return jax.shard_map(
        functools.partial(shards, mesh.shape["seq"], mesh.shape["batch"]),
        mesh=mesh,
        in_specs=placed,
        out_specs=(split, split, split) + (P(),) * 12,
        check_vma=False,
    )
```

```python
import functools

import jax
import jax.numpy as jnp
from jax import lax
from jax.experimental import pallas as pl
from jax.experimental.pallas import tpu as pltpu
from jax.sharding import PartitionSpec as P

f32 = jnp.float32
bf16 = jnp.bfloat16
EPS = 1e-05
DROP = -1e30
ONE, TOP, MASK = 0, 3, 6
VMEM_LIMIT = 20 << 20


def dot(a, b, ca, cb):
    return lax.dot_general(a, b, (((ca,), (cb,)), ((), ())), preferred_element_type=f32)


def shape(dims, dtype):
    return jax.ShapeDtypeStruct(dims, dtype)


def call(body, out, grid=(), ins=None, outs=None, scratch=(), limit=VMEM_LIMIT):
    kwargs = {}
    if grid:
        kwargs = dict(grid=grid, in_specs=ins, out_specs=outs)
    elif ins:
        kwargs = dict(in_specs=ins)
    return pl.pallas_call(
        body,
        out_shape=out,
        scratch_shapes=list(scratch),
        compiler_params=pltpu.CompilerParams(vmem_limit_bytes=limit),
        **kwargs,
    )


def whole(dims):
    return pl.BlockSpec(dims, lambda *_: (0,) * len(dims))


def one_of(dims):
    return pl.BlockSpec((1,) + dims, lambda i, *_: (i,) + (0,) * len(dims))


def split3(v):
    hi = v.astype(bf16).astype(f32)
    mid = (v - hi).astype(bf16).astype(f32)
    return hi, mid, v - hi - mid


def position():
    s = lax.axis_index("seq")
    return lax.rem(s, 2), lax.div(s, 2), lax.axis_index("batch")


def slot(start, size):
    return pl.ds(pl.multiple_of(start, size), size)


def tail_rows(rows, lanes):
    at = lax.broadcasted_iota(jnp.int32, (8, lanes), 0)
    tile = jnp.zeros((8, lanes), f32)
    for k, v in rows.items():
        tile = jnp.where(at == k, v, tile)
    return tile


def norm_parts(v):
    mean = jnp.mean(v, axis=-1, keepdims=True)
    centered = v - mean
    spread = jnp.mean(centered * centered, axis=-1, keepdims=True)
    scale = lax.rsqrt(spread + EPS)
    return centered * scale, scale


def norm_back(d_out, hat, scale, gain):
    d_hat = d_out * gain
    mean = jnp.mean(d_hat, axis=-1, keepdims=True)
    along = jnp.mean(d_hat * hat, axis=-1, keepdims=True)
    return scale * (d_hat - mean - hat * along)


def gelu_and_slope(v):
    cdf = 0.5 * (1.0 + lax.erf(v * (0.5**0.5)))
    pdf = jnp.exp(-0.5 * v * v) * (1.0 / (2.0 * 3.141592653589793) ** 0.5)
    return v * cdf, cdf + v * pdf


def chunks(n, size=256):
    return [(a, min(size, n - a)) for a in range(0, n, size)]


def query_kernel(scale, *refs):
    sources, (qk_ref, normed_ref), refs = refs[:5], refs[5:7], refs[7:]
    held, (pad_ref, sems) = refs[:5], refs[5:]
    copies = [pltpu.make_async_copy(a, b, sems.at[k]) for k, (a, b) in enumerate(zip(sources, held))]
    for copy in copies:
        copy.start()
    x_ref, gain_ref, shift_ref, wq_ref, wk_ref = held
    feats = wk_ref.shape[0]
    wide, lanes = qk_ref.shape
    for copy in copies[:3]:
        copy.wait()
    hat, _ = norm_parts(x_ref[...].astype(f32))
    normed = (hat * gain_ref[...] + shift_ref[...]).astype(bf16)
    normed_ref[...] = normed
    copies[3].wait()
    query = (dot(normed, wq_ref[...], 1, 0) * scale).astype(bf16)
    pad_ref[...] = jnp.zeros((wide, lanes), f32)
    copies[4].wait()
    pad_ref[:feats] = dot(wk_ref[...], query, 1, 1)
    pad_ref[wide - 8 :] = tail_rows({MASK: 1.0}, lanes)
    qk_ref[...] = pad_ref[...].astype(bf16)


def pixel_kernel(pix_ref, keep_ref, x_ref, t_ref, pad_ref):
    feats, n = pix_ref.shape[1:]
    wide = t_ref.shape[1]
    keep = keep_ref[pl.ds(pl.program_id(0), 1), :]
    bias = jnp.where(keep > 0, 0.0, DROP).astype(f32)
    pad_ref[wide - 16 :] = jnp.zeros((16, n), f32)
    pad_ref[:feats] = pix_ref[0].astype(f32)
    pad_ref[wide - 8 :] = tail_rows({ONE: 1.0, ONE + 1: 1.0, ONE + 2: 1.0, MASK: bias}, n)
    t_ref[0] = pad_ref[...].astype(bf16)
    x_ref[0] = pad_ref[...].T.astype(bf16)


def weight_kernel(wv_ref, wo_ref, g_ref, wd_ref, hi_ref, lo_ref, dact_ref, pad_ref):
    feats = wv_ref.shape[0]
    pad_ref[...] = jnp.zeros(pad_ref.shape, f32)
    pad_ref[:feats] = dot(wv_ref[...], wo_ref[...], 1, 0)
    v = pad_ref[...]
    hi = v.astype(bf16)
    hi_ref[...] = hi
    lo_ref[...] = (v - hi.astype(f32)).astype(bf16)
    dact_ref[...] = dot(g_ref[...], wd_ref[...], 1, 1)


def lay_lanes(i, rows, refs, out_ref):
    for k in range(2):

        @pl.when(i == k)
        def _():
            parts = [ref[b, :, k * rows : (k + 1) * rows] for ref in refs for b in range(ref.shape[0])]
            out_ref[...] = jnp.concatenate(parts, axis=1)


def unlay_lanes(i, rows, v, mine_ref, twin_ref):
    blocks = mine_ref.shape[0]
    for k in range(2):

        @pl.when(i == k)
        def _():
            for b in range(2 * blocks):
                ref = (mine_ref, twin_ref)[b // blocks]
                piece = v[:, b * rows : (b + 1) * rows].astype(ref.dtype)
                ref[b % blocks, :, k * rows : (k + 1) * rows] = piece


def attend_kernel(rows, x_ref, t_ref, *refs):
    *sides, p_ref, q_ref, top_ref, pm_ref, pt_ref, s_ref = refs
    i = pl.program_id(0)
    n = x_ref.shape[1]
    wide, lanes = q_ref.shape[1:]
    lay_lanes(i, rows, sides, q_ref.at[0])
    q = q_ref[0]
    top = jnp.full((1, lanes), -jnp.inf, f32)
    for a, size in chunks(n):
        s = dot(x_ref[0, a : a + size], q, 1, 0)
        s_ref[a : a + size] = s
        top = jnp.maximum(top, jnp.max(s, axis=0, keepdims=True))
    total = jnp.zeros((wide, lanes), f32)
    for a, size in chunks(n):
        p = jnp.exp(s_ref[a : a + size] - top).astype(bf16)
        p_ref[0, a : a + size] = p
        total = total + dot(t_ref[0, :, a : a + size], p, 1, 0)
    top_ref[0] = top
    tile = total[wide - 8 :]
    at = lax.broadcasted_iota(jnp.int32, tile.shape, 0)
    tile = jnp.where(at == TOP, top, jnp.where(at == ONE, tile, 0.0))
    unlay_lanes(i, rows, jnp.concatenate([total[: wide - 8], tile], axis=0), pm_ref, pt_ref)


def merge_kernel(a_ref, b_ref, *out_refs):
    blocks, wide, lanes = a_ref.shape
    base = wide - 8
    for k, ref in enumerate(out_refs):
        ta, tb = a_ref[k, pl.ds(base + TOP, 1)], b_ref[k, pl.ds(base + TOP, 1)]
        top = jnp.maximum(ta, tb)
        wa, wb = jnp.exp(ta - top), jnp.exp(tb - top)
        total = a_ref[k, pl.ds(base + ONE, 1)] * wa + b_ref[k, pl.ds(base + ONE, 1)] * wb
        ref[:base] = a_ref[k, :base] * wa + b_ref[k, :base] * wb
        ref[base:] = tail_rows({ONE: total, TOP: top}, lanes)


def mlp_kernel(feats, n_got, keep_ref, *refs):
    got_refs, refs = refs[:n_got], refs[n_got:]
    x_ref, g_ref, hi_ref, lo_ref, gain_ref, shift_ref, wu_ref, bu_ref, wd_ref, bd_ref, dact_ref, *outs = refs
    new_ref, dres_ref, trio_ref, ctx_ref, back_ref, csum_ref = outs
    wide, lanes = keep_ref.shape
    base = wide - 8
    part_refs = (keep_ref, *got_refs)
    parts = [ref[...] for ref in part_refs]
    tops = [ref[pl.ds(base + TOP, 1)] for ref in part_refs]
    sums = [ref[pl.ds(base + ONE, 1)] for ref in part_refs]
    peak = functools.reduce(jnp.maximum, tops)
    total = jnp.zeros((1, lanes), f32)
    ctx = jnp.zeros((wide, lanes), f32)
    for v, top, part in zip(parts, tops, sums):
        share = jnp.exp(top - peak)
        total = total + part * share
        ctx = ctx + v * share
    ctx = ctx / total
    lse = peak + jnp.log(total)
    row = lax.broadcasted_iota(jnp.int32, (wide, lanes), 0)
    ctx = jnp.where(row < feats, ctx, 0.0)
    ctx_ref[...] = ctx
    ctx_b = ctx.astype(bf16)
    resid = x_ref[...].astype(f32) + dot(ctx_b, hi_ref[...], 0, 0) + dot(ctx_b, lo_ref[...], 0, 0)
    hat, scale = norm_parts(resid)
    normed = (hat * gain_ref[...] + shift_ref[...]).astype(bf16)
    trio_ref[0] = normed
    pre = dot(normed, wu_ref[...], 1, 0) + bu_ref[...]
    act_f, slope = gelu_and_slope(pre)
    act = act_f.astype(bf16)
    trio_ref[1] = act
    d_pre = (dact_ref[...] * slope).astype(bf16)
    trio_ref[2] = d_pre
    d_normed = dot(d_pre, wu_ref[...], 1, 1)
    g = g_ref[...].astype(f32)
    d_resid = g + norm_back(d_normed, hat, scale, gain_ref[...])
    dres_ref[...] = d_resid
    d_resid_b = d_resid.astype(bf16)
    d_ctx = (dot(hi_ref[...], d_resid_b, 1, 1) + dot(lo_ref[...], d_resid_b, 1, 1)).astype(bf16)
    delta = jnp.sum(ctx * d_ctx.astype(f32), axis=0, keepdims=True)
    rows = {ONE + k: -v for k, v in enumerate(split3(delta))}
    rows.update({TOP + k: v for k, v in enumerate(split3(lse))})
    back_ref[...] = jnp.concatenate([d_ctx[:base], tail_rows(rows, lanes).astype(bf16)], axis=0)
    new_ref[...] = (resid + dot(act, wd_ref[...], 1, 0) + bd_ref[...]).astype(bf16)
    c = dot(ctx_b, d_resid_b, 1, 0)
    vectors = {
        0: jnp.sum(d_normed * hat, axis=0, keepdims=True),
        1: jnp.sum(d_normed, axis=0, keepdims=True),
        2: jnp.sum(d_pre.astype(f32), axis=0, keepdims=True),
        3: jnp.sum(g, axis=0, keepdims=True),
    }
    csum_ref[...] = jnp.concatenate([c[:base], tail_rows(vectors, c.shape[1])], axis=0)


def back_kernel(rows, x_ref, t_ref, p_ref, top_ref, *refs):
    sides, (ds_ref, dc_ref, dm_ref, dt_ref, b_ref) = refs[:2], refs[2:]
    i = pl.program_id(0)
    pix = x_ref.shape[1]
    wide, lanes = b_ref.shape
    lay_lanes(i, rows, sides, b_ref)
    b = b_ref[...]
    tail = b[wide - 16 :].astype(f32)[8:]
    at = lax.broadcasted_iota(jnp.int32, tail.shape, 0)
    lse = jnp.sum(jnp.where((at >= TOP) & (at < TOP + 3), tail, 0.0), axis=0, keepdims=True)
    ratio = jnp.exp(top_ref[0] - lse)
    dc_ref[0] = (b.astype(f32) * ratio).astype(bf16)
    sums = jnp.zeros((wide, lanes), f32)
    for a, size in chunks(pix):
        d = dot(x_ref[0, a : a + size], b, 1, 0)
        ds = (p_ref[0, a : a + size].astype(f32) * (d * ratio)).astype(bf16)
        ds_ref[0, a : a + size] = ds
        sums = sums + dot(t_ref[0, :, a : a + size], ds, 1, 0)
    unlay_lanes(i, rows, sums, dm_ref, dt_ref)


def pixel_grad_kernel(feats, ds_ref, p_ref, q_ref, dc_ref, out_ref):
    for i in range(ds_ref.shape[0]):
        v = dot(q_ref[i], ds_ref[i], 1, 1) + dot(dc_ref[i], p_ref[i], 1, 1)
        out_ref[:, i, :] = v[:feats]


def latent_kernel(scale, n_got, cut, *refs):
    dq_refs, refs = refs[: n_got + 1], refs[n_got + 1 :]
    ctx_ref, x_ref, normed_ref, gain_ref, wk_ref, wq_ref, dres_ref, c_ref, *outs = refs
    lat_ref, *outs, dq_ref = outs
    feats = wk_ref.shape[0]
    wide, lanes = dq_ref.shape
    base = wide - 8
    dq_ref[...] = dq_refs[0][...]
    for ref in dq_refs[1:]:
        dq_ref[...] += ref[:wide].astype(f32)
    d = dq_ref[...] - dq_ref[pl.ds(base + ONE, 1)] * ctx_ref[...]
    row = lax.broadcasted_iota(jnp.int32, (wide, lanes), 0)
    d = jnp.where(row < feats, d, 0.0).astype(bf16)
    d_query = dot(d[:feats], wk_ref[...], 0, 0).astype(bf16)
    d_normed = dot(d_query, wq_ref[...], 1, 1) * scale
    hat, spread = norm_parts(x_ref[...].astype(f32))
    vectors = {
        0: jnp.sum(d_normed * hat, axis=0, keepdims=True),
        1: jnp.sum(d_normed, axis=0, keepdims=True),
    }
    both_ref = outs[-1]
    both_ref[:base] = dot(d, normed_ref[...], 1, 0)[:base]
    both_ref[base:wide] = tail_rows(vectors, both_ref.shape[1])
    both_ref[wide:] = c_ref[...]
    if cut:
        mine_ref, twin_ref = outs[:2]
        core, chip, _ = position()
        n, _, part = mine_ref.shape
        for b in range(n):
            at = (chip ^ b) * part
            mine_ref[b] = both_ref[:, slot(core * n * part + at, part)]
            twin_ref[b] = both_ref[:, slot((1 - core) * n * part + at, part)].astype(bf16)
    lat_ref[...] = dres_ref[...] + norm_back(d_normed, hat, spread, gain_ref[...])


def halves_kernel(*refs):
    mine_ref, other_ref = refs[-2:]
    core, half = position()[0], mine_ref.shape[2]
    for j, ref in enumerate(refs[:-2]):
        mine_ref[j] = ref[:, slot(core * half, half)]
        other_ref[j] = ref[:, slot((1 - core) * half, half)]


def up_kernel(n, trio_ref, twin_ref, back_ref, *refs):
    core, chip, z = position()
    up_refs, act_refs = refs[:n], refs[n:]
    tall, half = up_refs[0].shape
    part = up_refs[1].shape[1]
    cols = slot(core * half, half)
    slab = act_refs[0].shape[1]
    for j, ref in enumerate(act_refs):
        rows = slot(lax.rem(z + j, len(act_refs)) * slab, slab)
        ref[...] = jnp.concatenate([trio_ref[1, :, rows], twin_ref[1, :, rows]], axis=0)
    d_pre = jnp.concatenate([trio_ref[2, :, cols], twin_ref[2, :, cols]], axis=0)
    for m, ref in enumerate(up_refs):
        rows = slot((chip ^ m) * tall, tall)
        normed = jnp.concatenate([trio_ref[0, :, rows], twin_ref[0, :, rows]], axis=0)
        v = dot(normed, d_pre, 0, 0)
        if m == 0:
            ref[...] = v
        else:
            for q in range(half // part):
                ref[q * tall : (q + 1) * tall] = v[:, q * part : (q + 1) * part].astype(bf16)
            ref[half // part * tall :] = back_ref[...]


def part_kernel(n, *refs):
    back_ref, up_ref, *got_refs = refs[: n + 1]
    sides_ref, sum_ref = refs[n + 1 :]
    tall, half = up_ref.shape
    wide, part = back_ref.shape
    base = got_refs[0].shape[0] - wide
    sides_ref[0] = back_ref[...]
    for m, ref in enumerate(got_refs, 1):
        sides_ref[m] = ref[base:]
    for q in range(half // part):
        cols = slice(q * part, (q + 1) * part)
        v = up_ref[:, cols]
        for ref in got_refs:
            v = v + ref[q * tall : (q + 1) * tall].astype(f32)
        sum_ref[:, cols] = v


def total(refs):
    v = refs[0][...].astype(f32)
    for ref in refs[1:]:
        v = v + ref[...].astype(f32)
    return v


def split_kernel(sum_ref, *out_refs):
    z = position()[2]
    size = out_refs[0].shape[0]
    for j, ref in enumerate(out_refs):
        ref[...] = sum_ref[slot(lax.rem(z + j, len(out_refs)) * size, size)].astype(ref.dtype)


def halve_kernel(bit, *refs):
    keep_ref, send_ref, sum_ref = refs[-3:]
    sum_ref[...] = total(refs[:-3])
    size = keep_ref.shape[0]
    mine = lax.rem(lax.div(position()[2], bit), 2)
    keep_ref[...] = sum_ref[slot(mine * size, size)]
    send_ref[...] = sum_ref[slot((1 - mine) * size, size)].astype(bf16)


def fold_kernel(n, mine_ref, twin_ref, keep_ref, *out_refs):
    keep_ref[...] = mine_ref[0] + twin_ref[0].astype(f32)
    for m, ref in enumerate(out_refs, 1):
        ref[...] = (mine_ref[m] + twin_ref[m].astype(f32)).astype(bf16)


def fold_down_kernel(n_batch, mine_ref, twin_ref, g_ref, g2_ref, *refs):
    act_refs, refs = refs[:n_batch], refs[n_batch:]
    keep_ref, own_ref, *send_refs, sum_ref = refs
    chip = position()[1]
    base, part = keep_ref.shape
    size = own_ref.shape[0]
    act = jnp.concatenate([ref[...] for ref in act_refs], axis=0)
    g = jnp.concatenate([ref[j] for j in range(n_batch) for ref in (g_ref, g2_ref)], axis=0)
    sum_ref[...] = dot(act, g, 0, 0)
    keep_ref[...] = mine_ref[0] + twin_ref[0].astype(f32)
    own_ref[...] = sum_ref[slot(chip * size, size)]
    for m, ref in enumerate(send_refs, 1):
        ref[:base] = (mine_ref[m] + twin_ref[m].astype(f32)).astype(bf16)
        v = sum_ref[slot((chip ^ m) * size, size)].astype(bf16)
        for q in range(v.shape[1] // part):
            ref[base + q * size : base + (q + 1) * size] = v[:, q * part : (q + 1) * part]


def unfold_kernel(own_ref, *refs):
    got_refs, out_ref = refs[:-1], refs[-1]
    size, half = own_ref.shape
    part = got_refs[0].shape[1]
    base = got_refs[0].shape[0] - size * (half // part)
    for q in range(half // part):
        cols = slice(q * part, (q + 1) * part)
        v = own_ref[:, cols]
        for ref in got_refs:
            v = v + ref[base + q * size : base + (q + 1) * size].astype(f32)
        out_ref[:, cols] = v.astype(bf16)


def add_kernel(*refs):
    refs[-1][...] = total(refs[:-1]).astype(refs[-1].dtype)


def stack_kernel(*refs):
    for j, ref in enumerate(refs[:-1]):
        refs[-1][j] = ref[...]


def forward_kernel(x_ref, y_ref, low_ref, high_ref):
    half = low_ref.shape[0]
    low_ref[...] = x_ref[:half]
    high_ref[...] = y_ref[half:]


def place_kernel(masks, firsts, n_old, *refs):
    n = len(masks)
    core, chip, z = position()
    pieces, (up_ref, down_ref, held_ref, sems) = refs[: 2 * n], refs[2 * n + n_old :]
    half = up_ref.shape[1] // 2
    n_batch = up_ref.shape[0] // (4 * held_ref.shape[1])
    size = held_ref.shape[1]
    copies = []
    for i, (m, first) in enumerate(zip(masks, firsts)):
        for j in range(pieces[i].shape[0]):
            k, z_at = chip ^ m, z ^ z_masks(n_batch)[first + j]
            for h, (out_ref, row) in enumerate(((up_ref, k * n_batch + z_at), (down_ref, z_at * 4 + k))):
                at = len(copies)
                for side, col in enumerate((core, 1 - core)):
                    held_ref[at, :, slot(col * half, half)] = pieces[side * n + i][j, h].astype(f32)
                copy = pltpu.make_async_copy(held_ref.at[at], out_ref.at[slot(row * size, size)], sems.at[at])
                copy.start()
                copies.append(copy)
    for copy in copies:
        copy.wait()


def final_kernel(scale, n, *refs):
    pieces, refs = refs[: 1 + (n > 0)], refs[1 + (n > 0) :]
    wq_ref, wk_ref, wv_ref, wo_ref, gq_ref, gk_ref, gv_ref, go_ref, *vector_refs, both_ref = refs
    j = pl.program_id(0)
    feats = wk_ref.shape[0]
    wide = both_ref.shape[0] // 2
    tall = gq_ref.shape[0]

    @pl.when(j == 0)
    def _():
        if n == 0:
            both_ref[...] = pieces[0][...].astype(bf16)
        else:
            core, chip, _ = position()
            for side, col in enumerate((core, 1 - core)):
                part = pieces[side].shape[2]
                for b in range(n):
                    both_ref[:, slot(col * n * part + (chip ^ b) * part, part)] = pieces[side][b]
        for k, ref in enumerate(vector_refs):
            base, at = (wide, k) if k < 2 else (2 * wide, k - 2)
            ref[...] = both_ref[base - 16 : base].astype(f32)[8 + at : 9 + at]

    m, c = both_ref[:wide], both_ref[wide:]
    gk_ref[...] = (dot(m, wq_ref[...], 1, 0) * scale)[:feats]
    gq_ref[...] = dot(both_ref[:wide, slot(j * tall, tall)][:feats], wk_ref[...], 0, 0) * scale
    gv_ref[...] = dot(c, wo_ref[...], 1, 1)[:feats]
    go_ref[...] = dot(wv_ref[...], c[:feats], 0, 0)


def seq_send(v, mask, n):
    return lax.ppermute(v, "seq", [(i, i ^ mask) for i in range(n)])


def batch_send(v, shift, n):
    return lax.ppermute(v, "batch", [(i, (i + shift) % n) for i in range(n)])


def z_masks(n):
    masks = [0]
    while len(masks) < n:
        masks = masks + [m ^ (2 * len(masks) - 1) for m in masks]
    return masks


class Comm:
    def __init__(self, n_seq, n_batch):
        self.n_seq, self.n_batch = n_seq, n_batch
        self.chips = n_seq // 2

    def twin(self, v):
        return seq_send(v, 1, self.n_seq)

    def swap_chip(self, v, mask):
        return seq_send(v, 2 * mask, self.n_seq)

    def to_chips(self, pieces):
        return [seq_send(v, 2 * m, self.n_seq) for m, v in enumerate(pieces, 1)]

    def to_z(self, pieces):
        n = self.n_batch
        order = sorted(range(1, n), key=lambda j: min(j, n - j))
        got = {j: batch_send(pieces[j - 1], j, n) for j in order}
        return [got[j] for j in range(1, n)]

    def next_z(self, v):
        return batch_send(v, 1, self.n_batch)

    def sum_scatter_z(self, pieces, mask, end):
        while mask > end:
            size, half = pieces[0].shape[0] // 2, pieces[0].shape[1]
            keep, send = call(
                functools.partial(halve_kernel, mask // 2),
                [shape((size, half), f32), shape((size, half), bf16)],
                scratch=[pltpu.VMEM((2 * size, half), f32)],
            )(*pieces)
            pairs = [(i, i ^ (mask - 1)) for i in range(self.n_batch)]
            pieces = [keep, lax.ppermute(send, "batch", pairs)]
            mask //= 2
        return pieces

    def sum_z(self, v):
        mask = 1
        while mask < self.n_batch:
            pairs = [(i, i ^ (2 * mask - 1)) for i in range(self.n_batch)]
            other = lax.ppermute(v, "batch", pairs)
            v = call(add_kernel, shape(v.shape, v.dtype))(v, other)
            mask *= 2
        return v

    def all_z(self, v):
        got = [v]
        while len(got) < self.n_batch:
            pairs = [(i, i ^ (2 * len(got) - 1)) for i in range(self.n_batch)]
            got = got + [lax.ppermute(piece, "batch", pairs) for piece in got]
        return got

    def all_chips(self, v):
        return [v] + self.to_chips([v] * (self.chips - 1))

    def spread(self, v, beside):
        mine, beside = tie(self.all_chips(v), beside)
        mine = call(stack_kernel, shape((self.chips, *v.shape), v.dtype))(*mine)
        return [mine, self.twin(mine)], beside


def tie(first, second):
    out = lax.optimization_barrier((*first, *second))
    return list(out[: len(first)]), list(out[len(first) :])


def add_all(first, rest):
    for v in rest:
        first = first + v.astype(f32)
    return first


def shards(
    n_seq,
    n_batch,
    latents,
    pixels,
    keep_mask,
    gain_attn,
    shift_attn,
    w_query,
    w_key,
    w_value,
    w_out,
    gain_mlp,
    shift_mlp,
    w_up,
    bias_up,
    w_down,
    bias_down,
    cotangent,
):
    images, rows, width = latents.shape
    pix, feats = pixels.shape[1:]
    hidden = w_up.shape[1]
    wide = -(-(feats + 8) // 16) * 16
    lanes = images * rows
    scale = width ** (-0.5)
    comm = Comm(n_seq, n_batch)
    blocks = comm.chips
    every = n_seq * rows
    x = latents.reshape(lanes, width)
    g = cotangent.reshape(lanes, width)
    gain1, shift1, gain2, shift2, b_up, b_down = (
        v.reshape(1, -1) for v in (gain_attn, shift_attn, gain_mlp, shift_mlp, bias_up, bias_down)
    )
    small = (blocks, wide, lanes)

    operands = (x, gain1, shift1, w_query, w_key)
    qk, normed = call(
        functools.partial(query_kernel, scale),
        [shape((wide, lanes), bf16), shape((lanes, width), bf16)],
        ins=[pl.BlockSpec(memory_space=pltpu.HBM)] * 5,
        scratch=[pltpu.VMEM(v.shape, v.dtype) for v in operands]
        + [pltpu.VMEM((wide, lanes), f32), pltpu.SemaphoreType.DMA((5,))],
        limit=60 << 20,
    )(*operands)

    pix_x, pix_t = call(
        pixel_kernel,
        [shape((images, pix, wide), bf16), shape((images, wide, pix), bf16)],
        grid=(images,),
        ins=[one_of((feats, pix)), whole((images, pix))],
        outs=[one_of((pix, wide)), one_of((wide, pix))],
        scratch=[pltpu.VMEM((wide, pix), f32)],
    )(pixels.transpose(0, 2, 1), keep_mask)
    (qk,), g_all = tie([qk], [g])
    g_all.append(comm.next_z(g_all[0]))
    q_sides, (pix_x, g_all[1]) = comm.spread(qk, [pix_x, g_all[1]])
    vo_hi, vo_lo, d_act = call(
        weight_kernel,
        [shape((wide, width), bf16)] * 2 + [shape((lanes, hidden), f32)],
        scratch=[pltpu.VMEM((wide, width), f32)],
    )(w_value, w_out, g, w_down)

    probs, q_all, top, part_mine, part_twin = call(
        functools.partial(attend_kernel, rows),
        [
            shape((images, pix, every), bf16),
            shape((images, wide, every), bf16),
            shape((images, 1, every), f32),
            shape(small, f32),
            shape(small, f32),
        ],
        grid=(images,),
        ins=[one_of((pix, wide)), one_of((wide, pix))] + [whole(small)] * 2,
        outs=[one_of((pix, every)), one_of((wide, every)), one_of((1, every)), whole(small), whole(small)],
        scratch=[pltpu.VMEM((pix, every), f32)],
    )(pix_x, pix_t, *q_sides)
    keep, *send = call(merge_kernel, [shape((wide, lanes), f32)] * blocks)(
        part_mine, comm.twin(part_twin)
    )
    g_next = comm.next_z(g_all[-1])
    got, (g_next,) = tie(comm.to_chips(send), [g_next])
    g_all.append(g_next)

    new_latents, d_resid, trio, ctx, back, c_part = call(
        functools.partial(mlp_kernel, feats, blocks - 1),
        [
            shape((lanes, width), bf16),
            shape((lanes, width), f32),
            shape((3, lanes, width), bf16),
            shape((wide, lanes), f32),
            shape((wide, lanes), bf16),
            shape((wide, width), f32),
        ],
    )(keep, *got, x, g, vo_hi, vo_lo, gain2, shift2, w_up, b_up, w_down, b_down, d_act)

    half = width // 2
    part = half // blocks
    quarter, tall, size = width // blocks, width // n_batch, width // blocks // n_batch
    cut = part == lanes and part % 128 == 0 and size % 16 == 0 and blocks == 4 and n_batch == 4
    tall = hidden // n_batch
    if cut:
        up = call(
            functools.partial(up_kernel, blocks),
            [shape((quarter, half), f32)]
            + [shape((blocks * quarter + wide, part), bf16)] * (blocks - 1)
            + [shape((2 * lanes, tall), bf16)] * n_batch,
        )(trio, comm.twin(trio), back)
        up, act = list(up[:blocks]), list(up[blocks:])
        for _ in range(3, n_batch):
            g_all.append(comm.next_z(g_all[-1]))
        up[1:] = comm.to_chips(up[1:])
        act[1:] = comm.to_z(act[1:])
        up, rest = tie(up, [*act, *g_all[3:]])
        act, g_all[3:] = rest[:n_batch], rest[n_batch:]
        sides, up = call(
            functools.partial(part_kernel, blocks), [shape(small, bf16), shape((quarter, half), f32)]
        )(back, *up)
        back_sides = [sides, comm.twin(sides)]
        g_mine, g_twin = call(halves_kernel, [shape((n_batch, lanes, half), bf16)] * 2)(*g_all)
        g_twin = comm.twin(g_twin)
    else:
        back_sides, _ = comm.spread(back, [])
    d_scores, d_ctx_all, dq_mine, dq_twin = call(
        functools.partial(back_kernel, rows),
        [
            shape((images, pix, every), bf16),
            shape((images, wide, every), bf16),
            shape(small, f32),
            shape(small, bf16),
        ],
        grid=(images,),
        ins=[one_of((pix, wide)), one_of((wide, pix)), one_of((pix, every)), one_of((1, every))]
        + [whole(small)] * 2,
        outs=[one_of((pix, every)), one_of((wide, every)), whole(small), whole(small)],
        scratch=[pltpu.VMEM((wide, every), bf16)],
    )(pix_x, pix_t, probs, top, *back_sides)

    step = 256
    pixel_grad = call(
        functools.partial(pixel_grad_kernel, feats),
        shape((feats, images, pix), f32),
        grid=(-(-pix // step),),
        ins=[pl.BlockSpec((images, step, every), lambda j: (0, j, 0))] * 2 + [whole((images, wide, every))] * 2,
        outs=pl.BlockSpec((feats, images, step), lambda j: (0, 0, j)),
    )(d_scores, probs, q_all, d_ctx_all)

    def place(masks, firsts, pieces, old=()):
        count = 2 * sum(v.shape[0] for v in pieces)
        hbm, vmem = pl.BlockSpec(memory_space=pltpu.HBM), pl.BlockSpec(memory_space=pltpu.VMEM)
        return list(
            pl.pallas_call(
                functools.partial(place_kernel, masks, firsts, len(old)),
                out_shape=[shape((width, width), f32)] * 2,
                in_specs=[vmem] * (2 * len(pieces)) + [hbm] * len(old),
                out_specs=[hbm] * 2,
                scratch_shapes=[pltpu.VMEM((count, size, width), f32), pltpu.SemaphoreType.DMA((count,))],
                input_output_aliases={2 * len(pieces) + i: i for i in range(len(old))},
                compiler_params=pltpu.CompilerParams(vmem_limit_bytes=VMEM_LIMIT),
            )(*pieces, *map(comm.twin, pieces), *old)
        )

    def folded(mine, twin):
        return call(
            functools.partial(fold_kernel, blocks),
            [shape(mine.shape[1:], f32)] + [shape(mine.shape[1:], bf16)] * (blocks - 1),
        )(mine, comm.twin(twin))

    if cut:
        up_keep, *up_send = call(
            split_kernel, [shape((size, half), f32)] + [shape((size, half), bf16)] * (n_batch - 1)
        )(up)
        (dq_twin,), up = tie([dq_twin], [up_keep] + comm.to_z(up_send))
        first, down, *rest = call(
            functools.partial(fold_down_kernel, n_batch),
            [shape((wide, lanes), f32), shape((size, half), f32)]
            + [shape((wide + blocks * size, lanes), bf16)] * (blocks - 1),
            scratch=[pltpu.VMEM((tall, half), f32)],
        )(dq_mine, comm.twin(dq_twin), g_mine, g_twin, *act)
        dq = [first] + comm.to_chips(rest)
    else:
        first, *rest = folded(dq_mine, dq_twin)
        dq = [first] + comm.to_chips(rest)
    latent_grad, *both = call(
        functools.partial(latent_kernel, scale, blocks - 1, cut),
        [shape((lanes, width), f32)]
        + [shape((blocks, 2 * wide, part), f32), shape((blocks, 2 * wide, part), bf16)] * cut
        + [shape((2 * wide, width), f32)] * (not cut),
        scratch=[pltpu.VMEM((2 * wide, width), f32)] * cut + [pltpu.VMEM((wide, lanes), f32)],
    )(*dq, ctx, x, normed, gain1, w_key, w_query, d_resid, c_part)
    if cut:
        first, *rest = folded(*both)
        up = call(add_kernel, shape((size, half), bf16))(*up)
        down = call(unfold_kernel, shape((size, half), bf16))(down, *dq[1:])
        own = call(stack_kernel, shape((2, size, half), bf16))(up, down)
        sums, (pixel_grad, *own) = tie([first] + comm.to_chips(rest), [pixel_grad, *comm.all_z(own)])
        own = call(stack_kernel, shape((n_batch, 2, size, half), bf16))(*own)
        sums = call(add_kernel, shape((2 * wide, part), bf16))(*sums)
        own = [own] + [comm.swap_chip(own, m) for m in (1, 2)]
        (sums,), own = tie([comm.sum_z(sums)], own)
        low, high = call(forward_kernel, [shape((n_batch // 2, 2, size, half), bf16)] * 2)(*own[1:])
        far = [comm.swap_chip(low, 2), comm.swap_chip(high, 1)]
        grads = place((0, 1, 2), (0, 0, 0), own)
        pieces, (*far, grads[0], grads[1]) = tie(comm.all_chips(sums), [*far, *grads])
        pieces = call(stack_kernel, shape((blocks, 2 * wide, part), bf16))(*pieces)
        grad_up, grad_down = place((3, 3), (0, n_batch // 2), far, grads)
        pieces = [pieces, comm.twin(pieces)]
    else:
        pieces = [lax.psum(both[0], ("batch", "seq"))]
    quart = width // 2
    by_rows = pl.BlockSpec((quart, width), lambda j: (j, 0))
    by_columns = pl.BlockSpec((feats, quart), lambda j: (0, j))
    row = whole((1, width))
    grad_query, grad_key, grad_value, grad_out, *vectors = call(
        functools.partial(final_kernel, scale, blocks if cut else 0),
        [
            shape((width, width), f32),
            shape((feats, width), f32),
            shape((feats, width), f32),
            shape((width, width), f32),
        ]
        + [shape((1, width), f32)] * 6,
        grid=(2,),
        ins=[whole(v.shape) for v in pieces]
        + [pl.BlockSpec((width, quart), lambda j: (0, j)), whole((feats, width)), by_columns, by_rows],
        outs=[by_rows, by_columns, by_columns, by_rows] + [row] * 6,
        scratch=[pltpu.VMEM((2 * wide, width), bf16)],
    )(*pieces, w_query, w_key, w_value, w_out)
    vectors = [v.reshape(width) for v in vectors]
    if not cut:
        grad_up = lax.psum(dot(trio[0], trio[2], 0, 0), ("batch", "seq"))
        grad_down = lax.psum(dot(trio[1], g, 0, 0), ("batch", "seq"))
    dims = (images, rows, width)
    return (
        new_latents.reshape(dims),
        latent_grad.reshape(dims),
        pixel_grad.transpose(1, 2, 0),
        vectors[0],
        vectors[1],
        grad_query,
        grad_key,
        grad_value,
        grad_out,
        vectors[2],
        vectors[3],
        grad_up,
        vectors[4],
        grad_down,
        vectors[5],
    )


def solution(mesh):
    split = P("batch", "seq", None)
    placed = (split, split, P("batch", "seq")) + (P(),) * 12 + (split,)
    return jax.shard_map(
        functools.partial(shards, mesh.shape["seq"], mesh.shape["batch"]),
        mesh=mesh,
        in_specs=placed,
        out_specs=(split, split, split) + (P(),) * 12,
        check_vma=False,
    )
```

```python
import functools

import jax
import jax.numpy as jnp
from jax import lax
from jax.experimental import pallas as pl
from jax.experimental.pallas import tpu as pltpu
from jax.sharding import PartitionSpec as P

f32 = jnp.float32
bf16 = jnp.bfloat16
EPS = 1e-05
DROP = -1e30
ONE, TOP, MASK = 0, 3, 6
VMEM_LIMIT = 20 << 20


def dot(a, b, ca, cb):
    return lax.dot_general(a, b, (((ca,), (cb,)), ((), ())), preferred_element_type=f32)


def shape(dims, dtype):
    return jax.ShapeDtypeStruct(dims, dtype)


def call(body, out, grid=(), ins=None, outs=None, scratch=(), limit=VMEM_LIMIT):
    kwargs = {}
    if grid:
        kwargs = dict(grid=grid, in_specs=ins, out_specs=outs)
    elif ins:
        kwargs = dict(in_specs=ins)
    return pl.pallas_call(
        body,
        out_shape=out,
        scratch_shapes=list(scratch),
        compiler_params=pltpu.CompilerParams(vmem_limit_bytes=limit),
        **kwargs,
    )


def whole(dims):
    return pl.BlockSpec(dims, lambda *_: (0,) * len(dims))


def one_of(dims):
    return pl.BlockSpec((1,) + dims, lambda i, *_: (i,) + (0,) * len(dims))


def split3(v):
    hi = v.astype(bf16).astype(f32)
    mid = (v - hi).astype(bf16).astype(f32)
    return hi, mid, v - hi - mid


def position():
    s = lax.axis_index("seq")
    return lax.rem(s, 2), lax.div(s, 2), lax.axis_index("batch")


def slot(start, size):
    return pl.ds(pl.multiple_of(start, size), size)


def tail_rows(rows, lanes):
    at = lax.broadcasted_iota(jnp.int32, (8, lanes), 0)
    tile = jnp.zeros((8, lanes), f32)
    for k, v in rows.items():
        tile = jnp.where(at == k, v, tile)
    return tile


def norm_parts(v):
    mean = jnp.mean(v, axis=-1, keepdims=True)
    centered = v - mean
    spread = jnp.mean(centered * centered, axis=-1, keepdims=True)
    scale = lax.rsqrt(spread + EPS)
    return centered * scale, scale


def norm_back(d_out, hat, scale, gain):
    d_hat = d_out * gain
    mean = jnp.mean(d_hat, axis=-1, keepdims=True)
    along = jnp.mean(d_hat * hat, axis=-1, keepdims=True)
    return scale * (d_hat - mean - hat * along)


def gelu_and_slope(v):
    cdf = 0.5 * (1.0 + lax.erf(v * (0.5**0.5)))
    pdf = jnp.exp(-0.5 * v * v) * (1.0 / (2.0 * 3.141592653589793) ** 0.5)
    return v * cdf, cdf + v * pdf


def chunks(n, size=256):
    return [(a, min(size, n - a)) for a in range(0, n, size)]


def query_kernel(scale, *refs):
    sources, (qk_ref, normed_ref), refs = refs[:5], refs[5:7], refs[7:]
    held, (pad_ref, sems) = refs[:5], refs[5:]
    x_ref, gain_ref, shift_ref, wq_ref, wk_ref = held
    steps = sems.shape[0] - 4
    tall = wq_ref.shape[0] // steps
    copies = [pltpu.make_async_copy(sources[k], held[k], sems.at[k]) for k in range(3)]
    for k in range(steps):
        rows = slice(k * tall, (k + 1) * tall)
        copies.append(pltpu.make_async_copy(sources[3].at[rows], wq_ref.at[rows], sems.at[3 + k]))
    copies.append(pltpu.make_async_copy(sources[4], wk_ref, sems.at[3 + steps]))
    for copy in copies:
        copy.start()
    feats = wk_ref.shape[0]
    wide, lanes = qk_ref.shape
    for copy in copies[:3]:
        copy.wait()
    hat, _ = norm_parts(x_ref[...].astype(f32))
    normed = (hat * gain_ref[...] + shift_ref[...]).astype(bf16)
    normed_ref[...] = normed
    pad_ref[wide - 16 :] = jnp.zeros((16, lanes), f32)
    query = jnp.zeros((lanes, wq_ref.shape[1]), f32)
    for k in range(steps):
        rows = slice(k * tall, (k + 1) * tall)
        copies[3 + k].wait()
        query = query + dot(normed[:, rows], wq_ref[rows], 1, 0)
    copies[3 + steps].wait()
    pad_ref[:feats] = dot(wk_ref[...], (query * scale).astype(bf16), 1, 1)
    pad_ref[wide - 8 :] = tail_rows({MASK: 1.0}, lanes)
    qk_ref[...] = pad_ref[...].astype(bf16)


def pixel_kernel(pix_ref, keep_ref, x_ref, t_ref, pad_ref):
    feats, n = pix_ref.shape[1:]
    wide = t_ref.shape[1]
    keep = keep_ref[pl.ds(pl.program_id(0), 1), :]
    bias = jnp.where(keep > 0, 0.0, DROP).astype(f32)
    pad_ref[wide - 16 :] = jnp.zeros((16, n), f32)
    pad_ref[:feats] = pix_ref[0].astype(f32)
    pad_ref[wide - 8 :] = tail_rows({ONE: 1.0, ONE + 1: 1.0, ONE + 2: 1.0, MASK: bias}, n)
    t_ref[0] = pad_ref[...].astype(bf16)
    x_ref[0] = pad_ref[...].T.astype(bf16)


def weight_kernel(wv_ref, wo_ref, g_ref, wd_ref, hi_ref, lo_ref, dact_ref, pad_ref):
    feats = wv_ref.shape[0]
    pad_ref[...] = jnp.zeros(pad_ref.shape, f32)
    pad_ref[:feats] = dot(wv_ref[...], wo_ref[...], 1, 0)
    v = pad_ref[...]
    hi = v.astype(bf16)
    hi_ref[...] = hi
    lo_ref[...] = (v - hi.astype(f32)).astype(bf16)
    dact_ref[...] = dot(g_ref[...], wd_ref[...], 1, 1)


def lay_lanes(i, rows, refs, out_ref):
    for k in range(2):

        @pl.when(i == k)
        def _():
            parts = [ref[b, :, k * rows : (k + 1) * rows] for ref in refs for b in range(ref.shape[0])]
            out_ref[...] = jnp.concatenate(parts, axis=1)


def unlay_lanes(i, rows, v, mine_ref, twin_ref):
    blocks = mine_ref.shape[0]
    for k in range(2):

        @pl.when(i == k)
        def _():
            for b in range(2 * blocks):
                ref = (mine_ref, twin_ref)[b // blocks]
                piece = v[:, b * rows : (b + 1) * rows].astype(ref.dtype)
                ref[b % blocks, :, k * rows : (k + 1) * rows] = piece


def attend_kernel(rows, x_ref, t_ref, *refs):
    *sides, p_ref, q_ref, top_ref, pm_ref, pt_ref, s_ref = refs
    i = pl.program_id(0)
    n = x_ref.shape[1]
    wide, lanes = q_ref.shape[1:]
    lay_lanes(i, rows, sides, q_ref.at[0])
    q = q_ref[0]
    top = jnp.full((1, lanes), -jnp.inf, f32)
    for a, size in chunks(n):
        s = dot(x_ref[0, a : a + size], q, 1, 0)
        s_ref[a : a + size] = s
        top = jnp.maximum(top, jnp.max(s, axis=0, keepdims=True))
    total = jnp.zeros((wide, lanes), f32)
    for a, size in chunks(n):
        p = jnp.exp(s_ref[a : a + size] - top).astype(bf16)
        p_ref[0, a : a + size] = p
        total = total + dot(t_ref[0, :, a : a + size], p, 1, 0)
    top_ref[0] = top
    tile = total[wide - 8 :]
    at = lax.broadcasted_iota(jnp.int32, tile.shape, 0)
    tile = jnp.where(at == TOP, top, jnp.where(at == ONE, tile, 0.0))
    unlay_lanes(i, rows, jnp.concatenate([total[: wide - 8], tile], axis=0), pm_ref, pt_ref)


def merge_kernel(a_ref, b_ref, keep_ref, *send_refs):
    blocks, wide, lanes = a_ref.shape
    base = wide - 8
    for k, ref in enumerate((keep_ref, *send_refs)):
        ta, tb = a_ref[k, pl.ds(base + TOP, 1)], b_ref[k, pl.ds(base + TOP, 1)]
        top = jnp.maximum(ta, tb)
        wa, wb = jnp.exp(ta - top), jnp.exp(tb - top)
        sums = a_ref[k, pl.ds(base + ONE, 1)] * wa + b_ref[k, pl.ds(base + ONE, 1)] * wb
        v = a_ref[k, :base] * wa + b_ref[k, :base] * wb
        rows = {ONE + j: piece for j, piece in enumerate(split3(sums))}
        rows.update({TOP + j: piece for j, piece in enumerate(split3(top))})
        ref[...] = jnp.concatenate([v, tail_rows(rows, lanes)], axis=0).astype(ref.dtype)


def mlp_kernel(feats, n_got, keep_ref, *refs):
    got_refs, refs = refs[:n_got], refs[n_got:]
    x_ref, g_ref, hi_ref, lo_ref, gain_ref, shift_ref, wu_ref, bu_ref, wd_ref, bd_ref, dact_ref, *outs = refs
    new_ref, dres_ref, trio_ref, ctx_ref, back_ref, csum_ref = outs
    wide, lanes = keep_ref.shape
    base = wide - 8
    parts = [keep_ref[...]] + [ref[...].astype(f32) for ref in got_refs]
    at = lax.broadcasted_iota(jnp.int32, (8, lanes), 0)
    tops, sums = (
        [jnp.sum(jnp.where((at >= k) & (at < k + 3), v[base:], 0.0), axis=0, keepdims=True) for v in parts]
        for k in (TOP, ONE)
    )
    peak = functools.reduce(jnp.maximum, tops)
    total = jnp.zeros((1, lanes), f32)
    ctx = jnp.zeros((wide, lanes), f32)
    for v, top, part in zip(parts, tops, sums):
        share = jnp.exp(top - peak)
        total = total + part * share
        ctx = ctx + v * share
    ctx = ctx / total
    lse = peak + jnp.log(total)
    row = lax.broadcasted_iota(jnp.int32, (wide, lanes), 0)
    ctx = jnp.where(row < feats, ctx, 0.0)
    ctx_ref[...] = ctx
    ctx_b = ctx.astype(bf16)
    resid = x_ref[...].astype(f32) + dot(ctx_b, hi_ref[...], 0, 0) + dot(ctx_b, lo_ref[...], 0, 0)
    hat, scale = norm_parts(resid)
    normed = (hat * gain_ref[...] + shift_ref[...]).astype(bf16)
    trio_ref[0] = normed
    pre = dot(normed, wu_ref[...], 1, 0) + bu_ref[...]
    act_f, slope = gelu_and_slope(pre)
    act = act_f.astype(bf16)
    trio_ref[1] = act
    d_pre = (dact_ref[...] * slope).astype(bf16)
    trio_ref[2] = d_pre
    d_normed = dot(d_pre, wu_ref[...], 1, 1)
    g = g_ref[...].astype(f32)
    d_resid = g + norm_back(d_normed, hat, scale, gain_ref[...])
    dres_ref[...] = d_resid
    d_resid_b = d_resid.astype(bf16)
    d_ctx = (dot(hi_ref[...], d_resid_b, 1, 1) + dot(lo_ref[...], d_resid_b, 1, 1)).astype(bf16)
    delta = jnp.sum(ctx * d_ctx.astype(f32), axis=0, keepdims=True)
    rows = {ONE + k: -v for k, v in enumerate(split3(delta))}
    rows.update({TOP + k: v for k, v in enumerate(split3(lse))})
    back_ref[...] = jnp.concatenate([d_ctx[:base], tail_rows(rows, lanes).astype(bf16)], axis=0)
    new_ref[...] = (resid + dot(act, wd_ref[...], 1, 0) + bd_ref[...]).astype(bf16)
    c = dot(ctx_b, d_resid_b, 1, 0)
    vectors = {
        0: jnp.sum(d_normed * hat, axis=0, keepdims=True),
        1: jnp.sum(d_normed, axis=0, keepdims=True),
        2: jnp.sum(d_pre.astype(f32), axis=0, keepdims=True),
        3: jnp.sum(g, axis=0, keepdims=True),
    }
    csum_ref[...] = jnp.concatenate([c[:base], tail_rows(vectors, c.shape[1])], axis=0)


def back_kernel(rows, x_ref, t_ref, p_ref, top_ref, *refs):
    sides, (ds_ref, dc_ref, dm_ref, dt_ref, b_ref) = refs[:2], refs[2:]
    i = pl.program_id(0)
    pix = x_ref.shape[1]
    wide, lanes = b_ref.shape
    lay_lanes(i, rows, sides, b_ref)
    b = b_ref[...]
    tail = b[wide - 16 :].astype(f32)[8:]
    at = lax.broadcasted_iota(jnp.int32, tail.shape, 0)
    lse = jnp.sum(jnp.where((at >= TOP) & (at < TOP + 3), tail, 0.0), axis=0, keepdims=True)
    ratio = jnp.exp(top_ref[0] - lse)
    dc_ref[0] = (b.astype(f32) * ratio).astype(bf16)
    sums = jnp.zeros((wide, lanes), f32)
    for a, size in chunks(pix):
        d = dot(x_ref[0, a : a + size], b, 1, 0)
        ds = (p_ref[0, a : a + size].astype(f32) * (d * ratio)).astype(bf16)
        ds_ref[0, a : a + size] = ds
        sums = sums + dot(t_ref[0, :, a : a + size], ds, 1, 0)
    unlay_lanes(i, rows, sums, dm_ref, dt_ref)


def pixel_grad_kernel(feats, ds_ref, p_ref, q_ref, dc_ref, out_ref):
    for i in range(ds_ref.shape[0]):
        for a, size in chunks(ds_ref.shape[1]):
            rows = slice(a, a + size)
            v = dot(q_ref[i], ds_ref[i, rows], 1, 1) + dot(dc_ref[i], p_ref[i, rows], 1, 1)
            out_ref[:, i, rows] = v[:feats]


def latent_kernel(scale, n_got, cut, *refs):
    dq_refs, refs = refs[: n_got + 1], refs[n_got + 1 :]
    ctx_ref, x_ref, normed_ref, gain_ref, wk_ref, wq_ref, dres_ref, c_ref, *outs = refs
    lat_ref, *outs, dq_ref = outs
    feats = wk_ref.shape[0]
    wide, lanes = dq_ref.shape
    base = wide - 8
    dq_ref[...] = dq_refs[0][...]
    for ref in dq_refs[1:]:
        dq_ref[...] += ref[:wide].astype(f32)
    d = dq_ref[...] - dq_ref[pl.ds(base + ONE, 1)] * ctx_ref[...]
    row = lax.broadcasted_iota(jnp.int32, (wide, lanes), 0)
    d = jnp.where(row < feats, d, 0.0).astype(bf16)
    d_query = dot(d[:feats], wk_ref[...], 0, 0).astype(bf16)
    d_normed = dot(d_query, wq_ref[...], 1, 1) * scale
    hat, spread = norm_parts(x_ref[...].astype(f32))
    vectors = {
        0: jnp.sum(d_normed * hat, axis=0, keepdims=True),
        1: jnp.sum(d_normed, axis=0, keepdims=True),
    }
    both_ref = outs[-1]
    both_ref[:base] = dot(d, normed_ref[...], 1, 0)[:base]
    both_ref[base:wide] = tail_rows(vectors, both_ref.shape[1])
    both_ref[wide:] = c_ref[...]
    if cut:
        mine_ref, twin_ref = outs[:2]
        core, chip, _ = position()
        n, _, part = mine_ref.shape
        for b in range(n):
            at = (chip ^ b) * part
            mine_ref[b] = both_ref[:, slot(core * n * part + at, part)]
            twin_ref[b] = both_ref[:, slot((1 - core) * n * part + at, part)].astype(bf16)
    lat_ref[...] = dres_ref[...] + norm_back(d_normed, hat, spread, gain_ref[...])


def halves_kernel(*refs):
    mine_ref, other_ref = refs[-2:]
    core, half = position()[0], mine_ref.shape[2]
    for j, ref in enumerate(refs[:-2]):
        mine_ref[j] = ref[:, slot(core * half, half)]
        other_ref[j] = ref[:, slot((1 - core) * half, half)]


def up_kernel(n, trio_ref, twin_ref, back_ref, *refs):
    core, chip, z = position()
    up_refs, act_refs = refs[:n], refs[n:]
    tall, half = up_refs[0].shape
    part = up_refs[1].shape[1]
    cols = slot(core * half, half)
    slab = act_refs[0].shape[1]
    for j, ref in enumerate(act_refs):
        rows = slot(lax.rem(z + j, len(act_refs)) * slab, slab)
        ref[...] = jnp.concatenate([trio_ref[1, :, rows], twin_ref[1, :, rows]], axis=0)
    d_pre = jnp.concatenate([trio_ref[2, :, cols], twin_ref[2, :, cols]], axis=0)
    for m, ref in enumerate(up_refs):
        rows = slot((chip ^ m) * tall, tall)
        normed = jnp.concatenate([trio_ref[0, :, rows], twin_ref[0, :, rows]], axis=0)
        v = dot(normed, d_pre, 0, 0)
        if m == 0:
            ref[...] = v
        else:
            for q in range(half // part):
                ref[q * tall : (q + 1) * tall] = v[:, q * part : (q + 1) * part].astype(bf16)
            ref[half // part * tall :] = back_ref[...]


def part_kernel(n, *refs):
    back_ref, up_ref, *got_refs = refs[: n + 1]
    sides_ref, sum_ref = refs[n + 1 :]
    tall, half = up_ref.shape
    wide, part = back_ref.shape
    base = got_refs[0].shape[0] - wide
    sides_ref[0] = back_ref[...]
    for m, ref in enumerate(got_refs, 1):
        sides_ref[m] = ref[base:]
    for q in range(half // part):
        cols = slice(q * part, (q + 1) * part)
        v = up_ref[:, cols]
        for ref in got_refs:
            v = v + ref[q * tall : (q + 1) * tall].astype(f32)
        sum_ref[:, cols] = v


def total(refs):
    v = refs[0][...].astype(f32)
    for ref in refs[1:]:
        v = v + ref[...].astype(f32)
    return v


def split_kernel(sum_ref, *out_refs):
    z = position()[2]
    size = out_refs[0].shape[0]
    for j, ref in enumerate(out_refs):
        ref[...] = sum_ref[slot(lax.rem(z + j, len(out_refs)) * size, size)].astype(ref.dtype)


def fold_kernel(n, mine_ref, twin_ref, keep_ref, *out_refs):
    keep_ref[...] = mine_ref[0] + twin_ref[0].astype(f32)
    for m, ref in enumerate(out_refs, 1):
        ref[...] = (mine_ref[m] + twin_ref[m].astype(f32)).astype(bf16)


def fold_down_kernel(n_batch, mine_ref, twin_ref, g_ref, g2_ref, *refs):
    act_refs, refs = refs[:n_batch], refs[n_batch:]
    keep_ref, own_ref, *send_refs, sum_ref = refs
    chip = position()[1]
    base, part = keep_ref.shape
    size = own_ref.shape[0]
    act = jnp.concatenate([ref[...] for ref in act_refs], axis=0)
    g = jnp.concatenate([ref[j] for j in range(n_batch) for ref in (g_ref, g2_ref)], axis=0)
    sum_ref[...] = dot(act, g, 0, 0)
    keep_ref[...] = mine_ref[0] + twin_ref[0].astype(f32)
    own_ref[...] = sum_ref[slot(chip * size, size)]
    for m, ref in enumerate(send_refs, 1):
        ref[:base] = (mine_ref[m] + twin_ref[m].astype(f32)).astype(bf16)
        v = sum_ref[slot((chip ^ m) * size, size)].astype(bf16)
        for q in range(v.shape[1] // part):
            ref[base + q * size : base + (q + 1) * size] = v[:, q * part : (q + 1) * part]


def unfold_kernel(own_ref, *refs):
    got_refs, out_ref = refs[:-1], refs[-1]
    size, half = own_ref.shape
    part = got_refs[0].shape[1]
    base = got_refs[0].shape[0] - size * (half // part)
    for q in range(half // part):
        cols = slice(q * part, (q + 1) * part)
        v = own_ref[:, cols]
        for ref in got_refs:
            v = v + ref[base + q * size : base + (q + 1) * size].astype(f32)
        out_ref[:, cols] = v.astype(bf16)


def add_kernel(*refs):
    refs[-1][...] = total(refs[:-1]).astype(refs[-1].dtype)


def stack_kernel(*refs):
    for j, ref in enumerate(refs[:-1]):
        refs[-1][j] = ref[...]


def forward_kernel(x_ref, y_ref, low_ref, high_ref):
    half = low_ref.shape[0]
    low_ref[...] = x_ref[:half]
    high_ref[...] = y_ref[half:]


def place_kernel(masks, firsts, n_old, *refs):
    n = len(masks)
    core, chip, z = position()
    pieces, (up_ref, down_ref, held_ref, sems) = refs[: 2 * n], refs[2 * n + n_old :]
    half = up_ref.shape[1] // 2
    n_batch = up_ref.shape[0] // (4 * held_ref.shape[1])
    size = held_ref.shape[1]
    copies = []
    for i, (m, first) in enumerate(zip(masks, firsts)):
        for j in range(pieces[i].shape[0]):
            k, z_at = chip ^ m, z ^ z_masks(n_batch)[first + j]
            for h, (out_ref, row) in enumerate(((up_ref, k * n_batch + z_at), (down_ref, z_at * 4 + k))):
                at = len(copies)
                for side, col in enumerate((core, 1 - core)):
                    held_ref[at, :, slot(col * half, half)] = pieces[side * n + i][j, h].astype(f32)
                copy = pltpu.make_async_copy(held_ref.at[at], out_ref.at[slot(row * size, size)], sems.at[at])
                copy.start()
                copies.append(copy)
    for copy in copies:
        copy.wait()


def final_kernel(scale, n, *refs):
    pieces, refs = refs[: 1 + (n > 0)], refs[1 + (n > 0) :]
    wq_ref, wk_ref, wv_ref, wo_ref, *out_refs, both_ref, tall_ref, flat_ref, sems = refs
    vector_refs, out_refs = out_refs[:6], out_refs[6:]
    feats, width = wk_ref.shape
    wide = both_ref.shape[0] // 2
    steps = tall_ref.shape[1]
    tall = width // steps
    if n == 0:
        both_ref[...] = pieces[0][...].astype(bf16)
    else:
        core, chip, _ = position()
        for side, col in enumerate((core, 1 - core)):
            part = pieces[side].shape[2]
            for b in range(n):
                both_ref[:, slot(col * n * part + (chip ^ b) * part, part)] = pieces[side][b]
    for k, ref in enumerate(vector_refs):
        base, at = (wide, k) if k < 2 else (2 * wide, k - 2)
        ref[...] = both_ref[base - 16 : base].astype(f32)[8 + at : 9 + at]
    copies = []
    for h, (base, w_ref) in enumerate(((0, wk_ref), (wide, wv_ref))):
        for j in range(steps):
            rows = slice(j * tall, (j + 1) * tall)
            if h == 0:
                v = dot(both_ref[:wide, rows][:feats], w_ref[...], 0, 0) * scale
            else:
                v = dot(w_ref[:, rows], both_ref[wide:][:feats], 0, 0)
            tall_ref[h, j] = v
            copies.append(pltpu.make_async_copy(tall_ref.at[h, j], out_refs[h].at[rows], sems.at[len(copies)]))
            copies[-1].start()
    for h in range(2):
        if h == 0:
            v = dot(both_ref[:wide], wq_ref[...], 1, 0) * scale
        else:
            v = dot(both_ref[wide:], wo_ref[...], 1, 1)
        flat_ref[h] = v[:feats]
        copies.append(pltpu.make_async_copy(flat_ref.at[h], out_refs[2 + h], sems.at[len(copies)]))
        copies[-1].start()
    for copy in copies:
        copy.wait()


def seq_send(v, mask, n):
    return lax.ppermute(v, "seq", [(i, i ^ mask) for i in range(n)])


def batch_send(v, shift, n):
    return lax.ppermute(v, "batch", [(i, (i + shift) % n) for i in range(n)])


def z_masks(n):
    masks = [0]
    while len(masks) < n:
        masks = masks + [m ^ (2 * len(masks) - 1) for m in masks]
    return masks


class Comm:
    def __init__(self, n_seq, n_batch):
        self.n_seq, self.n_batch = n_seq, n_batch
        self.chips = n_seq // 2

    def twin(self, v):
        return seq_send(v, 1, self.n_seq)

    def swap_chip(self, v, mask):
        return seq_send(v, 2 * mask, self.n_seq)

    def to_chips(self, pieces):
        return [seq_send(v, 2 * m, self.n_seq) for m, v in enumerate(pieces, 1)]

    def to_z(self, pieces):
        n = self.n_batch
        order = sorted(range(1, n), key=lambda j: min(j, n - j))
        got = {j: batch_send(pieces[j - 1], j, n) for j in order}
        return [got[j] for j in range(1, n)]

    def next_z(self, v):
        return batch_send(v, 1, self.n_batch)

    def sum_z(self, v):
        mask = 1
        while mask < self.n_batch:
            pairs = [(i, i ^ (2 * mask - 1)) for i in range(self.n_batch)]
            other = lax.ppermute(v, "batch", pairs)
            v = call(add_kernel, shape(v.shape, v.dtype))(v, other)
            mask *= 2
        return v

    def all_z(self, v):
        got = [v]
        while len(got) < self.n_batch:
            pairs = [(i, i ^ (2 * len(got) - 1)) for i in range(self.n_batch)]
            got = got + [lax.ppermute(piece, "batch", pairs) for piece in got]
        return got

    def all_chips(self, v):
        return [v] + self.to_chips([v] * (self.chips - 1))

    def spread(self, v, beside):
        mine, beside = tie(self.all_chips(v), beside)
        mine = call(stack_kernel, shape((self.chips, *v.shape), v.dtype))(*mine)
        return [mine, self.twin(mine)], beside


def tie(first, second):
    out = lax.optimization_barrier((*first, *second))
    return list(out[: len(first)]), list(out[len(first) :])


def add_all(first, rest):
    for v in rest:
        first = first + v.astype(f32)
    return first


def shards(
    n_seq,
    n_batch,
    latents,
    pixels,
    keep_mask,
    gain_attn,
    shift_attn,
    w_query,
    w_key,
    w_value,
    w_out,
    gain_mlp,
    shift_mlp,
    w_up,
    bias_up,
    w_down,
    bias_down,
    cotangent,
):
    images, rows, width = latents.shape
    pix, feats = pixels.shape[1:]
    hidden = w_up.shape[1]
    wide = -(-(feats + 8) // 16) * 16
    lanes = images * rows
    scale = width ** (-0.5)
    comm = Comm(n_seq, n_batch)
    blocks = comm.chips
    every = n_seq * rows
    x = latents.reshape(lanes, width)
    g = cotangent.reshape(lanes, width)
    gain1, shift1, gain2, shift2, b_up, b_down = (
        v.reshape(1, -1) for v in (gain_attn, shift_attn, gain_mlp, shift_mlp, bias_up, bias_down)
    )
    small = (blocks, wide, lanes)

    operands = (x, gain1, shift1, w_query, w_key)
    qk, normed = call(
        functools.partial(query_kernel, scale),
        [shape((wide, lanes), bf16), shape((lanes, width), bf16)],
        ins=[pl.BlockSpec(memory_space=pltpu.HBM)] * 5,
        scratch=[pltpu.VMEM(v.shape, v.dtype) for v in operands]
        + [pltpu.VMEM((wide, lanes), f32), pltpu.SemaphoreType.DMA((8,))],
        limit=60 << 20,
    )(*operands)

    pix_x, pix_t = call(
        pixel_kernel,
        [shape((images, pix, wide), bf16), shape((images, wide, pix), bf16)],
        grid=(images,),
        ins=[one_of((feats, pix)), whole((images, pix))],
        outs=[one_of((pix, wide)), one_of((wide, pix))],
        scratch=[pltpu.VMEM((wide, pix), f32)],
    )(pixels.transpose(0, 2, 1), keep_mask)
    (qk,), g_all = tie([qk], [g])
    g_all.append(comm.next_z(g_all[0]))
    q_sides, (pix_x, g_all[1]) = comm.spread(qk, [pix_x, g_all[1]])
    vo_hi, vo_lo, d_act = call(
        weight_kernel,
        [shape((wide, width), bf16)] * 2 + [shape((lanes, hidden), f32)],
        scratch=[pltpu.VMEM((wide, width), f32)],
    )(w_value, w_out, g, w_down)

    probs, q_all, top, part_mine, part_twin = call(
        functools.partial(attend_kernel, rows),
        [
            shape((images, pix, every), bf16),
            shape((images, wide, every), bf16),
            shape((images, 1, every), f32),
            shape(small, f32),
            shape(small, f32),
        ],
        grid=(images,),
        ins=[one_of((pix, wide)), one_of((wide, pix))] + [whole(small)] * 2,
        outs=[one_of((pix, every)), one_of((wide, every)), one_of((1, every)), whole(small), whole(small)],
        scratch=[pltpu.VMEM((pix, every), f32)],
    )(pix_x, pix_t, *q_sides)
    keep, *send = call(
        merge_kernel, [shape((wide, lanes), f32)] + [shape((wide, lanes), bf16)] * (blocks - 1)
    )(
        part_mine, comm.twin(part_twin)
    )
    g_next = comm.next_z(g_all[-1])
    got, (g_next,) = tie(comm.to_chips(send), [g_next])
    g_all.append(g_next)

    new_latents, d_resid, trio, ctx, back, c_part = call(
        functools.partial(mlp_kernel, feats, blocks - 1),
        [
            shape((lanes, width), bf16),
            shape((lanes, width), f32),
            shape((3, lanes, width), bf16),
            shape((wide, lanes), f32),
            shape((wide, lanes), bf16),
            shape((wide, width), f32),
        ],
    )(keep, *got, x, g, vo_hi, vo_lo, gain2, shift2, w_up, b_up, w_down, b_down, d_act)

    half = width // 2
    part = half // blocks
    quarter, tall, size = width // blocks, width // n_batch, width // blocks // n_batch
    cut = part == lanes and part % 128 == 0 and size % 16 == 0 and blocks == 4 and n_batch == 4
    tall = hidden // n_batch
    if cut:
        up = call(
            functools.partial(up_kernel, blocks),
            [shape((quarter, half), f32)]
            + [shape((blocks * quarter + wide, part), bf16)] * (blocks - 1)
            + [shape((2 * lanes, tall), bf16)] * n_batch,
        )(trio, comm.twin(trio), back)
        up, act = list(up[:blocks]), list(up[blocks:])
        for _ in range(3, n_batch):
            g_all.append(comm.next_z(g_all[-1]))
        up[1:] = comm.to_chips(up[1:])
        act[1:] = comm.to_z(act[1:])
        up, rest = tie(up, [*act, *g_all[3:]])
        act, g_all[3:] = rest[:n_batch], rest[n_batch:]
        sides, up = call(
            functools.partial(part_kernel, blocks), [shape(small, bf16), shape((quarter, half), f32)]
        )(back, *up)
        back_sides = [sides, comm.twin(sides)]
        g_mine, g_twin = call(halves_kernel, [shape((n_batch, lanes, half), bf16)] * 2)(*g_all)
        g_twin = comm.twin(g_twin)
    else:
        back_sides, _ = comm.spread(back, [])
    d_scores, d_ctx_all, dq_mine, dq_twin = call(
        functools.partial(back_kernel, rows),
        [
            shape((images, pix, every), bf16),
            shape((images, wide, every), bf16),
            shape(small, f32),
            shape(small, bf16),
        ],
        grid=(images,),
        ins=[one_of((pix, wide)), one_of((wide, pix)), one_of((pix, every)), one_of((1, every))]
        + [whole(small)] * 2,
        outs=[one_of((pix, every)), one_of((wide, every)), whole(small), whole(small)],
        scratch=[pltpu.VMEM((wide, every), bf16)],
    )(pix_x, pix_t, probs, top, *back_sides)

    pixel_grad = call(
        functools.partial(pixel_grad_kernel, feats), shape((feats, images, pix), f32)
    )(d_scores, probs, q_all, d_ctx_all)

    def place(masks, firsts, pieces, old=()):
        count = 2 * sum(v.shape[0] for v in pieces)
        hbm, vmem = pl.BlockSpec(memory_space=pltpu.HBM), pl.BlockSpec(memory_space=pltpu.VMEM)
        return list(
            pl.pallas_call(
                functools.partial(place_kernel, masks, firsts, len(old)),
                out_shape=[shape((width, width), f32)] * 2,
                in_specs=[vmem] * (2 * len(pieces)) + [hbm] * len(old),
                out_specs=[hbm] * 2,
                scratch_shapes=[pltpu.VMEM((count, size, width), f32), pltpu.SemaphoreType.DMA((count,))],
                input_output_aliases={2 * len(pieces) + i: i for i in range(len(old))},
                compiler_params=pltpu.CompilerParams(vmem_limit_bytes=VMEM_LIMIT),
            )(*pieces, *map(comm.twin, pieces), *old)
        )

    def folded(mine, twin):
        return call(
            functools.partial(fold_kernel, blocks),
            [shape(mine.shape[1:], f32)] + [shape(mine.shape[1:], bf16)] * (blocks - 1),
        )(mine, comm.twin(twin))

    if cut:
        first, down, *rest = call(
            functools.partial(fold_down_kernel, n_batch),
            [shape((wide, lanes), f32), shape((size, half), f32)]
            + [shape((wide + blocks * size, lanes), bf16)] * (blocks - 1),
            scratch=[pltpu.VMEM((tall, half), f32)],
        )(dq_mine, comm.twin(dq_twin), g_mine, g_twin, *act)
        up_keep, *up_send = call(
            split_kernel, [shape((size, half), f32)] + [shape((size, half), bf16)] * (n_batch - 1)
        )(up)
        up = [up_keep] + comm.to_z(up_send)
        dq = [first] + comm.to_chips(rest)
    else:
        first, *rest = folded(dq_mine, dq_twin)
        dq = [first] + comm.to_chips(rest)
    latent_grad, *both = call(
        functools.partial(latent_kernel, scale, blocks - 1, cut),
        [shape((lanes, width), f32)]
        + [shape((blocks, 2 * wide, part), f32), shape((blocks, 2 * wide, part), bf16)] * cut
        + [shape((2 * wide, width), f32)] * (not cut),
        scratch=[pltpu.VMEM((2 * wide, width), f32)] * cut + [pltpu.VMEM((wide, lanes), f32)],
    )(*dq, ctx, x, normed, gain1, w_key, w_query, d_resid, c_part)
    if cut:
        both, up = tie(both, up)
        first, *rest = folded(*both)
        up = call(add_kernel, shape((size, half), bf16))(*up)
        down = call(unfold_kernel, shape((size, half), bf16))(down, *dq[1:])
        own = call(stack_kernel, shape((2, size, half), bf16))(up, down)
        sums, (pixel_grad, *own) = tie([first] + comm.to_chips(rest), [pixel_grad, *comm.all_z(own)])
        own = call(stack_kernel, shape((n_batch, 2, size, half), bf16))(*own)
        sums = call(add_kernel, shape((2 * wide, part), bf16))(*sums)
        own = [own] + [comm.swap_chip(own, m) for m in (1, 2)]
        (sums,), own = tie([comm.sum_z(sums)], own)
        low, high = call(forward_kernel, [shape((n_batch // 2, 2, size, half), bf16)] * 2)(*own[1:])
        far = [comm.swap_chip(low, 2), comm.swap_chip(high, 1)]
        grads = place((0, 1, 2), (0, 0, 0), own)
        pieces, (*far, grads[0], grads[1]) = tie(comm.all_chips(sums), [*far, *grads])
        pieces = call(stack_kernel, shape((blocks, 2 * wide, part), bf16))(*pieces)
        grad_up, grad_down = place((3, 3), (0, n_batch // 2), far, grads)
        pieces = [pieces, comm.twin(pieces)]
    else:
        pieces = [lax.psum(both[0], ("batch", "seq"))]
    steps = 4
    hbm, vmem = pl.BlockSpec(memory_space=pltpu.HBM), pl.BlockSpec(memory_space=pltpu.VMEM)
    *vectors, grad_query, grad_out, grad_key, grad_value = pl.pallas_call(
        functools.partial(final_kernel, scale, blocks if cut else 0),
        out_shape=[shape((1, width), f32)] * 6 + [shape((width, width), f32)] * 2 + [shape((feats, width), f32)] * 2,
        in_specs=[vmem] * (len(pieces) + 4),
        out_specs=[vmem] * 6 + [hbm] * 4,
        scratch_shapes=[
            pltpu.VMEM((2 * wide, width), bf16),
            pltpu.VMEM((2, steps, width // steps, width), f32),
            pltpu.VMEM((2, feats, width), f32),
            pltpu.SemaphoreType.DMA((2 * steps + 2,)),
        ],
        compiler_params=pltpu.CompilerParams(vmem_limit_bytes=24 << 20),
    )(*pieces, w_query, w_key, w_value, w_out)
    vectors = [v.reshape(width) for v in vectors]
    if not cut:
        grad_up = lax.psum(dot(trio[0], trio[2], 0, 0), ("batch", "seq"))
        grad_down = lax.psum(dot(trio[1], g, 0, 0), ("batch", "seq"))
    dims = (images, rows, width)
    return (
        new_latents.reshape(dims),
        latent_grad.reshape(dims),
        pixel_grad.transpose(1, 2, 0),
        vectors[0],
        vectors[1],
        grad_query,
        grad_key,
        grad_value,
        grad_out,
        vectors[2],
        vectors[3],
        grad_up,
        vectors[4],
        grad_down,
        vectors[5],
    )


def solution(mesh):
    split = P("batch", "seq", None)
    placed = (split, split, P("batch", "seq")) + (P(),) * 12 + (split,)
    return jax.shard_map(
        functools.partial(shards, mesh.shape["seq"], mesh.shape["batch"]),
        mesh=mesh,
        in_specs=placed,
        out_specs=(split, split, split) + (P(),) * 12,
        check_vma=False,
    )
```

```python
import functools

import jax
import jax.numpy as jnp
from jax import lax
from jax.experimental import pallas as pl
from jax.experimental.pallas import tpu as pltpu
from jax.sharding import PartitionSpec as P

f32 = jnp.float32
bf16 = jnp.bfloat16
EPS = 1e-05
DROP = -1e30
ONE, TOP, MASK = 0, 3, 6
VMEM_LIMIT = 20 << 20


def dot(a, b, ca, cb):
    return lax.dot_general(a, b, (((ca,), (cb,)), ((), ())), preferred_element_type=f32)


def shape(dims, dtype):
    return jax.ShapeDtypeStruct(dims, dtype)


def call(body, out, grid=(), ins=None, outs=None, scratch=(), limit=VMEM_LIMIT):
    kwargs = {}
    if grid:
        kwargs = dict(grid=grid, in_specs=ins, out_specs=outs)
    elif ins:
        kwargs = dict(in_specs=ins)
    return pl.pallas_call(
        body,
        out_shape=out,
        scratch_shapes=list(scratch),
        compiler_params=pltpu.CompilerParams(vmem_limit_bytes=limit),
        **kwargs,
    )


def whole(dims):
    return pl.BlockSpec(dims, lambda *_: (0,) * len(dims))


def one_of(dims):
    return pl.BlockSpec((1,) + dims, lambda i, *_: (i,) + (0,) * len(dims))


def split3(v):
    hi = v.astype(bf16).astype(f32)
    mid = (v - hi).astype(bf16).astype(f32)
    return hi, mid, v - hi - mid


def position():
    s = lax.axis_index("seq")
    return lax.rem(s, 2), lax.div(s, 2), lax.axis_index("batch")


def slot(start, size):
    return pl.ds(pl.multiple_of(start, size), size)


def tail_rows(rows, lanes):
    at = lax.broadcasted_iota(jnp.int32, (8, lanes), 0)
    tile = jnp.zeros((8, lanes), f32)
    for k, v in rows.items():
        tile = jnp.where(at == k, v, tile)
    return tile


def norm_parts(v):
    mean = jnp.mean(v, axis=-1, keepdims=True)
    centered = v - mean
    spread = jnp.mean(centered * centered, axis=-1, keepdims=True)
    scale = lax.rsqrt(spread + EPS)
    return centered * scale, scale


def norm_back(d_out, hat, scale, gain):
    d_hat = d_out * gain
    mean = jnp.mean(d_hat, axis=-1, keepdims=True)
    along = jnp.mean(d_hat * hat, axis=-1, keepdims=True)
    return scale * (d_hat - mean - hat * along)


def gelu_and_slope(v):
    cdf = 0.5 * (1.0 + lax.erf(v * (0.5**0.5)))
    pdf = jnp.exp(-0.5 * v * v) * (1.0 / (2.0 * 3.141592653589793) ** 0.5)
    return v * cdf, cdf + v * pdf


def chunks(n, size=256):
    return [(a, min(size, n - a)) for a in range(0, n, size)]


def query_kernel(scale, *refs):
    sources, (qk_ref, normed_ref), refs = refs[:5], refs[5:7], refs[7:]
    held, (pad_ref, sems) = refs[:5], refs[5:]
    x_ref, gain_ref, shift_ref, wq_ref, wk_ref = held
    steps = sems.shape[0] - 4
    tall = wq_ref.shape[0] // steps
    copies = [pltpu.make_async_copy(sources[k], held[k], sems.at[k]) for k in range(3)]
    for k in range(steps):
        rows = slice(k * tall, (k + 1) * tall)
        copies.append(pltpu.make_async_copy(sources[3].at[rows], wq_ref.at[rows], sems.at[3 + k]))
    copies.append(pltpu.make_async_copy(sources[4], wk_ref, sems.at[3 + steps]))
    for copy in copies:
        copy.start()
    feats = wk_ref.shape[0]
    wide, lanes = qk_ref.shape
    for copy in copies[:3]:
        copy.wait()
    hat, _ = norm_parts(x_ref[...].astype(f32))
    normed = (hat * gain_ref[...] + shift_ref[...]).astype(bf16)
    normed_ref[...] = normed
    pad_ref[wide - 16 :] = jnp.zeros((16, lanes), f32)
    query = jnp.zeros((lanes, wq_ref.shape[1]), f32)
    for k in range(steps):
        rows = slice(k * tall, (k + 1) * tall)
        copies[3 + k].wait()
        query = query + dot(normed[:, rows], wq_ref[rows], 1, 0)
    copies[3 + steps].wait()
    pad_ref[:feats] = dot(wk_ref[...], (query * scale).astype(bf16), 1, 1)
    pad_ref[wide - 8 :] = tail_rows({MASK: 1.0}, lanes)
    qk_ref[...] = pad_ref[...].astype(bf16)


def pixel_kernel(pix_ref, keep_ref, x_ref, t_ref, pad_ref):
    feats, n = pix_ref.shape[1:]
    wide = t_ref.shape[1]
    keep = keep_ref[pl.ds(pl.program_id(0), 1), :]
    bias = jnp.where(keep > 0, 0.0, DROP).astype(f32)
    pad_ref[wide - 16 :] = jnp.zeros((16, n), f32)
    pad_ref[:feats] = pix_ref[0].astype(f32)
    pad_ref[wide - 8 :] = tail_rows({ONE: 1.0, ONE + 1: 1.0, ONE + 2: 1.0, MASK: bias}, n)
    t_ref[0] = pad_ref[...].astype(bf16)
    x_ref[0] = pad_ref[...].T.astype(bf16)


def weight_kernel(wv_ref, wo_ref, g_ref, wd_ref, hi_ref, lo_ref, dact_ref, pad_ref):
    feats = wv_ref.shape[0]
    pad_ref[...] = jnp.zeros(pad_ref.shape, f32)
    pad_ref[:feats] = dot(wv_ref[...], wo_ref[...], 1, 0)
    v = pad_ref[...]
    hi = v.astype(bf16)
    hi_ref[...] = hi
    lo_ref[...] = (v - hi.astype(f32)).astype(bf16)
    dact_ref[...] = dot(g_ref[...], wd_ref[...], 1, 1)


def lay_lanes(i, rows, refs, out_ref):
    for k in range(2):

        @pl.when(i == k)
        def _():
            parts = [ref[b, :, k * rows : (k + 1) * rows] for ref in refs for b in range(ref.shape[0])]
            out_ref[...] = jnp.concatenate(parts, axis=1)


def unlay_lanes(i, rows, v, mine_ref, twin_ref):
    blocks = mine_ref.shape[0]
    for k in range(2):

        @pl.when(i == k)
        def _():
            for b in range(2 * blocks):
                ref = (mine_ref, twin_ref)[b // blocks]
                piece = v[:, b * rows : (b + 1) * rows].astype(ref.dtype)
                ref[b % blocks, :, k * rows : (k + 1) * rows] = piece


def attend_kernel(rows, x_ref, t_ref, *refs):
    *sides, p_ref, q_ref, top_ref, pm_ref, pt_ref, s_ref = refs
    i = pl.program_id(0)
    n = x_ref.shape[1]
    wide, lanes = q_ref.shape[1:]
    lay_lanes(i, rows, sides, q_ref.at[0])
    q = q_ref[0]
    top = jnp.full((1, lanes), -jnp.inf, f32)
    for a, size in chunks(n):
        s = dot(x_ref[0, a : a + size], q, 1, 0)
        s_ref[a : a + size] = s
        top = jnp.maximum(top, jnp.max(s, axis=0, keepdims=True))
    total = jnp.zeros((wide, lanes), f32)
    for a, size in chunks(n):
        p = jnp.exp(s_ref[a : a + size] - top).astype(bf16)
        p_ref[0, a : a + size] = p
        total = total + dot(t_ref[0, :, a : a + size], p, 1, 0)
    top_ref[0] = top
    tile = total[wide - 8 :]
    at = lax.broadcasted_iota(jnp.int32, tile.shape, 0)
    sums = jnp.sum(jnp.where(at == ONE, tile, 0.0), axis=0, keepdims=True)
    stats = {ONE + j: piece for j, piece in enumerate(split3(sums))}
    stats.update({TOP + j: piece for j, piece in enumerate(split3(top))})
    tile = tail_rows(stats, lanes)
    unlay_lanes(i, rows, jnp.concatenate([total[: wide - 8], tile], axis=0), pm_ref, pt_ref)


def merge_kernel(a_ref, b_ref, keep_ref, *send_refs):
    blocks, wide, lanes = a_ref.shape
    base = wide - 8
    at = lax.broadcasted_iota(jnp.int32, (8, lanes), 0)
    for k, ref in enumerate((keep_ref, *send_refs)):
        sides = [a_ref[k], b_ref[k].astype(f32)]
        (ta, tb), (sa, sb) = (
            [jnp.sum(jnp.where((at >= r) & (at < r + 3), v[base:], 0.0), axis=0, keepdims=True) for v in sides]
            for r in (TOP, ONE)
        )
        top = jnp.maximum(ta, tb)
        wa, wb = jnp.exp(ta - top), jnp.exp(tb - top)
        v = sides[0][:base] * wa + sides[1][:base] * wb
        rows = {ONE + j: piece for j, piece in enumerate(split3(sa * wa + sb * wb))}
        rows.update({TOP + j: piece for j, piece in enumerate(split3(top))})
        ref[...] = jnp.concatenate([v, tail_rows(rows, lanes)], axis=0).astype(ref.dtype)


def mlp_forward_kernel(feats, n_got, keep_ref, *refs):
    got_refs, refs = refs[:n_got], refs[n_got:]
    x_ref, hi_ref, lo_ref, gain_ref, shift_ref, wu_ref, bu_ref, dact_ref, *outs = refs
    trio_ref, ctx_ref, lse_ref, resid_ref = outs
    wide, lanes = keep_ref.shape
    base = wide - 8
    parts = [keep_ref[...]] + [ref[...].astype(f32) for ref in got_refs]
    at = lax.broadcasted_iota(jnp.int32, (8, lanes), 0)
    tops, sums = (
        [jnp.sum(jnp.where((at >= k) & (at < k + 3), v[base:], 0.0), axis=0, keepdims=True) for v in parts]
        for k in (TOP, ONE)
    )
    peak = functools.reduce(jnp.maximum, tops)
    total = jnp.zeros((1, lanes), f32)
    ctx = jnp.zeros((wide, lanes), f32)
    for v, top, part in zip(parts, tops, sums):
        share = jnp.exp(top - peak)
        total = total + part * share
        ctx = ctx + v * share
    ctx = ctx / total
    lse_ref[...] = peak + jnp.log(total)
    row = lax.broadcasted_iota(jnp.int32, (wide, lanes), 0)
    ctx = jnp.where(row < feats, ctx, 0.0)
    ctx_ref[...] = ctx
    ctx_b = ctx.astype(bf16)
    resid = x_ref[...].astype(f32) + dot(ctx_b, hi_ref[...], 0, 0) + dot(ctx_b, lo_ref[...], 0, 0)
    resid_ref[...] = resid
    hat, _ = norm_parts(resid)
    normed = (hat * gain_ref[...] + shift_ref[...]).astype(bf16)
    trio_ref[0] = normed
    pre = dot(normed, wu_ref[...], 1, 0) + bu_ref[...]
    act_f, slope = gelu_and_slope(pre)
    trio_ref[1] = act_f.astype(bf16)
    trio_ref[2] = (dact_ref[...] * slope).astype(bf16)


def mlp_backward_kernel(trio_ref, ctx_ref, lse_ref, resid_ref, g_ref, hi_ref, lo_ref, gain_ref, wu_ref, *outs):
    dres_ref, back_ref, vector_ref = outs
    wide, lanes = ctx_ref.shape
    hat, scale = norm_parts(resid_ref[...])
    d_pre = trio_ref[2]
    d_normed = dot(d_pre, wu_ref[...], 1, 1)
    g = g_ref[...].astype(f32)
    d_resid = g + norm_back(d_normed, hat, scale, gain_ref[...])
    dres_ref[...] = d_resid
    d_resid_b = d_resid.astype(bf16)
    d_ctx = (dot(hi_ref[...], d_resid_b, 1, 1) + dot(lo_ref[...], d_resid_b, 1, 1)).astype(bf16)
    delta = jnp.sum(ctx_ref[...] * d_ctx.astype(f32), axis=0, keepdims=True)
    rows = {ONE + k: -v for k, v in enumerate(split3(delta))}
    rows.update({TOP + k: v for k, v in enumerate(split3(lse_ref[...]))})
    back_ref[...] = jnp.concatenate([d_ctx[: wide - 8], tail_rows(rows, lanes).astype(bf16)], axis=0)
    vectors = {
        0: jnp.sum(d_normed * hat, axis=0, keepdims=True),
        1: jnp.sum(d_normed, axis=0, keepdims=True),
        2: jnp.sum(d_pre.astype(f32), axis=0, keepdims=True),
        3: jnp.sum(g, axis=0, keepdims=True),
    }
    vector_ref[...] = tail_rows(vectors, g.shape[1])


def mlp_rest_kernel(trio_ref, ctx_ref, resid_ref, dres_ref, vector_ref, wd_ref, bd_ref, new_ref, csum_ref):
    base = csum_ref.shape[0] - 8
    new_ref[...] = (resid_ref[...] + dot(trio_ref[1], wd_ref[...], 1, 0) + bd_ref[...]).astype(bf16)
    csum_ref[:base] = dot(ctx_ref[...].astype(bf16), dres_ref[...].astype(bf16), 1, 0)[:base]
    csum_ref[base:] = vector_ref[...]


def back_kernel(rows, x_ref, t_ref, p_ref, top_ref, *refs):
    sides, (ds_ref, dc_ref, dm_ref, dt_ref, b_ref) = refs[:2], refs[2:]
    i = pl.program_id(0)
    pix = x_ref.shape[1]
    wide, lanes = b_ref.shape
    lay_lanes(i, rows, sides, b_ref)
    b = b_ref[...]
    tail = b[wide - 16 :].astype(f32)[8:]
    at = lax.broadcasted_iota(jnp.int32, tail.shape, 0)
    lse = jnp.sum(jnp.where((at >= TOP) & (at < TOP + 3), tail, 0.0), axis=0, keepdims=True)
    ratio = jnp.exp(top_ref[0] - lse)
    dc_ref[0] = (b.astype(f32) * ratio).astype(bf16)
    sums = jnp.zeros((wide, lanes), f32)
    for a, size in chunks(pix):
        d = dot(x_ref[0, a : a + size], b, 1, 0)
        ds = (p_ref[0, a : a + size].astype(f32) * (d * ratio)).astype(bf16)
        ds_ref[0, a : a + size] = ds
        sums = sums + dot(t_ref[0, :, a : a + size], ds, 1, 0)
    unlay_lanes(i, rows, sums, dm_ref, dt_ref)


def pixel_grad_kernel(feats, ds_ref, p_ref, q_ref, dc_ref, out_ref):
    for i in range(ds_ref.shape[0]):
        for a, size in chunks(ds_ref.shape[1]):
            rows = slice(a, a + size)
            v = dot(q_ref[i], ds_ref[i, rows], 1, 1) + dot(dc_ref[i], p_ref[i, rows], 1, 1)
            out_ref[:, i, rows] = v[:feats]


def latent_kernel(scale, n_got, cut, *refs):
    dq_refs, refs = refs[: n_got + 1], refs[n_got + 1 :]
    ctx_ref, x_ref, normed_ref, gain_ref, wk_ref, wq_ref, dres_ref, c_ref, *outs = refs
    lat_ref, *outs, dq_ref = outs
    feats = wk_ref.shape[0]
    wide, lanes = dq_ref.shape
    base = wide - 8
    dq_ref[...] = dq_refs[0][...]
    for ref in dq_refs[1:]:
        dq_ref[...] += ref[:wide].astype(f32)
    d = dq_ref[...] - dq_ref[pl.ds(base + ONE, 1)] * ctx_ref[...]
    row = lax.broadcasted_iota(jnp.int32, (wide, lanes), 0)
    d = jnp.where(row < feats, d, 0.0).astype(bf16)
    d_query = dot(d[:feats], wk_ref[...], 0, 0).astype(bf16)
    d_normed = dot(d_query, wq_ref[...], 1, 1) * scale
    hat, spread = norm_parts(x_ref[...].astype(f32))
    vectors = {
        0: jnp.sum(d_normed * hat, axis=0, keepdims=True),
        1: jnp.sum(d_normed, axis=0, keepdims=True),
    }
    both_ref = outs[-1]
    both_ref[:base] = dot(d, normed_ref[...], 1, 0)[:base]
    both_ref[base:wide] = tail_rows(vectors, both_ref.shape[1])
    both_ref[wide:] = c_ref[...]
    if cut:
        mine_ref, twin_ref = outs[:2]
        core, chip, _ = position()
        n, _, part = mine_ref.shape
        for b in range(n):
            at = (chip ^ b) * part
            mine_ref[b] = both_ref[:, slot(core * n * part + at, part)]
            twin_ref[b] = both_ref[:, slot((1 - core) * n * part + at, part)].astype(bf16)
    lat_ref[...] = dres_ref[...] + norm_back(d_normed, hat, spread, gain_ref[...])


def halves_kernel(*refs):
    mine_ref, other_ref = refs[-2:]
    core, half = position()[0], mine_ref.shape[2]
    for j, ref in enumerate(refs[:-2]):
        mine_ref[j] = ref[:, slot(core * half, half)]
        other_ref[j] = ref[:, slot((1 - core) * half, half)]


def up_kernel(n, trio_ref, twin_ref, back_ref, *refs):
    core, chip, z = position()
    up_refs, act_refs = refs[:n], refs[n:]
    tall, half = up_refs[0].shape
    part = up_refs[1].shape[1]
    cols = slot(core * half, half)
    slab = act_refs[0].shape[1]
    for j, ref in enumerate(act_refs):
        rows = slot(lax.rem(z + j, len(act_refs)) * slab, slab)
        ref[...] = jnp.concatenate([trio_ref[1, :, rows], twin_ref[1, :, rows]], axis=0)
    d_pre = jnp.concatenate([trio_ref[2, :, cols], twin_ref[2, :, cols]], axis=0)
    for m, ref in enumerate(up_refs):
        rows = slot((chip ^ m) * tall, tall)
        normed = jnp.concatenate([trio_ref[0, :, rows], twin_ref[0, :, rows]], axis=0)
        v = dot(normed, d_pre, 0, 0)
        if m == 0:
            ref[...] = v
        else:
            for q in range(half // part):
                ref[q * tall : (q + 1) * tall] = v[:, q * part : (q + 1) * part].astype(bf16)
            ref[half // part * tall :] = back_ref[...]


def part_kernel(n, *refs):
    back_ref, up_ref, *got_refs = refs[: n + 1]
    sides_ref, sum_ref = refs[n + 1 :]
    tall, half = up_ref.shape
    wide, part = back_ref.shape
    base = got_refs[0].shape[0] - wide
    sides_ref[0] = back_ref[...]
    for m, ref in enumerate(got_refs, 1):
        sides_ref[m] = ref[base:]
    for q in range(half // part):
        cols = slice(q * part, (q + 1) * part)
        v = up_ref[:, cols]
        for ref in got_refs:
            v = v + ref[q * tall : (q + 1) * tall].astype(f32)
        sum_ref[:, cols] = v


def total(refs):
    v = refs[0][...].astype(f32)
    for ref in refs[1:]:
        v = v + ref[...].astype(f32)
    return v


def split_kernel(sum_ref, *out_refs):
    z = position()[2]
    size = out_refs[0].shape[0]
    for j, ref in enumerate(out_refs):
        ref[...] = sum_ref[slot(lax.rem(z + j, len(out_refs)) * size, size)].astype(ref.dtype)


def fold_kernel(n, mine_ref, twin_ref, keep_ref, *out_refs):
    keep_ref[...] = mine_ref[0] + twin_ref[0].astype(f32)
    for m, ref in enumerate(out_refs, 1):
        ref[...] = (mine_ref[m] + twin_ref[m].astype(f32)).astype(bf16)


def fold_down_kernel(n_batch, mine_ref, twin_ref, g_ref, g2_ref, *refs):
    act_refs, refs = refs[:n_batch], refs[n_batch:]
    keep_ref, own_ref, *send_refs, sum_ref = refs
    chip = position()[1]
    base, part = keep_ref.shape
    size = own_ref.shape[0]
    act = jnp.concatenate([ref[...] for ref in act_refs], axis=0)
    g = jnp.concatenate([ref[j] for j in range(n_batch) for ref in (g_ref, g2_ref)], axis=0)
    sum_ref[...] = dot(act, g, 0, 0)
    keep_ref[...] = mine_ref[0] + twin_ref[0].astype(f32)
    own_ref[...] = sum_ref[slot(chip * size, size)]
    for m, ref in enumerate(send_refs, 1):
        ref[:base] = (mine_ref[m] + twin_ref[m].astype(f32)).astype(bf16)
        v = sum_ref[slot((chip ^ m) * size, size)].astype(bf16)
        for q in range(v.shape[1] // part):
            ref[base + q * size : base + (q + 1) * size] = v[:, q * part : (q + 1) * part]


def unfold_kernel(own_ref, *refs):
    got_refs, out_ref = refs[:-1], refs[-1]
    size, half = own_ref.shape
    part = got_refs[0].shape[1]
    base = got_refs[0].shape[0] - size * (half // part)
    for q in range(half // part):
        cols = slice(q * part, (q + 1) * part)
        v = own_ref[:, cols]
        for ref in got_refs:
            v = v + ref[base + q * size : base + (q + 1) * size].astype(f32)
        out_ref[:, cols] = v.astype(bf16)


def add_kernel(*refs):
    refs[-1][...] = total(refs[:-1]).astype(refs[-1].dtype)


def stack_kernel(*refs):
    for j, ref in enumerate(refs[:-1]):
        refs[-1][j] = ref[...]


def forward_kernel(x_ref, y_ref, low_ref, high_ref):
    half = low_ref.shape[0]
    low_ref[...] = x_ref[:half]
    high_ref[...] = y_ref[half:]


def place_kernel(masks, firsts, n_old, *refs):
    n = len(masks)
    core, chip, z = position()
    pieces, (up_ref, down_ref, held_ref, sems) = refs[: 2 * n], refs[2 * n + n_old :]
    half = up_ref.shape[1] // 2
    n_batch = up_ref.shape[0] // (4 * held_ref.shape[1])
    size = held_ref.shape[1]
    copies = []
    for i, (m, first) in enumerate(zip(masks, firsts)):
        for j in range(pieces[i].shape[0]):
            k, z_at = chip ^ m, z ^ z_masks(n_batch)[first + j]
            for h, (out_ref, row) in enumerate(((up_ref, k * n_batch + z_at), (down_ref, z_at * 4 + k))):
                at = len(copies)
                for side, col in enumerate((core, 1 - core)):
                    held_ref[at, :, slot(col * half, half)] = pieces[side * n + i][j, h].astype(f32)
                copy = pltpu.make_async_copy(held_ref.at[at], out_ref.at[slot(row * size, size)], sems.at[at])
                copy.start()
                copies.append(copy)
    for copy in copies:
        copy.wait()


def final_kernel(scale, n, *refs):
    pieces, refs = refs[: 1 + (n > 0)], refs[1 + (n > 0) :]
    wq_ref, wk_ref, wv_ref, wo_ref, *out_refs, both_ref, tall_ref, flat_ref, sems = refs
    vector_refs, out_refs = out_refs[:6], out_refs[6:]
    feats, width = wk_ref.shape
    wide = both_ref.shape[0] // 2
    steps = tall_ref.shape[1]
    tall = width // steps
    if n == 0:
        both_ref[...] = pieces[0][...].astype(bf16)
    else:
        core, chip, _ = position()
        for side, col in enumerate((core, 1 - core)):
            part = pieces[side].shape[2]
            for b in range(n):
                both_ref[:, slot(col * n * part + (chip ^ b) * part, part)] = pieces[side][b]
    for k, ref in enumerate(vector_refs):
        base, at = (wide, k) if k < 2 else (2 * wide, k - 2)
        ref[...] = both_ref[base - 16 : base].astype(f32)[8 + at : 9 + at]
    copies = []
    for h, (base, w_ref) in enumerate(((0, wk_ref), (wide, wv_ref))):
        for j in range(steps):
            rows = slice(j * tall, (j + 1) * tall)
            if h == 0:
                v = dot(both_ref[:wide, rows][:feats], w_ref[...], 0, 0) * scale
            else:
                v = dot(w_ref[:, rows], both_ref[wide:][:feats], 0, 0)
            tall_ref[h, j] = v
            copies.append(pltpu.make_async_copy(tall_ref.at[h, j], out_refs[h].at[rows], sems.at[len(copies)]))
            copies[-1].start()
    for h in range(2):
        if h == 0:
            v = dot(both_ref[:wide], wq_ref[...], 1, 0) * scale
        else:
            v = dot(both_ref[wide:], wo_ref[...], 1, 1)
        flat_ref[h] = v[:feats]
        copies.append(pltpu.make_async_copy(flat_ref.at[h], out_refs[2 + h], sems.at[len(copies)]))
        copies[-1].start()
    for copy in copies:
        copy.wait()


def seq_send(v, mask, n):
    return lax.ppermute(v, "seq", [(i, i ^ mask) for i in range(n)])


def batch_send(v, shift, n):
    return lax.ppermute(v, "batch", [(i, (i + shift) % n) for i in range(n)])


def z_masks(n):
    masks = [0]
    while len(masks) < n:
        masks = masks + [m ^ (2 * len(masks) - 1) for m in masks]
    return masks


class Comm:
    def __init__(self, n_seq, n_batch):
        self.n_seq, self.n_batch = n_seq, n_batch
        self.chips = n_seq // 2

    def twin(self, v):
        return seq_send(v, 1, self.n_seq)

    def swap_chip(self, v, mask):
        return seq_send(v, 2 * mask, self.n_seq)

    def to_chips(self, pieces):
        return [seq_send(v, 2 * m, self.n_seq) for m, v in enumerate(pieces, 1)]

    def to_z(self, pieces):
        n = self.n_batch
        order = sorted(range(1, n), key=lambda j: min(j, n - j))
        got = {j: batch_send(pieces[j - 1], j, n) for j in order}
        return [got[j] for j in range(1, n)]

    def next_z(self, v):
        return batch_send(v, 1, self.n_batch)

    def sum_z(self, v):
        mask = 1
        while mask < self.n_batch:
            pairs = [(i, i ^ (2 * mask - 1)) for i in range(self.n_batch)]
            other = lax.ppermute(v, "batch", pairs)
            v = call(add_kernel, shape(v.shape, v.dtype))(v, other)
            mask *= 2
        return v

    def all_z(self, v):
        got = [v]
        while len(got) < self.n_batch:
            pairs = [(i, i ^ (2 * len(got) - 1)) for i in range(self.n_batch)]
            got = got + [lax.ppermute(piece, "batch", pairs) for piece in got]
        return got

    def all_chips(self, v):
        return [v] + self.to_chips([v] * (self.chips - 1))

    def spread(self, v, beside):
        mine, beside = tie(self.all_chips(v), beside)
        mine = call(stack_kernel, shape((self.chips, *v.shape), v.dtype))(*mine)
        return [mine, self.twin(mine)], beside


def tie(first, second):
    out = lax.optimization_barrier((*first, *second))
    return list(out[: len(first)]), list(out[len(first) :])


def add_all(first, rest):
    for v in rest:
        first = first + v.astype(f32)
    return first


def shards(
    n_seq,
    n_batch,
    latents,
    pixels,
    keep_mask,
    gain_attn,
    shift_attn,
    w_query,
    w_key,
    w_value,
    w_out,
    gain_mlp,
    shift_mlp,
    w_up,
    bias_up,
    w_down,
    bias_down,
    cotangent,
):
    images, rows, width = latents.shape
    pix, feats = pixels.shape[1:]
    hidden = w_up.shape[1]
    wide = -(-(feats + 8) // 16) * 16
    lanes = images * rows
    scale = width ** (-0.5)
    comm = Comm(n_seq, n_batch)
    blocks = comm.chips
    every = n_seq * rows
    x = latents.reshape(lanes, width)
    g = cotangent.reshape(lanes, width)
    gain1, shift1, gain2, shift2, b_up, b_down = (
        v.reshape(1, -1) for v in (gain_attn, shift_attn, gain_mlp, shift_mlp, bias_up, bias_down)
    )
    small = (blocks, wide, lanes)

    operands = (x, gain1, shift1, w_query, w_key)
    qk, normed = call(
        functools.partial(query_kernel, scale),
        [shape((wide, lanes), bf16), shape((lanes, width), bf16)],
        ins=[pl.BlockSpec(memory_space=pltpu.HBM)] * 5,
        scratch=[pltpu.VMEM(v.shape, v.dtype) for v in operands]
        + [pltpu.VMEM((wide, lanes), f32), pltpu.SemaphoreType.DMA((8,))],
        limit=60 << 20,
    )(*operands)

    pix_x, pix_t = call(
        pixel_kernel,
        [shape((images, pix, wide), bf16), shape((images, wide, pix), bf16)],
        grid=(images,),
        ins=[one_of((feats, pix)), whole((images, pix))],
        outs=[one_of((pix, wide)), one_of((wide, pix))],
        scratch=[pltpu.VMEM((wide, pix), f32)],
    )(pixels.transpose(0, 2, 1), keep_mask)
    (qk,), g_all = tie([qk], [g])
    g_all.append(comm.next_z(g_all[0]))
    q_sides, (pix_x, g_all[1]) = comm.spread(qk, [pix_x, g_all[1]])
    vo_hi, vo_lo, d_act = call(
        weight_kernel,
        [shape((wide, width), bf16)] * 2 + [shape((lanes, hidden), f32)],
        scratch=[pltpu.VMEM((wide, width), f32)],
    )(w_value, w_out, g, w_down)

    probs, q_all, top, part_mine, part_twin = call(
        functools.partial(attend_kernel, rows),
        [
            shape((images, pix, every), bf16),
            shape((images, wide, every), bf16),
            shape((images, 1, every), f32),
            shape(small, f32),
            shape(small, bf16),
        ],
        grid=(images,),
        ins=[one_of((pix, wide)), one_of((wide, pix))] + [whole(small)] * 2,
        outs=[one_of((pix, every)), one_of((wide, every)), one_of((1, every)), whole(small), whole(small)],
        scratch=[pltpu.VMEM((pix, every), f32)],
    )(pix_x, pix_t, *q_sides)
    keep, *send = call(
        merge_kernel, [shape((wide, lanes), f32)] + [shape((wide, lanes), bf16)] * (blocks - 1)
    )(
        part_mine, comm.twin(part_twin)
    )
    g_next = comm.next_z(g_all[-1])
    got = comm.to_chips(send)

    trio, ctx, lse, resid = call(
        functools.partial(mlp_forward_kernel, feats, blocks - 1),
        [
            shape((3, lanes, width), bf16),
            shape((wide, lanes), f32),
            shape((1, lanes), f32),
            shape((lanes, width), f32),
        ],
    )(keep, *got, x, vo_hi, vo_lo, gain2, shift2, w_up, b_up, d_act)
    (trio_sent,), (g_next,) = tie([trio], [g_next])
    g_all.append(g_next)
    d_resid, back, vector_rows = call(
        mlp_backward_kernel,
        [shape((lanes, width), f32), shape((wide, lanes), bf16), shape((8, width), f32)],
    )(trio, ctx, lse, resid, g, vo_hi, vo_lo, gain2, w_up)
    new_latents, c_part = call(mlp_rest_kernel, [shape((lanes, width), bf16), shape((wide, width), f32)])(
        trio, ctx, resid, d_resid, vector_rows, w_down, b_down
    )

    half = width // 2
    part = half // blocks
    quarter, tall, size = width // blocks, width // n_batch, width // blocks // n_batch
    cut = part == lanes and part % 128 == 0 and size % 16 == 0 and blocks == 4 and n_batch == 4
    tall = hidden // n_batch
    if cut:
        up = call(
            functools.partial(up_kernel, blocks),
            [shape((quarter, half), f32)]
            + [shape((blocks * quarter + wide, part), bf16)] * (blocks - 1)
            + [shape((2 * lanes, tall), bf16)] * n_batch,
        )(trio, comm.twin(trio_sent), back)
        up, act = list(up[:blocks]), list(up[blocks:])
        for _ in range(3, n_batch):
            g_all.append(comm.next_z(g_all[-1]))
        up[1:] = comm.to_chips(up[1:])
        act[1:] = comm.to_z(act[1:])
        up, (new_latents, c_part, *rest) = tie(up, [new_latents, c_part, *act, *g_all[3:]])
        act, g_all[3:] = rest[:n_batch], rest[n_batch:]
        sides, up = call(
            functools.partial(part_kernel, blocks), [shape(small, bf16), shape((quarter, half), f32)]
        )(back, *up)
        back_sides = [sides, comm.twin(sides)]
        g_mine, g_twin = call(halves_kernel, [shape((n_batch, lanes, half), bf16)] * 2)(*g_all)
        g_twin = comm.twin(g_twin)
    else:
        back_sides, _ = comm.spread(back, [])
    d_scores, d_ctx_all, dq_mine, dq_twin = call(
        functools.partial(back_kernel, rows),
        [
            shape((images, pix, every), bf16),
            shape((images, wide, every), bf16),
            shape(small, f32),
            shape(small, bf16),
        ],
        grid=(images,),
        ins=[one_of((pix, wide)), one_of((wide, pix)), one_of((pix, every)), one_of((1, every))]
        + [whole(small)] * 2,
        outs=[one_of((pix, every)), one_of((wide, every)), whole(small), whole(small)],
        scratch=[pltpu.VMEM((wide, every), bf16)],
    )(pix_x, pix_t, probs, top, *back_sides)

    pixel_grad = call(
        functools.partial(pixel_grad_kernel, feats), shape((feats, images, pix), f32)
    )(d_scores, probs, q_all, d_ctx_all)

    def place(masks, firsts, pieces, old=()):
        count = 2 * sum(v.shape[0] for v in pieces)
        hbm, vmem = pl.BlockSpec(memory_space=pltpu.HBM), pl.BlockSpec(memory_space=pltpu.VMEM)
        return list(
            pl.pallas_call(
                functools.partial(place_kernel, masks, firsts, len(old)),
                out_shape=[shape((width, width), f32)] * 2,
                in_specs=[vmem] * (2 * len(pieces)) + [hbm] * len(old),
                out_specs=[hbm] * 2,
                scratch_shapes=[pltpu.VMEM((count, size, width), f32), pltpu.SemaphoreType.DMA((count,))],
                input_output_aliases={2 * len(pieces) + i: i for i in range(len(old))},
                compiler_params=pltpu.CompilerParams(vmem_limit_bytes=VMEM_LIMIT),
            )(*pieces, *map(comm.twin, pieces), *old)
        )

    def folded(mine, twin):
        return call(
            functools.partial(fold_kernel, blocks),
            [shape(mine.shape[1:], f32)] + [shape(mine.shape[1:], bf16)] * (blocks - 1),
        )(mine, comm.twin(twin))

    if cut:
        first, down, *rest = call(
            functools.partial(fold_down_kernel, n_batch),
            [shape((wide, lanes), f32), shape((size, half), f32)]
            + [shape((wide + blocks * size, lanes), bf16)] * (blocks - 1),
            scratch=[pltpu.VMEM((tall, half), f32)],
        )(dq_mine, comm.twin(dq_twin), g_mine, g_twin, *act)
        up_keep, *up_send = call(
            split_kernel, [shape((size, half), f32)] + [shape((size, half), bf16)] * (n_batch - 1)
        )(up)
        up = [up_keep] + comm.to_z(up_send)
        dq = [first] + comm.to_chips(rest)
    else:
        first, *rest = folded(dq_mine, dq_twin)
        dq = [first] + comm.to_chips(rest)
    latent_grad, *both = call(
        functools.partial(latent_kernel, scale, blocks - 1, cut),
        [shape((lanes, width), f32)]
        + [shape((blocks, 2 * wide, part), f32), shape((blocks, 2 * wide, part), bf16)] * cut
        + [shape((2 * wide, width), f32)] * (not cut),
        scratch=[pltpu.VMEM((2 * wide, width), f32)] * cut + [pltpu.VMEM((wide, lanes), f32)],
    )(*dq, ctx, x, normed, gain1, w_key, w_query, d_resid, c_part)
    if cut:
        both, up = tie(both, up)
        first, *rest = folded(*both)
        up = call(add_kernel, shape((size, half), bf16))(*up)
        down = call(unfold_kernel, shape((size, half), bf16))(down, *dq[1:])
        own = call(stack_kernel, shape((2, size, half), bf16))(up, down)
        sums, (pixel_grad, *own) = tie([first] + comm.to_chips(rest), [pixel_grad, *comm.all_z(own)])
        own = call(stack_kernel, shape((n_batch, 2, size, half), bf16))(*own)
        sums = call(add_kernel, shape((2 * wide, part), bf16))(*sums)
        own = [own] + [comm.swap_chip(own, m) for m in (1, 2)]
        (sums,), own = tie([comm.sum_z(sums)], own)
        low, high = call(forward_kernel, [shape((n_batch // 2, 2, size, half), bf16)] * 2)(*own[1:])
        far = [comm.swap_chip(low, 2), comm.swap_chip(high, 1)]
        grads = place((0, 1, 2), (0, 0, 0), own)
        pieces, (*far, grads[0], grads[1]) = tie(comm.all_chips(sums), [*far, *grads])
        pieces = call(stack_kernel, shape((blocks, 2 * wide, part), bf16))(*pieces)
        pieces = [pieces, comm.twin(pieces)]
    else:
        pieces = [lax.psum(both[0], ("batch", "seq"))]
    steps = 4
    hbm, vmem = pl.BlockSpec(memory_space=pltpu.HBM), pl.BlockSpec(memory_space=pltpu.VMEM)
    *vectors, grad_query, grad_out, grad_key, grad_value = pl.pallas_call(
        functools.partial(final_kernel, scale, blocks if cut else 0),
        out_shape=[shape((1, width), f32)] * 6 + [shape((width, width), f32)] * 2 + [shape((feats, width), f32)] * 2,
        in_specs=[vmem] * (len(pieces) + 4),
        out_specs=[vmem] * 6 + [hbm] * 4,
        scratch_shapes=[
            pltpu.VMEM((2 * wide, width), bf16),
            pltpu.VMEM((2, steps, width // steps, width), f32),
            pltpu.VMEM((2, feats, width), f32),
            pltpu.SemaphoreType.DMA((2 * steps + 2,)),
        ],
        compiler_params=pltpu.CompilerParams(vmem_limit_bytes=24 << 20),
    )(*pieces, w_query, w_key, w_value, w_out)
    if cut:
        grads[:1], vectors[:1] = tie(grads[:1], vectors[:1])
        grad_up, grad_down = place((3, 3), (0, n_batch // 2), far, grads)
    vectors = [v.reshape(width) for v in vectors]
    if not cut:
        grad_up = lax.psum(dot(trio[0], trio[2], 0, 0), ("batch", "seq"))
        grad_down = lax.psum(dot(trio[1], g, 0, 0), ("batch", "seq"))
    dims = (images, rows, width)
    return (
        new_latents.reshape(dims),
        latent_grad.reshape(dims),
        pixel_grad.transpose(1, 2, 0),
        vectors[0],
        vectors[1],
        grad_query,
        grad_key,
        grad_value,
        grad_out,
        vectors[2],
        vectors[3],
        grad_up,
        vectors[4],
        grad_down,
        vectors[5],
    )


def solution(mesh):
    split = P("batch", "seq", None)
    placed = (split, split, P("batch", "seq")) + (P(),) * 12 + (split,)
    return jax.shard_map(
        functools.partial(shards, mesh.shape["seq"], mesh.shape["batch"]),
        mesh=mesh,
        in_specs=placed,
        out_specs=(split, split, split) + (P(),) * 12,
        check_vma=False,
    )
```

```python
import functools

import jax
import jax.numpy as jnp
from jax import lax
from jax.experimental import pallas as pl
from jax.experimental.pallas import tpu as pltpu
from jax.sharding import PartitionSpec as P

f32 = jnp.float32
bf16 = jnp.bfloat16
EPS = 1e-05
DROP = -1e30
ONE, TOP, MASK = 0, 3, 6
VMEM_LIMIT = 20 << 20


def dot(a, b, ca, cb):
    return lax.dot_general(a, b, (((ca,), (cb,)), ((), ())), preferred_element_type=f32)


def shape(dims, dtype):
    return jax.ShapeDtypeStruct(dims, dtype)


def call(body, out, grid=(), ins=None, outs=None, scratch=(), limit=VMEM_LIMIT):
    kwargs = {}
    if grid:
        kwargs = dict(grid=grid, in_specs=ins, out_specs=outs)
    elif ins:
        kwargs = dict(in_specs=ins)
    return pl.pallas_call(
        body,
        out_shape=out,
        scratch_shapes=list(scratch),
        compiler_params=pltpu.CompilerParams(vmem_limit_bytes=limit),
        **kwargs,
    )


def whole(dims):
    return pl.BlockSpec(dims, lambda *_: (0,) * len(dims))


def one_of(dims):
    return pl.BlockSpec((1,) + dims, lambda i, *_: (i,) + (0,) * len(dims))


def split3(v):
    hi = v.astype(bf16).astype(f32)
    mid = (v - hi).astype(bf16).astype(f32)
    return hi, mid, v - hi - mid


def position():
    s = lax.axis_index("seq")
    return lax.rem(s, 2), lax.div(s, 2), lax.axis_index("batch")


def slot(start, size):
    return pl.ds(pl.multiple_of(start, size), size)


def tail_rows(rows, lanes):
    at = lax.broadcasted_iota(jnp.int32, (8, lanes), 0)
    tile = jnp.zeros((8, lanes), f32)
    for k, v in rows.items():
        tile = jnp.where(at == k, v, tile)
    return tile


def norm_parts(v):
    mean = jnp.mean(v, axis=-1, keepdims=True)
    centered = v - mean
    spread = jnp.mean(centered * centered, axis=-1, keepdims=True)
    scale = lax.rsqrt(spread + EPS)
    return centered * scale, scale


def norm_back(d_out, hat, scale, gain):
    d_hat = d_out * gain
    mean = jnp.mean(d_hat, axis=-1, keepdims=True)
    along = jnp.mean(d_hat * hat, axis=-1, keepdims=True)
    return scale * (d_hat - mean - hat * along)


def gelu_and_slope(v):
    cdf = 0.5 * (1.0 + lax.erf(v * (0.5**0.5)))
    pdf = jnp.exp(-0.5 * v * v) * (1.0 / (2.0 * 3.141592653589793) ** 0.5)
    return v * cdf, cdf + v * pdf


def chunks(n, size=256):
    return [(a, min(size, n - a)) for a in range(0, n, size)]


def query_kernel(scale, *refs):
    sources, (qk_ref, normed_ref), refs = refs[:5], refs[5:7], refs[7:]
    held, (pad_ref, sems) = refs[:5], refs[5:]
    x_ref, gain_ref, shift_ref, wq_ref, wk_ref = held
    steps = sems.shape[0] - 4
    tall = wq_ref.shape[0] // steps
    copies = [pltpu.make_async_copy(sources[k], held[k], sems.at[k]) for k in range(3)]
    for k in range(steps):
        rows = slice(k * tall, (k + 1) * tall)
        copies.append(pltpu.make_async_copy(sources[3].at[rows], wq_ref.at[rows], sems.at[3 + k]))
    copies.append(pltpu.make_async_copy(sources[4], wk_ref, sems.at[3 + steps]))
    for copy in copies:
        copy.start()
    feats = wk_ref.shape[0]
    wide, lanes = qk_ref.shape
    for copy in copies[:3]:
        copy.wait()
    hat, _ = norm_parts(x_ref[...].astype(f32))
    normed = (hat * gain_ref[...] + shift_ref[...]).astype(bf16)
    normed_ref[...] = normed
    pad_ref[wide - 16 :] = jnp.zeros((16, lanes), f32)
    query = jnp.zeros((lanes, wq_ref.shape[1]), f32)
    for k in range(steps):
        rows = slice(k * tall, (k + 1) * tall)
        copies[3 + k].wait()
        query = query + dot(normed[:, rows], wq_ref[rows], 1, 0)
    copies[3 + steps].wait()
    pad_ref[:feats] = dot(wk_ref[...], (query * scale).astype(bf16), 1, 1)
    pad_ref[wide - 8 :] = tail_rows({MASK: 1.0}, lanes)
    qk_ref[...] = pad_ref[...].astype(bf16)


def pixel_kernel(pix_ref, keep_ref, x_ref, t_ref, pad_ref):
    feats, n = pix_ref.shape[1:]
    wide = t_ref.shape[1]
    keep = keep_ref[pl.ds(pl.program_id(0), 1), :]
    bias = jnp.where(keep > 0, 0.0, DROP).astype(f32)
    pad_ref[wide - 16 :] = jnp.zeros((16, n), f32)
    pad_ref[:feats] = pix_ref[0].astype(f32)
    pad_ref[wide - 8 :] = tail_rows({ONE: 1.0, ONE + 1: 1.0, ONE + 2: 1.0, MASK: bias}, n)
    t_ref[0] = pad_ref[...].astype(bf16)
    x_ref[0] = pad_ref[...].T.astype(bf16)


def weight_kernel(wv_ref, wo_ref, g_ref, wd_ref, hi_ref, lo_ref, dact_ref, pad_ref):
    feats = wv_ref.shape[0]
    pad_ref[...] = jnp.zeros(pad_ref.shape, f32)
    pad_ref[:feats] = dot(wv_ref[...], wo_ref[...], 1, 0)
    v = pad_ref[...]
    hi = v.astype(bf16)
    hi_ref[...] = hi
    lo_ref[...] = (v - hi.astype(f32)).astype(bf16)
    dact_ref[...] = dot(g_ref[...], wd_ref[...], 1, 1)


def lay_lanes(i, rows, refs, out_ref):
    for k in range(2):

        @pl.when(i == k)
        def _():
            parts = [ref[b, :, k * rows : (k + 1) * rows] for ref in refs for b in range(ref.shape[0])]
            out_ref[...] = jnp.concatenate(parts, axis=1)


def unlay_lanes(i, rows, v, mine_ref, twin_ref):
    blocks = mine_ref.shape[0]
    for k in range(2):

        @pl.when(i == k)
        def _():
            for b in range(2 * blocks):
                ref = (mine_ref, twin_ref)[b // blocks]
                piece = v[:, b * rows : (b + 1) * rows].astype(ref.dtype)
                ref[b % blocks, :, k * rows : (k + 1) * rows] = piece


def attend_kernel(rows, x_ref, t_ref, *refs):
    *sides, p_ref, q_ref, top_ref, pm_ref, pt_ref, s_ref = refs
    i = pl.program_id(0)
    n = x_ref.shape[1]
    wide, lanes = q_ref.shape[1:]
    lay_lanes(i, rows, sides, q_ref.at[0])
    q = q_ref[0]
    top = jnp.full((1, lanes), -jnp.inf, f32)
    for a, size in chunks(n):
        s = dot(x_ref[0, a : a + size], q, 1, 0)
        s_ref[a : a + size] = s
        top = jnp.maximum(top, jnp.max(s, axis=0, keepdims=True))
    total = jnp.zeros((wide, lanes), f32)
    for a, size in chunks(n):
        p = jnp.exp(s_ref[a : a + size] - top).astype(bf16)
        p_ref[0, a : a + size] = p
        total = total + dot(t_ref[0, :, a : a + size], p, 1, 0)
    top_ref[0] = top
    tile = total[wide - 8 :]
    at = lax.broadcasted_iota(jnp.int32, tile.shape, 0)
    sums = jnp.sum(jnp.where(at == ONE, tile, 0.0), axis=0, keepdims=True)
    stats = {ONE + j: piece for j, piece in enumerate(split3(sums))}
    stats.update({TOP + j: piece for j, piece in enumerate(split3(top))})
    tile = tail_rows(stats, lanes)
    unlay_lanes(i, rows, jnp.concatenate([total[: wide - 8], tile], axis=0), pm_ref, pt_ref)


def merge_kernel(a_ref, b_ref, keep_ref, *send_refs):
    blocks, wide, lanes = a_ref.shape
    base = wide - 8
    at = lax.broadcasted_iota(jnp.int32, (8, lanes), 0)
    for k, ref in enumerate((keep_ref, *send_refs)):
        sides = [a_ref[k], b_ref[k].astype(f32)]
        (ta, tb), (sa, sb) = (
            [jnp.sum(jnp.where((at >= r) & (at < r + 3), v[base:], 0.0), axis=0, keepdims=True) for v in sides]
            for r in (TOP, ONE)
        )
        top = jnp.maximum(ta, tb)
        wa, wb = jnp.exp(ta - top), jnp.exp(tb - top)
        v = sides[0][:base] * wa + sides[1][:base] * wb
        rows = {ONE + j: piece for j, piece in enumerate(split3(sa * wa + sb * wb))}
        rows.update({TOP + j: piece for j, piece in enumerate(split3(top))})
        ref[...] = jnp.concatenate([v, tail_rows(rows, lanes)], axis=0).astype(ref.dtype)


def mlp_forward_kernel(feats, n_got, keep_ref, *refs):
    got_refs, refs = refs[:n_got], refs[n_got:]
    x_ref, hi_ref, lo_ref, gain_ref, shift_ref, wu_ref, bu_ref, dact_ref, *outs = refs
    trio_ref, ctx_ref, lse_ref, resid_ref = outs
    wide, lanes = keep_ref.shape
    base = wide - 8
    parts = [keep_ref[...]] + [ref[...].astype(f32) for ref in got_refs]
    at = lax.broadcasted_iota(jnp.int32, (8, lanes), 0)
    tops, sums = (
        [jnp.sum(jnp.where((at >= k) & (at < k + 3), v[base:], 0.0), axis=0, keepdims=True) for v in parts]
        for k in (TOP, ONE)
    )
    peak = functools.reduce(jnp.maximum, tops)
    total = jnp.zeros((1, lanes), f32)
    ctx = jnp.zeros((wide, lanes), f32)
    for v, top, part in zip(parts, tops, sums):
        share = jnp.exp(top - peak)
        total = total + part * share
        ctx = ctx + v * share
    ctx = ctx / total
    lse_ref[...] = peak + jnp.log(total)
    row = lax.broadcasted_iota(jnp.int32, (wide, lanes), 0)
    ctx = jnp.where(row < feats, ctx, 0.0)
    ctx_ref[...] = ctx
    ctx_b = ctx.astype(bf16)
    resid = x_ref[...].astype(f32) + dot(ctx_b, hi_ref[...], 0, 0) + dot(ctx_b, lo_ref[...], 0, 0)
    resid_ref[...] = resid
    hat, _ = norm_parts(resid)
    normed = (hat * gain_ref[...] + shift_ref[...]).astype(bf16)
    trio_ref[0] = normed
    pre = dot(normed, wu_ref[...], 1, 0) + bu_ref[...]
    act_f, slope = gelu_and_slope(pre)
    trio_ref[1] = act_f.astype(bf16)
    trio_ref[2] = (dact_ref[...] * slope).astype(bf16)


def mlp_backward_kernel(trio_ref, ctx_ref, lse_ref, resid_ref, g_ref, hi_ref, lo_ref, gain_ref, wu_ref, *outs):
    dres_ref, back_ref, vector_ref = outs
    wide, lanes = ctx_ref.shape
    hat, scale = norm_parts(resid_ref[...])
    d_pre = trio_ref[2]
    d_normed = dot(d_pre, wu_ref[...], 1, 1)
    g = g_ref[...].astype(f32)
    d_resid = g + norm_back(d_normed, hat, scale, gain_ref[...])
    dres_ref[...] = d_resid
    d_resid_b = d_resid.astype(bf16)
    d_ctx = (dot(hi_ref[...], d_resid_b, 1, 1) + dot(lo_ref[...], d_resid_b, 1, 1)).astype(bf16)
    delta = jnp.sum(ctx_ref[...] * d_ctx.astype(f32), axis=0, keepdims=True)
    rows = {ONE + k: -v for k, v in enumerate(split3(delta))}
    rows.update({TOP + k: v for k, v in enumerate(split3(lse_ref[...]))})
    back_ref[...] = jnp.concatenate([d_ctx[: wide - 8], tail_rows(rows, lanes).astype(bf16)], axis=0)
    vectors = {
        0: jnp.sum(d_normed * hat, axis=0, keepdims=True),
        1: jnp.sum(d_normed, axis=0, keepdims=True),
        2: jnp.sum(d_pre.astype(f32), axis=0, keepdims=True),
        3: jnp.sum(g, axis=0, keepdims=True),
    }
    vector_ref[...] = tail_rows(vectors, g.shape[1])


def mlp_rest_kernel(trio_ref, ctx_ref, resid_ref, dres_ref, vector_ref, wd_ref, bd_ref, new_ref, csum_ref):
    base = csum_ref.shape[0] - 8
    new_ref[...] = (resid_ref[...] + dot(trio_ref[1], wd_ref[...], 1, 0) + bd_ref[...]).astype(bf16)
    csum_ref[:base] = dot(ctx_ref[...].astype(bf16), dres_ref[...].astype(bf16), 1, 0)[:base]
    csum_ref[base:] = vector_ref[...]


def back_kernel(rows, x_ref, t_ref, p_ref, top_ref, *refs):
    sides, (ds_ref, dc_ref, dm_ref, dt_ref, b_ref) = refs[:2], refs[2:]
    i = pl.program_id(0)
    pix = x_ref.shape[1]
    wide, lanes = b_ref.shape
    lay_lanes(i, rows, sides, b_ref)
    b = b_ref[...]
    tail = b[wide - 16 :].astype(f32)[8:]
    at = lax.broadcasted_iota(jnp.int32, tail.shape, 0)
    lse = jnp.sum(jnp.where((at >= TOP) & (at < TOP + 3), tail, 0.0), axis=0, keepdims=True)
    ratio = jnp.exp(top_ref[0] - lse)
    dc_ref[0] = (b.astype(f32) * ratio).astype(bf16)
    sums = jnp.zeros((wide, lanes), f32)
    for a, size in chunks(pix):
        d = dot(x_ref[0, a : a + size], b, 1, 0)
        ds = (p_ref[0, a : a + size].astype(f32) * (d * ratio)).astype(bf16)
        ds_ref[0, a : a + size] = ds
        sums = sums + dot(t_ref[0, :, a : a + size], ds, 1, 0)
    unlay_lanes(i, rows, sums, dm_ref, dt_ref)


def pixel_grad_kernel(feats, ds_ref, p_ref, q_ref, dc_ref, out_ref):
    for i in range(ds_ref.shape[0]):
        for a, size in chunks(ds_ref.shape[1]):
            rows = slice(a, a + size)
            v = dot(q_ref[i], ds_ref[i, rows], 1, 1) + dot(dc_ref[i], p_ref[i, rows], 1, 1)
            out_ref[:, i, rows] = v[:feats]


def latent_kernel(scale, n_got, cut, *refs):
    dq_refs, refs = refs[: n_got + 1], refs[n_got + 1 :]
    ctx_ref, x_ref, normed_ref, gain_ref, wk_ref, wq_ref, dres_ref, c_ref, *outs = refs
    lat_ref, *outs, dq_ref = outs
    feats = wk_ref.shape[0]
    wide, lanes = dq_ref.shape
    base = wide - 8
    dq_ref[...] = dq_refs[0][...]
    for ref in dq_refs[1:]:
        dq_ref[...] += ref[:wide].astype(f32)
    d = dq_ref[...] - dq_ref[pl.ds(base + ONE, 1)] * ctx_ref[...]
    row = lax.broadcasted_iota(jnp.int32, (wide, lanes), 0)
    d = jnp.where(row < feats, d, 0.0).astype(bf16)
    d_query = dot(d[:feats], wk_ref[...], 0, 0).astype(bf16)
    d_normed = dot(d_query, wq_ref[...], 1, 1) * scale
    hat, spread = norm_parts(x_ref[...].astype(f32))
    vectors = {
        0: jnp.sum(d_normed * hat, axis=0, keepdims=True),
        1: jnp.sum(d_normed, axis=0, keepdims=True),
    }
    both_ref = outs[-1]
    both_ref[:base] = dot(d, normed_ref[...], 1, 0)[:base]
    both_ref[base:wide] = tail_rows(vectors, both_ref.shape[1])
    both_ref[wide:] = c_ref[...]
    if cut:
        mine_ref, twin_ref = outs[:2]
        core, chip, _ = position()
        n, _, part = mine_ref.shape
        for b in range(n):
            at = (chip ^ b) * part
            mine_ref[b] = both_ref[:, slot(core * n * part + at, part)]
            twin_ref[b] = both_ref[:, slot((1 - core) * n * part + at, part)].astype(bf16)
    lat_ref[...] = dres_ref[...] + norm_back(d_normed, hat, spread, gain_ref[...])


def halves_kernel(*refs):
    mine_ref, other_ref = refs[-2:]
    core, half = position()[0], mine_ref.shape[2]
    for j, ref in enumerate(refs[:-2]):
        mine_ref[j] = ref[:, slot(core * half, half)]
        other_ref[j] = ref[:, slot((1 - core) * half, half)]


def up_kernel(n, trio_ref, twin_ref, back_ref, *refs):
    core, chip, z = position()
    up_refs, act_refs = refs[:n], refs[n:]
    tall, half = up_refs[0].shape
    part = up_refs[1].shape[1]
    cols = slot(core * half, half)
    slab = act_refs[0].shape[1]
    for j, ref in enumerate(act_refs):
        rows = slot(lax.rem(z + j, len(act_refs)) * slab, slab)
        ref[...] = jnp.concatenate([trio_ref[1, :, rows], twin_ref[1, :, rows]], axis=0)
    d_pre = jnp.concatenate([trio_ref[2, :, cols], twin_ref[2, :, cols]], axis=0)
    for m, ref in enumerate(up_refs):
        rows = slot((chip ^ m) * tall, tall)
        normed = jnp.concatenate([trio_ref[0, :, rows], twin_ref[0, :, rows]], axis=0)
        v = dot(normed, d_pre, 0, 0)
        if m == 0:
            ref[...] = v
        else:
            for q in range(half // part):
                ref[q * tall : (q + 1) * tall] = v[:, q * part : (q + 1) * part].astype(bf16)
            ref[half // part * tall :] = back_ref[...]


def part_kernel(n, *refs):
    back_ref, up_ref, *got_refs = refs[: n + 1]
    sides_ref, sum_ref = refs[n + 1 :]
    tall, half = up_ref.shape
    wide, part = back_ref.shape
    base = got_refs[0].shape[0] - wide
    sides_ref[0] = back_ref[...]
    for m, ref in enumerate(got_refs, 1):
        sides_ref[m] = ref[base:]
    for q in range(half // part):
        cols = slice(q * part, (q + 1) * part)
        v = up_ref[:, cols]
        for ref in got_refs:
            v = v + ref[q * tall : (q + 1) * tall].astype(f32)
        sum_ref[:, cols] = v


def total(refs):
    v = refs[0][...].astype(f32)
    for ref in refs[1:]:
        v = v + ref[...].astype(f32)
    return v


def split_kernel(sum_ref, *out_refs):
    z = position()[2]
    size = out_refs[0].shape[0]
    for j, ref in enumerate(out_refs):
        ref[...] = sum_ref[slot(lax.rem(z + j, len(out_refs)) * size, size)].astype(ref.dtype)


def fold_kernel(n, mine_ref, twin_ref, keep_ref, *out_refs):
    keep_ref[...] = mine_ref[0] + twin_ref[0].astype(f32)
    for m, ref in enumerate(out_refs, 1):
        ref[...] = (mine_ref[m] + twin_ref[m].astype(f32)).astype(bf16)


def fold_down_kernel(n_batch, mine_ref, twin_ref, g_ref, g2_ref, *refs):
    act_refs, refs = refs[:n_batch], refs[n_batch:]
    keep_ref, own_ref, *send_refs, sum_ref = refs
    chip = position()[1]
    base, part = keep_ref.shape
    size = own_ref.shape[0]
    act = jnp.concatenate([ref[...] for ref in act_refs], axis=0)
    g = jnp.concatenate([ref[j] for j in range(n_batch) for ref in (g_ref, g2_ref)], axis=0)
    sum_ref[...] = dot(act, g, 0, 0)
    keep_ref[...] = mine_ref[0] + twin_ref[0].astype(f32)
    own_ref[...] = sum_ref[slot(chip * size, size)]
    for m, ref in enumerate(send_refs, 1):
        ref[:base] = (mine_ref[m] + twin_ref[m].astype(f32)).astype(bf16)
        v = sum_ref[slot((chip ^ m) * size, size)].astype(bf16)
        for q in range(v.shape[1] // part):
            ref[base + q * size : base + (q + 1) * size] = v[:, q * part : (q + 1) * part]


def unfold_kernel(own_ref, *refs):
    got_refs, out_ref = refs[:-1], refs[-1]
    size, half = own_ref.shape
    part = got_refs[0].shape[1]
    base = got_refs[0].shape[0] - size * (half // part)
    for q in range(half // part):
        cols = slice(q * part, (q + 1) * part)
        v = own_ref[:, cols]
        for ref in got_refs:
            v = v + ref[base + q * size : base + (q + 1) * size].astype(f32)
        out_ref[:, cols] = v.astype(bf16)


def add_kernel(*refs):
    refs[-1][...] = total(refs[:-1]).astype(refs[-1].dtype)


def stack_kernel(*refs):
    for j, ref in enumerate(refs[:-1]):
        refs[-1][j] = ref[...]


def forward_kernel(x_ref, y_ref, low_ref, high_ref):
    half = low_ref.shape[0]
    low_ref[...] = x_ref[:half]
    high_ref[...] = y_ref[half:]


def place_blocks(masks, firsts, pieces, up_ref, down_ref, held_ref, sems):
    n = len(masks)
    core, chip, z = position()
    half = up_ref.shape[1] // 2
    n_batch = up_ref.shape[0] // (4 * held_ref.shape[1])
    size = held_ref.shape[1]
    copies = []
    for i, (m, first) in enumerate(zip(masks, firsts)):
        for j in range(pieces[i].shape[0]):
            k, z_at = chip ^ m, z ^ z_masks(n_batch)[first + j]
            for h, (out_ref, row) in enumerate(((up_ref, k * n_batch + z_at), (down_ref, z_at * 4 + k))):
                at = len(copies)
                for side, col in enumerate((core, 1 - core)):
                    held_ref[at, :, slot(col * half, half)] = pieces[side * n + i][j, h].astype(f32)
                copy = pltpu.make_async_copy(held_ref.at[at], out_ref.at[slot(row * size, size)], sems.at[at])
                copy.start()
                copies.append(copy)
    return copies


def place_kernel(masks, firsts, *refs):
    pieces, outs = refs[: 2 * len(masks)], refs[2 * len(masks) :]
    for copy in place_blocks(masks, firsts, pieces, *outs):
        copy.wait()


def final_kernel(scale, n, *refs):
    pieces, refs = refs[: 1 + (n > 0)], refs[1 + (n > 0) :]
    if n > 0:
        far, refs = refs[:4], refs[6:]
        *refs, up_ref, down_ref, both_ref, tall_ref, flat_ref, sems, held_ref, held_sems = refs
        refs = (*refs, both_ref, tall_ref, flat_ref, sems)
    wq_ref, wk_ref, wv_ref, wo_ref, *out_refs, both_ref, tall_ref, flat_ref, sems = refs
    vector_refs, out_refs = out_refs[:6], out_refs[6:]
    feats, width = wk_ref.shape
    wide = both_ref.shape[0] // 2
    steps = tall_ref.shape[1]
    tall = width // steps
    if n == 0:
        both_ref[...] = pieces[0][...].astype(bf16)
    else:
        core, chip, _ = position()
        for side, col in enumerate((core, 1 - core)):
            part = pieces[side].shape[2]
            for b in range(n):
                both_ref[:, slot(col * n * part + (chip ^ b) * part, part)] = pieces[side][b]
    for k, ref in enumerate(vector_refs):
        base, at = (wide, k) if k < 2 else (2 * wide, k - 2)
        ref[...] = both_ref[base - 16 : base].astype(f32)[8 + at : 9 + at]
    copies = []
    placed = []
    for h, (base, w_ref) in enumerate(((0, wk_ref), (wide, wv_ref))):
        for j in range(steps):
            rows = slice(j * tall, (j + 1) * tall)
            if h == 0:
                v = dot(both_ref[:wide, rows][:feats], w_ref[...], 0, 0) * scale
            else:
                v = dot(w_ref[:, rows], both_ref[wide:][:feats], 0, 0)
            tall_ref[h, j] = v
            copies.append(pltpu.make_async_copy(tall_ref.at[h, j], out_refs[h].at[rows], sems.at[len(copies)]))
            copies[-1].start()
    if n > 0:
        placed = place_blocks((3, 3), (0, far[0].shape[0]), far, up_ref, down_ref, held_ref, held_sems)
    for h in range(2):
        if h == 0:
            v = dot(both_ref[:wide], wq_ref[...], 1, 0) * scale
        else:
            v = dot(both_ref[wide:], wo_ref[...], 1, 1)
        flat_ref[h] = v[:feats]
        copies.append(pltpu.make_async_copy(flat_ref.at[h], out_refs[2 + h], sems.at[len(copies)]))
        copies[-1].start()
    for copy in copies + placed:
        copy.wait()


def seq_send(v, mask, n):
    return lax.ppermute(v, "seq", [(i, i ^ mask) for i in range(n)])


def batch_send(v, shift, n):
    return lax.ppermute(v, "batch", [(i, (i + shift) % n) for i in range(n)])


def z_masks(n):
    masks = [0]
    while len(masks) < n:
        masks = masks + [m ^ (2 * len(masks) - 1) for m in masks]
    return masks


class Comm:
    def __init__(self, n_seq, n_batch):
        self.n_seq, self.n_batch = n_seq, n_batch
        self.chips = n_seq // 2

    def twin(self, v):
        return seq_send(v, 1, self.n_seq)

    def swap_chip(self, v, mask):
        return seq_send(v, 2 * mask, self.n_seq)

    def to_chips(self, pieces):
        return [seq_send(v, 2 * m, self.n_seq) for m, v in enumerate(pieces, 1)]

    def to_z(self, pieces):
        n = self.n_batch
        order = sorted(range(1, n), key=lambda j: min(j, n - j))
        got = {j: batch_send(pieces[j - 1], j, n) for j in order}
        return [got[j] for j in range(1, n)]

    def next_z(self, v):
        return batch_send(v, 1, self.n_batch)

    def sum_z(self, v):
        mask = 1
        while mask < self.n_batch:
            pairs = [(i, i ^ (2 * mask - 1)) for i in range(self.n_batch)]
            other = lax.ppermute(v, "batch", pairs)
            v = call(add_kernel, shape(v.shape, v.dtype))(v, other)
            mask *= 2
        return v

    def all_z(self, v):
        got = [v]
        while len(got) < self.n_batch:
            pairs = [(i, i ^ (2 * len(got) - 1)) for i in range(self.n_batch)]
            got = got + [lax.ppermute(piece, "batch", pairs) for piece in got]
        return got

    def all_chips(self, v):
        return [v] + self.to_chips([v] * (self.chips - 1))

    def spread(self, v, beside):
        mine, beside = tie(self.all_chips(v), beside)
        mine = call(stack_kernel, shape((self.chips, *v.shape), v.dtype))(*mine)
        return [mine, self.twin(mine)], beside


def tie(first, second):
    out = lax.optimization_barrier((*first, *second))
    return list(out[: len(first)]), list(out[len(first) :])


def add_all(first, rest):
    for v in rest:
        first = first + v.astype(f32)
    return first


def shards(
    n_seq,
    n_batch,
    latents,
    pixels,
    keep_mask,
    gain_attn,
    shift_attn,
    w_query,
    w_key,
    w_value,
    w_out,
    gain_mlp,
    shift_mlp,
    w_up,
    bias_up,
    w_down,
    bias_down,
    cotangent,
):
    images, rows, width = latents.shape
    pix, feats = pixels.shape[1:]
    hidden = w_up.shape[1]
    wide = -(-(feats + 8) // 16) * 16
    lanes = images * rows
    scale = width ** (-0.5)
    comm = Comm(n_seq, n_batch)
    blocks = comm.chips
    every = n_seq * rows
    x = latents.reshape(lanes, width)
    g = cotangent.reshape(lanes, width)
    gain1, shift1, gain2, shift2, b_up, b_down = (
        v.reshape(1, -1) for v in (gain_attn, shift_attn, gain_mlp, shift_mlp, bias_up, bias_down)
    )
    small = (blocks, wide, lanes)

    operands = (x, gain1, shift1, w_query, w_key)
    qk, normed = call(
        functools.partial(query_kernel, scale),
        [shape((wide, lanes), bf16), shape((lanes, width), bf16)],
        ins=[pl.BlockSpec(memory_space=pltpu.HBM)] * 5,
        scratch=[pltpu.VMEM(v.shape, v.dtype) for v in operands]
        + [pltpu.VMEM((wide, lanes), f32), pltpu.SemaphoreType.DMA((8,))],
        limit=60 << 20,
    )(*operands)

    pix_x, pix_t = call(
        pixel_kernel,
        [shape((images, pix, wide), bf16), shape((images, wide, pix), bf16)],
        grid=(images,),
        ins=[one_of((feats, pix)), whole((images, pix))],
        outs=[one_of((pix, wide)), one_of((wide, pix))],
        scratch=[pltpu.VMEM((wide, pix), f32)],
    )(pixels.transpose(0, 2, 1), keep_mask)
    (qk,), g_all = tie([qk], [g])
    g_all.append(comm.next_z(g_all[0]))
    q_sides, (pix_x, g_all[1]) = comm.spread(qk, [pix_x, g_all[1]])
    vo_hi, vo_lo, d_act = call(
        weight_kernel,
        [shape((wide, width), bf16)] * 2 + [shape((lanes, hidden), f32)],
        scratch=[pltpu.VMEM((wide, width), f32)],
    )(w_value, w_out, g, w_down)

    probs, q_all, top, part_mine, part_twin = call(
        functools.partial(attend_kernel, rows),
        [
            shape((images, pix, every), bf16),
            shape((images, wide, every), bf16),
            shape((images, 1, every), f32),
            shape(small, f32),
            shape(small, bf16),
        ],
        grid=(images,),
        ins=[one_of((pix, wide)), one_of((wide, pix))] + [whole(small)] * 2,
        outs=[one_of((pix, every)), one_of((wide, every)), one_of((1, every)), whole(small), whole(small)],
        scratch=[pltpu.VMEM((pix, every), f32)],
    )(pix_x, pix_t, *q_sides)
    keep, *send = call(
        merge_kernel, [shape((wide, lanes), f32)] + [shape((wide, lanes), bf16)] * (blocks - 1)
    )(
        part_mine, comm.twin(part_twin)
    )
    g_next = comm.next_z(g_all[-1])
    got = comm.to_chips(send)

    trio, ctx, lse, resid = call(
        functools.partial(mlp_forward_kernel, feats, blocks - 1),
        [
            shape((3, lanes, width), bf16),
            shape((wide, lanes), f32),
            shape((1, lanes), f32),
            shape((lanes, width), f32),
        ],
    )(keep, *got, x, vo_hi, vo_lo, gain2, shift2, w_up, b_up, d_act)
    (trio_sent,), (g_next,) = tie([trio], [g_next])
    g_all.append(g_next)
    d_resid, back, vector_rows = call(
        mlp_backward_kernel,
        [shape((lanes, width), f32), shape((wide, lanes), bf16), shape((8, width), f32)],
    )(trio, ctx, lse, resid, g, vo_hi, vo_lo, gain2, w_up)
    new_latents, c_part = call(mlp_rest_kernel, [shape((lanes, width), bf16), shape((wide, width), f32)])(
        trio, ctx, resid, d_resid, vector_rows, w_down, b_down
    )

    half = width // 2
    part = half // blocks
    quarter, tall, size = width // blocks, width // n_batch, width // blocks // n_batch
    cut = part == lanes and part % 128 == 0 and size % 16 == 0 and blocks == 4 and n_batch == 4
    tall = hidden // n_batch
    if cut:
        up = call(
            functools.partial(up_kernel, blocks),
            [shape((quarter, half), f32)]
            + [shape((blocks * quarter + wide, part), bf16)] * (blocks - 1)
            + [shape((2 * lanes, tall), bf16)] * n_batch,
        )(trio, comm.twin(trio_sent), back)
        up, act = list(up[:blocks]), list(up[blocks:])
        for _ in range(3, n_batch):
            g_all.append(comm.next_z(g_all[-1]))
        up[1:] = comm.to_chips(up[1:])
        act[1:] = comm.to_z(act[1:])
        up, (new_latents, c_part, *rest) = tie(up, [new_latents, c_part, *act, *g_all[3:]])
        act, g_all[3:] = rest[:n_batch], rest[n_batch:]
        sides, up = call(
            functools.partial(part_kernel, blocks), [shape(small, bf16), shape((quarter, half), f32)]
        )(back, *up)
        back_sides = [sides, comm.twin(sides)]
        g_mine, g_twin = call(halves_kernel, [shape((n_batch, lanes, half), bf16)] * 2)(*g_all)
        g_twin = comm.twin(g_twin)
    else:
        back_sides, _ = comm.spread(back, [])
    d_scores, d_ctx_all, dq_mine, dq_twin = call(
        functools.partial(back_kernel, rows),
        [
            shape((images, pix, every), bf16),
            shape((images, wide, every), bf16),
            shape(small, f32),
            shape(small, bf16),
        ],
        grid=(images,),
        ins=[one_of((pix, wide)), one_of((wide, pix)), one_of((pix, every)), one_of((1, every))]
        + [whole(small)] * 2,
        outs=[one_of((pix, every)), one_of((wide, every)), whole(small), whole(small)],
        scratch=[pltpu.VMEM((wide, every), bf16)],
    )(pix_x, pix_t, probs, top, *back_sides)

    pixel_grad = call(
        functools.partial(pixel_grad_kernel, feats), shape((feats, images, pix), f32)
    )(d_scores, probs, q_all, d_ctx_all)

    hbm, vmem = pl.BlockSpec(memory_space=pltpu.HBM), pl.BlockSpec(memory_space=pltpu.VMEM)

    def place(masks, firsts, pieces):
        count = 2 * sum(v.shape[0] for v in pieces)
        return list(
            pl.pallas_call(
                functools.partial(place_kernel, masks, firsts),
                out_shape=[shape((width, width), f32)] * 2,
                in_specs=[vmem] * (2 * len(pieces)),
                out_specs=[hbm] * 2,
                scratch_shapes=[pltpu.VMEM((count, size, width), f32), pltpu.SemaphoreType.DMA((count,))],
                compiler_params=pltpu.CompilerParams(vmem_limit_bytes=VMEM_LIMIT),
            )(*pieces, *map(comm.twin, pieces))
        )

    def folded(mine, twin):
        return call(
            functools.partial(fold_kernel, blocks),
            [shape(mine.shape[1:], f32)] + [shape(mine.shape[1:], bf16)] * (blocks - 1),
        )(mine, comm.twin(twin))

    if cut:
        first, down, *rest = call(
            functools.partial(fold_down_kernel, n_batch),
            [shape((wide, lanes), f32), shape((size, half), f32)]
            + [shape((wide + blocks * size, lanes), bf16)] * (blocks - 1),
            scratch=[pltpu.VMEM((tall, half), f32)],
        )(dq_mine, comm.twin(dq_twin), g_mine, g_twin, *act)
        up_keep, *up_send = call(
            split_kernel, [shape((size, half), f32)] + [shape((size, half), bf16)] * (n_batch - 1)
        )(up)
        up = [up_keep] + comm.to_z(up_send)
        dq = [first] + comm.to_chips(rest)
    else:
        first, *rest = folded(dq_mine, dq_twin)
        dq = [first] + comm.to_chips(rest)
    latent_grad, *both = call(
        functools.partial(latent_kernel, scale, blocks - 1, cut),
        [shape((lanes, width), f32)]
        + [shape((blocks, 2 * wide, part), f32), shape((blocks, 2 * wide, part), bf16)] * cut
        + [shape((2 * wide, width), f32)] * (not cut),
        scratch=[pltpu.VMEM((2 * wide, width), f32)] * cut + [pltpu.VMEM((wide, lanes), f32)],
    )(*dq, ctx, x, normed, gain1, w_key, w_query, d_resid, c_part)
    if cut:
        both, up = tie(both, up)
        first, *rest = folded(*both)
        up = call(add_kernel, shape((size, half), bf16))(*up)
        down = call(unfold_kernel, shape((size, half), bf16))(down, *dq[1:])
        own = call(stack_kernel, shape((2, size, half), bf16))(up, down)
        sums, (pixel_grad, *own) = tie([first] + comm.to_chips(rest), [pixel_grad, *comm.all_z(own)])
        own = call(stack_kernel, shape((n_batch, 2, size, half), bf16))(*own)
        sums = call(add_kernel, shape((2 * wide, part), bf16))(*sums)
        own = [own] + [comm.swap_chip(own, m) for m in (1, 2)]
        (sums,), own = tie([comm.sum_z(sums)], own)
        low, high = call(forward_kernel, [shape((n_batch // 2, 2, size, half), bf16)] * 2)(*own[1:])
        far = [comm.swap_chip(low, 2), comm.swap_chip(high, 1)]
        grads = place((0, 1, 2), (0, 0, 0), own)
        pieces, (*far, grads[0], grads[1]) = tie(comm.all_chips(sums), [*far, *grads])
        pieces = call(stack_kernel, shape((blocks, 2 * wide, part), bf16))(*pieces)
        pieces = [pieces, comm.twin(pieces)]
    else:
        pieces = [lax.psum(both[0], ("batch", "seq"))]
    steps = 4
    old = [*far, *map(comm.twin, far), *grads] if cut else []
    aliases = {len(pieces) + len(far) * 2 + i: 10 + i for i in range(2)} if cut else {}
    results = pl.pallas_call(
        functools.partial(final_kernel, scale, blocks if cut else 0),
        out_shape=[shape((1, width), f32)] * 6
        + [shape((width, width), f32)] * 2
        + [shape((feats, width), f32)] * 2
        + [shape((width, width), f32)] * (2 * cut),
        in_specs=[vmem] * len(pieces) + ([vmem] * 4 + [hbm] * 2) * cut + [vmem] * 4,
        out_specs=[vmem] * 6 + [hbm] * (4 + 2 * cut),
        scratch_shapes=[
            pltpu.VMEM((2 * wide, width), bf16),
            pltpu.VMEM((2, steps, width // steps, width), f32),
            pltpu.VMEM((2, feats, width), f32),
            pltpu.SemaphoreType.DMA((2 * steps + 2,)),
        ]
        + [pltpu.VMEM((2 * n_batch, size, width), f32), pltpu.SemaphoreType.DMA((2 * n_batch,))] * cut,
        input_output_aliases=aliases,
        compiler_params=pltpu.CompilerParams(vmem_limit_bytes=28 << 20),
    )(*pieces, *old, w_query, w_key, w_value, w_out)
    vectors = [v.reshape(width) for v in results[:6]]
    grad_query, grad_out, grad_key, grad_value = results[6:10]
    if cut:
        grad_up, grad_down = results[10:]
    if not cut:
        grad_up = lax.psum(dot(trio[0], trio[2], 0, 0), ("batch", "seq"))
        grad_down = lax.psum(dot(trio[1], g, 0, 0), ("batch", "seq"))
    dims = (images, rows, width)
    return (
        new_latents.reshape(dims),
        latent_grad.reshape(dims),
        pixel_grad.transpose(1, 2, 0),
        vectors[0],
        vectors[1],
        grad_query,
        grad_key,
        grad_value,
        grad_out,
        vectors[2],
        vectors[3],
        grad_up,
        vectors[4],
        grad_down,
        vectors[5],
    )


def solution(mesh):
    split = P("batch", "seq", None)
    placed = (split, split, P("batch", "seq")) + (P(),) * 12 + (split,)
    return jax.shard_map(
        functools.partial(shards, mesh.shape["seq"], mesh.shape["batch"]),
        mesh=mesh,
        in_specs=placed,
        out_specs=(split, split, split) + (P(),) * 12,
        check_vma=False,
    )
```

```python
import functools

import jax
import jax.numpy as jnp
from jax import lax
from jax.experimental import pallas as pl
from jax.experimental.pallas import tpu as pltpu
from jax.sharding import PartitionSpec as P

f32 = jnp.float32
bf16 = jnp.bfloat16
EPS = 1e-05
DROP = -1e30
ONE, TOP, MASK = 0, 3, 6
VMEM_LIMIT = 20 << 20


def dot(a, b, ca, cb):
    return lax.dot_general(a, b, (((ca,), (cb,)), ((), ())), preferred_element_type=f32)


def shape(dims, dtype):
    return jax.ShapeDtypeStruct(dims, dtype)


def call(body, out, grid=(), ins=None, outs=None, scratch=(), limit=VMEM_LIMIT):
    kwargs = {}
    if grid:
        kwargs = dict(grid=grid, in_specs=ins, out_specs=outs)
    elif ins:
        kwargs = dict(in_specs=ins)
    return pl.pallas_call(
        body,
        out_shape=out,
        scratch_shapes=list(scratch),
        compiler_params=pltpu.CompilerParams(vmem_limit_bytes=limit),
        **kwargs,
    )


def whole(dims):
    return pl.BlockSpec(dims, lambda *_: (0,) * len(dims))


def one_of(dims):
    return pl.BlockSpec((1,) + dims, lambda i, *_: (i,) + (0,) * len(dims))


def split3(v):
    hi = v.astype(bf16).astype(f32)
    mid = (v - hi).astype(bf16).astype(f32)
    return hi, mid, v - hi - mid


def position():
    s = lax.axis_index("seq")
    return lax.rem(s, 2), lax.div(s, 2), lax.axis_index("batch")


def slot(start, size):
    return pl.ds(pl.multiple_of(start, size), size)


def tail_rows(rows, lanes):
    at = lax.broadcasted_iota(jnp.int32, (8, lanes), 0)
    tile = jnp.zeros((8, lanes), f32)
    for k, v in rows.items():
        tile = jnp.where(at == k, v, tile)
    return tile


def norm_parts(v):
    mean = jnp.mean(v, axis=-1, keepdims=True)
    centered = v - mean
    spread = jnp.mean(centered * centered, axis=-1, keepdims=True)
    scale = lax.rsqrt(spread + EPS)
    return centered * scale, scale


def norm_back(d_out, hat, scale, gain):
    d_hat = d_out * gain
    mean = jnp.mean(d_hat, axis=-1, keepdims=True)
    along = jnp.mean(d_hat * hat, axis=-1, keepdims=True)
    return scale * (d_hat - mean - hat * along)


def gelu_and_slope(v):
    cdf = 0.5 * (1.0 + lax.erf(v * (0.5**0.5)))
    pdf = jnp.exp(-0.5 * v * v) * (1.0 / (2.0 * 3.141592653589793) ** 0.5)
    return v * cdf, cdf + v * pdf


def chunks(n, size=256):
    return [(a, min(size, n - a)) for a in range(0, n, size)]


def query_kernel(scale, *refs):
    sources, (qk_ref, normed_ref), refs = refs[:5], refs[5:7], refs[7:]
    held, (pad_ref, sems) = refs[:5], refs[5:]
    x_ref, gain_ref, shift_ref, wq_ref, wk_ref = held
    steps = sems.shape[0] - 4
    tall = wq_ref.shape[0] // steps
    copies = [pltpu.make_async_copy(sources[k], held[k], sems.at[k]) for k in range(3)]
    for k in range(steps):
        rows = slice(k * tall, (k + 1) * tall)
        copies.append(pltpu.make_async_copy(sources[3].at[rows], wq_ref.at[rows], sems.at[3 + k]))
    copies.append(pltpu.make_async_copy(sources[4], wk_ref, sems.at[3 + steps]))
    for copy in copies:
        copy.start()
    feats = wk_ref.shape[0]
    wide, lanes = qk_ref.shape
    for copy in copies[:3]:
        copy.wait()
    hat, _ = norm_parts(x_ref[...].astype(f32))
    normed = (hat * gain_ref[...] + shift_ref[...]).astype(bf16)
    normed_ref[...] = normed
    pad_ref[wide - 16 :] = jnp.zeros((16, lanes), f32)
    query = jnp.zeros((lanes, wq_ref.shape[1]), f32)
    for k in range(steps):
        rows = slice(k * tall, (k + 1) * tall)
        copies[3 + k].wait()
        query = query + dot(normed[:, rows], wq_ref[rows], 1, 0)
    copies[3 + steps].wait()
    pad_ref[:feats] = dot(wk_ref[...], (query * scale).astype(bf16), 1, 1)
    pad_ref[wide - 8 :] = tail_rows({MASK: 1.0}, lanes)
    qk_ref[...] = pad_ref[...].astype(bf16)


def pixel_kernel(pix_ref, keep_ref, x_ref, t_ref, pad_ref):
    feats, n = pix_ref.shape[1:]
    wide = t_ref.shape[1]
    keep = keep_ref[pl.ds(pl.program_id(0), 1), :]
    bias = jnp.where(keep > 0, 0.0, DROP).astype(f32)
    pad_ref[wide - 16 :] = jnp.zeros((16, n), f32)
    pad_ref[:feats] = pix_ref[0].astype(f32)
    pad_ref[wide - 8 :] = tail_rows({ONE: 1.0, ONE + 1: 1.0, ONE + 2: 1.0, MASK: bias}, n)
    t_ref[0] = pad_ref[...].astype(bf16)
    x_ref[0] = pad_ref[...].T.astype(bf16)


def weight_kernel(wv_ref, wo_ref, g_ref, wd_ref, hi_ref, lo_ref, dact_ref, pad_ref):
    feats = wv_ref.shape[0]
    pad_ref[...] = jnp.zeros(pad_ref.shape, f32)
    pad_ref[:feats] = dot(wv_ref[...], wo_ref[...], 1, 0)
    v = pad_ref[...]
    hi = v.astype(bf16)
    hi_ref[...] = hi
    lo_ref[...] = (v - hi.astype(f32)).astype(bf16)
    dact_ref[...] = dot(g_ref[...], wd_ref[...], 1, 1)


def lay_lanes(i, rows, refs, out_ref):
    for k in range(2):

        @pl.when(i == k)
        def _():
            parts = [ref[b, :, k * rows : (k + 1) * rows] for ref in refs for b in range(ref.shape[0])]
            out_ref[...] = jnp.concatenate(parts, axis=1)


def unlay_lanes(i, rows, v, mine_ref, twin_ref):
    blocks = mine_ref.shape[0]
    for k in range(2):

        @pl.when(i == k)
        def _():
            for b in range(2 * blocks):
                ref = (mine_ref, twin_ref)[b // blocks]
                piece = v[:, b * rows : (b + 1) * rows].astype(ref.dtype)
                ref[b % blocks, :, k * rows : (k + 1) * rows] = piece


def attend_kernel(rows, x_ref, t_ref, *refs):
    *sides, p_ref, q_ref, top_ref, pm_ref, pt_ref, s_ref = refs
    i = pl.program_id(0)
    n = x_ref.shape[1]
    wide, lanes = q_ref.shape[1:]
    lay_lanes(i, rows, sides, q_ref.at[0])
    q = q_ref[0]
    top = jnp.full((1, lanes), -jnp.inf, f32)
    for a, size in chunks(n):
        s = dot(x_ref[0, a : a + size], q, 1, 0)
        s_ref[a : a + size] = s
        top = jnp.maximum(top, jnp.max(s, axis=0, keepdims=True))
    total = jnp.zeros((wide, lanes), f32)
    for a, size in chunks(n):
        p = jnp.exp(s_ref[a : a + size] - top).astype(bf16)
        p_ref[0, a : a + size] = p
        total = total + dot(t_ref[0, :, a : a + size], p, 1, 0)
    top_ref[0] = top
    tile = total[wide - 8 :]
    at = lax.broadcasted_iota(jnp.int32, tile.shape, 0)
    sums = jnp.sum(jnp.where(at == ONE, tile, 0.0), axis=0, keepdims=True)
    stats = {ONE + j: piece for j, piece in enumerate(split3(sums))}
    stats.update({TOP + j: piece for j, piece in enumerate(split3(top))})
    tile = tail_rows(stats, lanes)
    unlay_lanes(i, rows, jnp.concatenate([total[: wide - 8], tile], axis=0), pm_ref, pt_ref)


def merge_kernel(a_ref, b_ref, keep_ref, *send_refs):
    blocks, wide, lanes = a_ref.shape
    base = wide - 8
    at = lax.broadcasted_iota(jnp.int32, (8, lanes), 0)
    for k, ref in enumerate((keep_ref, *send_refs)):
        sides = [a_ref[k], b_ref[k].astype(f32)]
        (ta, tb), (sa, sb) = (
            [jnp.sum(jnp.where((at >= r) & (at < r + 3), v[base:], 0.0), axis=0, keepdims=True) for v in sides]
            for r in (TOP, ONE)
        )
        top = jnp.maximum(ta, tb)
        wa, wb = jnp.exp(ta - top), jnp.exp(tb - top)
        v = sides[0][:base] * wa + sides[1][:base] * wb
        rows = {ONE + j: piece for j, piece in enumerate(split3(sa * wa + sb * wb))}
        rows.update({TOP + j: piece for j, piece in enumerate(split3(top))})
        ref[...] = jnp.concatenate([v, tail_rows(rows, lanes)], axis=0).astype(ref.dtype)


def mlp_forward_kernel(feats, n_got, keep_ref, *refs):
    got_refs, refs = refs[:n_got], refs[n_got:]
    x_ref, hi_ref, lo_ref, gain_ref, shift_ref, wu_ref, bu_ref, dact_ref, *outs = refs
    trio_ref, ctx_ref, lse_ref, resid_ref = outs
    wide, lanes = keep_ref.shape
    base = wide - 8
    parts = [keep_ref[...]] + [ref[...].astype(f32) for ref in got_refs]
    at = lax.broadcasted_iota(jnp.int32, (8, lanes), 0)
    tops, sums = (
        [jnp.sum(jnp.where((at >= k) & (at < k + 3), v[base:], 0.0), axis=0, keepdims=True) for v in parts]
        for k in (TOP, ONE)
    )
    peak = functools.reduce(jnp.maximum, tops)
    total = jnp.zeros((1, lanes), f32)
    ctx = jnp.zeros((wide, lanes), f32)
    for v, top, part in zip(parts, tops, sums):
        share = jnp.exp(top - peak)
        total = total + part * share
        ctx = ctx + v * share
    ctx = ctx / total
    lse_ref[...] = peak + jnp.log(total)
    row = lax.broadcasted_iota(jnp.int32, (wide, lanes), 0)
    ctx = jnp.where(row < feats, ctx, 0.0)
    ctx_ref[...] = ctx
    ctx_b = ctx.astype(bf16)
    resid = x_ref[...].astype(f32) + dot(ctx_b, hi_ref[...], 0, 0) + dot(ctx_b, lo_ref[...], 0, 0)
    resid_ref[...] = resid
    hat, _ = norm_parts(resid)
    normed = (hat * gain_ref[...] + shift_ref[...]).astype(bf16)
    trio_ref[0] = normed
    pre = dot(normed, wu_ref[...], 1, 0) + bu_ref[...]
    act_f, slope = gelu_and_slope(pre)
    trio_ref[1] = act_f.astype(bf16)
    trio_ref[2] = (dact_ref[...] * slope).astype(bf16)


def mlp_backward_kernel(trio_ref, ctx_ref, lse_ref, resid_ref, g_ref, hi_ref, lo_ref, gain_ref, wu_ref, *outs):
    dres_ref, back_ref, vector_ref = outs
    wide, lanes = ctx_ref.shape
    hat, scale = norm_parts(resid_ref[...])
    d_pre = trio_ref[2]
    d_normed = dot(d_pre, wu_ref[...], 1, 1)
    g = g_ref[...].astype(f32)
    d_resid = g + norm_back(d_normed, hat, scale, gain_ref[...])
    dres_ref[...] = d_resid
    d_resid_b = d_resid.astype(bf16)
    d_ctx = (dot(hi_ref[...], d_resid_b, 1, 1) + dot(lo_ref[...], d_resid_b, 1, 1)).astype(bf16)
    delta = jnp.sum(ctx_ref[...] * d_ctx.astype(f32), axis=0, keepdims=True)
    rows = {ONE + k: -v for k, v in enumerate(split3(delta))}
    rows.update({TOP + k: v for k, v in enumerate(split3(lse_ref[...]))})
    back_ref[...] = jnp.concatenate([d_ctx[: wide - 8], tail_rows(rows, lanes).astype(bf16)], axis=0)
    vectors = {
        0: jnp.sum(d_normed * hat, axis=0, keepdims=True),
        1: jnp.sum(d_normed, axis=0, keepdims=True),
        2: jnp.sum(d_pre.astype(f32), axis=0, keepdims=True),
        3: jnp.sum(g, axis=0, keepdims=True),
    }
    vector_ref[...] = tail_rows(vectors, g.shape[1])


def mlp_rest_kernel(trio_ref, ctx_ref, resid_ref, dres_ref, vector_ref, wd_ref, bd_ref, new_ref, csum_ref):
    base = csum_ref.shape[0] - 8
    new_ref[...] = (resid_ref[...] + dot(trio_ref[1], wd_ref[...], 1, 0) + bd_ref[...]).astype(bf16)
    csum_ref[:base] = dot(ctx_ref[...].astype(bf16), dres_ref[...].astype(bf16), 1, 0)[:base]
    csum_ref[base:] = vector_ref[...]


def back_kernel(rows, x_ref, t_ref, p_ref, top_ref, *refs):
    sides, (ds_ref, dc_ref, dm_ref, dt_ref, b_ref) = refs[:2], refs[2:]
    i = pl.program_id(0)
    pix = x_ref.shape[1]
    wide, lanes = b_ref.shape
    lay_lanes(i, rows, sides, b_ref)
    b = b_ref[...]
    tail = b[wide - 16 :].astype(f32)[8:]
    at = lax.broadcasted_iota(jnp.int32, tail.shape, 0)
    lse = jnp.sum(jnp.where((at >= TOP) & (at < TOP + 3), tail, 0.0), axis=0, keepdims=True)
    ratio = jnp.exp(top_ref[0] - lse)
    dc_ref[0] = (b.astype(f32) * ratio).astype(bf16)
    sums = jnp.zeros((wide, lanes), f32)
    for a, size in chunks(pix):
        d = dot(x_ref[0, a : a + size], b, 1, 0)
        ds = (p_ref[0, a : a + size].astype(f32) * (d * ratio)).astype(bf16)
        ds_ref[0, a : a + size] = ds
        sums = sums + dot(t_ref[0, :, a : a + size], ds, 1, 0)
    unlay_lanes(i, rows, sums, dm_ref, dt_ref)


def pixel_grad_kernel(feats, ds_ref, p_ref, q_ref, dc_ref, out_ref):
    for i in range(ds_ref.shape[0]):
        for a, size in chunks(ds_ref.shape[1]):
            rows = slice(a, a + size)
            v = dot(q_ref[i], ds_ref[i, rows], 1, 1) + dot(dc_ref[i], p_ref[i, rows], 1, 1)
            out_ref[:, i, rows] = v[:feats]


def latent_kernel(scale, n_got, cut, *refs):
    dq_refs, refs = refs[: n_got + 1], refs[n_got + 1 :]
    ctx_ref, x_ref, normed_ref, gain_ref, wk_ref, wq_ref, dres_ref, c_ref, *outs = refs
    lat_ref, *outs, dq_ref = outs
    feats = wk_ref.shape[0]
    wide, lanes = dq_ref.shape
    base = wide - 8
    dq_ref[...] = dq_refs[0][...]
    for ref in dq_refs[1:]:
        dq_ref[...] += ref[:wide].astype(f32)
    d = dq_ref[...] - dq_ref[pl.ds(base + ONE, 1)] * ctx_ref[...]
    row = lax.broadcasted_iota(jnp.int32, (wide, lanes), 0)
    d = jnp.where(row < feats, d, 0.0).astype(bf16)
    d_query = dot(d[:feats], wk_ref[...], 0, 0).astype(bf16)
    d_normed = dot(d_query, wq_ref[...], 1, 1) * scale
    hat, spread = norm_parts(x_ref[...].astype(f32))
    vectors = {
        0: jnp.sum(d_normed * hat, axis=0, keepdims=True),
        1: jnp.sum(d_normed, axis=0, keepdims=True),
    }
    both_ref = outs[-1]
    both_ref[:base] = dot(d, normed_ref[...], 1, 0)[:base]
    both_ref[base:wide] = tail_rows(vectors, both_ref.shape[1])
    both_ref[wide:] = c_ref[...]
    if cut:
        mine_ref, twin_ref = outs[:2]
        core, chip, _ = position()
        n, _, part = mine_ref.shape
        for b in range(n):
            at = (chip ^ b) * part
            mine_ref[b] = both_ref[:, slot(core * n * part + at, part)]
            twin_ref[b] = both_ref[:, slot((1 - core) * n * part + at, part)].astype(bf16)
    lat_ref[...] = dres_ref[...] + norm_back(d_normed, hat, spread, gain_ref[...])


def halves_kernel(*refs):
    mine_ref, other_ref = refs[-2:]
    core, half = position()[0], mine_ref.shape[2]
    for j, ref in enumerate(refs[:-2]):
        mine_ref[j] = ref[:, slot(core * half, half)]
        other_ref[j] = ref[:, slot((1 - core) * half, half)]


def up_kernel(n, trio_ref, twin_ref, back_ref, *refs):
    core, chip, z = position()
    up_refs, act_refs = refs[:n], refs[n:]
    tall, half = up_refs[0].shape
    part = up_refs[1].shape[1]
    cols = slot(core * half, half)
    slab = act_refs[0].shape[1]
    for j, ref in enumerate(act_refs):
        rows = slot(lax.rem(z + j, len(act_refs)) * slab, slab)
        ref[...] = jnp.concatenate([trio_ref[1, :, rows], twin_ref[1, :, rows]], axis=0)
    d_pre = jnp.concatenate([trio_ref[2, :, cols], twin_ref[2, :, cols]], axis=0)
    for m, ref in enumerate(up_refs):
        rows = slot((chip ^ m) * tall, tall)
        normed = jnp.concatenate([trio_ref[0, :, rows], twin_ref[0, :, rows]], axis=0)
        v = dot(normed, d_pre, 0, 0)
        if m == 0:
            ref[...] = v
        else:
            for q in range(half // part):
                ref[q * tall : (q + 1) * tall] = v[:, q * part : (q + 1) * part].astype(bf16)
            ref[half // part * tall :] = back_ref[...]


def part_kernel(n, *refs):
    back_ref, up_ref, *got_refs = refs[: n + 1]
    sides_ref, sum_ref = refs[n + 1 :]
    tall, half = up_ref.shape
    wide, part = back_ref.shape
    base = got_refs[0].shape[0] - wide
    sides_ref[0] = back_ref[...]
    for m, ref in enumerate(got_refs, 1):
        sides_ref[m] = ref[base:]
    for q in range(half // part):
        cols = slice(q * part, (q + 1) * part)
        v = up_ref[:, cols]
        for ref in got_refs:
            v = v + ref[q * tall : (q + 1) * tall].astype(f32)
        sum_ref[:, cols] = v


def total(refs):
    v = refs[0][...].astype(f32)
    for ref in refs[1:]:
        v = v + ref[...].astype(f32)
    return v


def split_kernel(sum_ref, *out_refs):
    z = position()[2]
    size = out_refs[0].shape[0]
    for j, ref in enumerate(out_refs):
        ref[...] = sum_ref[slot(lax.rem(z + j, len(out_refs)) * size, size)].astype(ref.dtype)


def fold_kernel(n, mine_ref, twin_ref, keep_ref, *out_refs):
    keep_ref[...] = mine_ref[0] + twin_ref[0].astype(f32)
    for m, ref in enumerate(out_refs, 1):
        ref[...] = (mine_ref[m] + twin_ref[m].astype(f32)).astype(bf16)


def fold_down_kernel(n_batch, mine_ref, twin_ref, g_ref, g2_ref, *refs):
    act_refs, refs = refs[:n_batch], refs[n_batch:]
    keep_ref, own_ref, *send_refs, sum_ref = refs
    chip = position()[1]
    base, part = keep_ref.shape
    size = own_ref.shape[0]
    act = jnp.concatenate([ref[...] for ref in act_refs], axis=0)
    g = jnp.concatenate([ref[j] for j in range(n_batch) for ref in (g_ref, g2_ref)], axis=0)
    sum_ref[...] = dot(act, g, 0, 0)
    keep_ref[...] = mine_ref[0] + twin_ref[0].astype(f32)
    own_ref[...] = sum_ref[slot(chip * size, size)]
    for m, ref in enumerate(send_refs, 1):
        ref[:base] = (mine_ref[m] + twin_ref[m].astype(f32)).astype(bf16)
        v = sum_ref[slot((chip ^ m) * size, size)].astype(bf16)
        for q in range(v.shape[1] // part):
            ref[base + q * size : base + (q + 1) * size] = v[:, q * part : (q + 1) * part]


def unfold_kernel(own_ref, *refs):
    got_refs, out_ref = refs[:-1], refs[-1]
    size, half = own_ref.shape
    part = got_refs[0].shape[1]
    base = got_refs[0].shape[0] - size * (half // part)
    for q in range(half // part):
        cols = slice(q * part, (q + 1) * part)
        v = own_ref[:, cols]
        for ref in got_refs:
            v = v + ref[base + q * size : base + (q + 1) * size].astype(f32)
        out_ref[:, cols] = v.astype(bf16)


def add_kernel(*refs):
    refs[-1][...] = total(refs[:-1]).astype(refs[-1].dtype)


def stack_kernel(*refs):
    for j, ref in enumerate(refs[:-1]):
        refs[-1][j] = ref[...]


def forward_kernel(x_ref, y_ref, low_ref, high_ref):
    half = low_ref.shape[0]
    low_ref[...] = x_ref[:half]
    high_ref[...] = y_ref[half:]


def place_kernel(masks, firsts, n_old, *refs):
    n = len(masks)
    core, chip, z = position()
    pieces, (up_ref, down_ref, held_ref, sems) = refs[: 2 * n], refs[2 * n + n_old :]
    half = up_ref.shape[1] // 2
    n_batch = up_ref.shape[0] // (4 * held_ref.shape[1])
    size = held_ref.shape[1]
    copies = []
    for i, (m, first) in enumerate(zip(masks, firsts)):
        for j in range(pieces[i].shape[0]):
            k, z_at = chip ^ m, z ^ z_masks(n_batch)[first + j]
            for h, (out_ref, row) in enumerate(((up_ref, k * n_batch + z_at), (down_ref, z_at * 4 + k))):
                at = len(copies)
                for side, col in enumerate((core, 1 - core)):
                    held_ref[at, :, slot(col * half, half)] = pieces[side * n + i][j, h].astype(f32)
                copy = pltpu.make_async_copy(held_ref.at[at], out_ref.at[slot(row * size, size)], sems.at[at])
                copy.start()
                copies.append(copy)
    for copy in copies:
        copy.wait()


def final_kernel(scale, n, *refs):
    pieces, refs = refs[: 1 + (n > 0)], refs[1 + (n > 0) :]
    wq_ref, wk_ref, wv_ref, wo_ref, *out_refs, both_ref, tall_ref, flat_ref, sems = refs
    vector_refs, out_refs = out_refs[:6], out_refs[6:]
    feats, width = wk_ref.shape
    wide = both_ref.shape[0] // 2
    steps = tall_ref.shape[1]
    tall = width // steps
    if n == 0:
        both_ref[...] = pieces[0][...].astype(bf16)
    else:
        core, chip, _ = position()
        for side, col in enumerate((core, 1 - core)):
            part = pieces[side].shape[2]
            for b in range(n):
                both_ref[:, slot(col * n * part + (chip ^ b) * part, part)] = pieces[side][b]
    for k, ref in enumerate(vector_refs):
        base, at = (wide, k) if k < 2 else (2 * wide, k - 2)
        ref[...] = both_ref[base - 16 : base].astype(f32)[8 + at : 9 + at]
    copies = []
    for h, (base, w_ref) in enumerate(((0, wk_ref), (wide, wv_ref))):
        for j in range(steps):
            rows = slice(j * tall, (j + 1) * tall)
            if h == 0:
                v = dot(both_ref[:wide, rows][:feats], w_ref[...], 0, 0) * scale
            else:
                v = dot(w_ref[:, rows], both_ref[wide:][:feats], 0, 0)
            tall_ref[h, j] = v
            copies.append(pltpu.make_async_copy(tall_ref.at[h, j], out_refs[h].at[rows], sems.at[len(copies)]))
            copies[-1].start()
    for h in range(2):
        if h == 0:
            v = dot(both_ref[:wide], wq_ref[...], 1, 0) * scale
        else:
            v = dot(both_ref[wide:], wo_ref[...], 1, 1)
        flat_ref[h] = v[:feats]
        copies.append(pltpu.make_async_copy(flat_ref.at[h], out_refs[2 + h], sems.at[len(copies)]))
        copies[-1].start()
    for copy in copies:
        copy.wait()


def seq_send(v, mask, n):
    return lax.ppermute(v, "seq", [(i, i ^ mask) for i in range(n)])


def batch_send(v, shift, n):
    return lax.ppermute(v, "batch", [(i, (i + shift) % n) for i in range(n)])


def z_masks(n):
    masks = [0]
    while len(masks) < n:
        masks = masks + [m ^ (2 * len(masks) - 1) for m in masks]
    return masks


class Comm:
    def __init__(self, n_seq, n_batch):
        self.n_seq, self.n_batch = n_seq, n_batch
        self.chips = n_seq // 2

    def twin(self, v):
        return seq_send(v, 1, self.n_seq)

    def swap_chip(self, v, mask):
        return seq_send(v, 2 * mask, self.n_seq)

    def to_chips(self, pieces):
        return [seq_send(v, 2 * m, self.n_seq) for m, v in enumerate(pieces, 1)]

    def to_z(self, pieces):
        n = self.n_batch
        order = sorted(range(1, n), key=lambda j: -min(j, n - j))
        got = {j: batch_send(pieces[j - 1], j, n) for j in order}
        return [got[j] for j in range(1, n)]

    def next_z(self, v):
        return batch_send(v, 1, self.n_batch)

    def sum_z(self, v):
        mask = 1
        while mask < self.n_batch:
            pairs = [(i, i ^ (2 * mask - 1)) for i in range(self.n_batch)]
            other = lax.ppermute(v, "batch", pairs)
            v = call(add_kernel, shape(v.shape, v.dtype))(v, other)
            mask *= 2
        return v

    def all_z(self, v):
        got = [v]
        while len(got) < self.n_batch:
            pairs = [(i, i ^ (2 * len(got) - 1)) for i in range(self.n_batch)]
            got = got + [lax.ppermute(piece, "batch", pairs) for piece in got]
        return got

    def all_chips(self, v):
        return [v] + self.to_chips([v] * (self.chips - 1))

    def spread(self, v, beside):
        mine, beside = tie(self.all_chips(v), beside)
        mine = call(stack_kernel, shape((self.chips, *v.shape), v.dtype))(*mine)
        return [mine, self.twin(mine)], beside


def tie(first, second):
    out = lax.optimization_barrier((*first, *second))
    return list(out[: len(first)]), list(out[len(first) :])


def add_all(first, rest):
    for v in rest:
        first = first + v.astype(f32)
    return first


def shards(
    n_seq,
    n_batch,
    latents,
    pixels,
    keep_mask,
    gain_attn,
    shift_attn,
    w_query,
    w_key,
    w_value,
    w_out,
    gain_mlp,
    shift_mlp,
    w_up,
    bias_up,
    w_down,
    bias_down,
    cotangent,
):
    images, rows, width = latents.shape
    pix, feats = pixels.shape[1:]
    hidden = w_up.shape[1]
    wide = -(-(feats + 8) // 16) * 16
    lanes = images * rows
    scale = width ** (-0.5)
    comm = Comm(n_seq, n_batch)
    blocks = comm.chips
    every = n_seq * rows
    x = latents.reshape(lanes, width)
    g = cotangent.reshape(lanes, width)
    gain1, shift1, gain2, shift2, b_up, b_down = (
        v.reshape(1, -1) for v in (gain_attn, shift_attn, gain_mlp, shift_mlp, bias_up, bias_down)
    )
    small = (blocks, wide, lanes)

    operands = (x, gain1, shift1, w_query, w_key)
    qk, normed = call(
        functools.partial(query_kernel, scale),
        [shape((wide, lanes), bf16), shape((lanes, width), bf16)],
        ins=[pl.BlockSpec(memory_space=pltpu.HBM)] * 5,
        scratch=[pltpu.VMEM(v.shape, v.dtype) for v in operands]
        + [pltpu.VMEM((wide, lanes), f32), pltpu.SemaphoreType.DMA((8,))],
        limit=60 << 20,
    )(*operands)

    pix_x, pix_t = call(
        pixel_kernel,
        [shape((images, pix, wide), bf16), shape((images, wide, pix), bf16)],
        grid=(images,),
        ins=[one_of((feats, pix)), whole((images, pix))],
        outs=[one_of((pix, wide)), one_of((wide, pix))],
        scratch=[pltpu.VMEM((wide, pix), f32)],
    )(pixels.transpose(0, 2, 1), keep_mask)
    (qk,), g_all = tie([qk], [g])
    g_all.append(comm.next_z(g_all[0]))
    q_sides, (pix_x, g_all[1]) = comm.spread(qk, [pix_x, g_all[1]])
    vo_hi, vo_lo, d_act = call(
        weight_kernel,
        [shape((wide, width), bf16)] * 2 + [shape((lanes, hidden), f32)],
        scratch=[pltpu.VMEM((wide, width), f32)],
    )(w_value, w_out, g, w_down)

    probs, q_all, top, part_mine, part_twin = call(
        functools.partial(attend_kernel, rows),
        [
            shape((images, pix, every), bf16),
            shape((images, wide, every), bf16),
            shape((images, 1, every), f32),
            shape(small, f32),
            shape(small, bf16),
        ],
        grid=(images,),
        ins=[one_of((pix, wide)), one_of((wide, pix))] + [whole(small)] * 2,
        outs=[one_of((pix, every)), one_of((wide, every)), one_of((1, every)), whole(small), whole(small)],
        scratch=[pltpu.VMEM((pix, every), f32)],
    )(pix_x, pix_t, *q_sides)
    keep, *send = call(
        merge_kernel, [shape((wide, lanes), f32)] + [shape((wide, lanes), bf16)] * (blocks - 1)
    )(
        part_mine, comm.twin(part_twin)
    )
    g_next = comm.next_z(g_all[-1])
    got = comm.to_chips(send)

    trio, ctx, lse, resid = call(
        functools.partial(mlp_forward_kernel, feats, blocks - 1),
        [
            shape((3, lanes, width), bf16),
            shape((wide, lanes), f32),
            shape((1, lanes), f32),
            shape((lanes, width), f32),
        ],
    )(keep, *got, x, vo_hi, vo_lo, gain2, shift2, w_up, b_up, d_act)
    (trio_sent,), (g_next,) = tie([trio], [g_next])
    g_all.append(g_next)
    d_resid, back, vector_rows = call(
        mlp_backward_kernel,
        [shape((lanes, width), f32), shape((wide, lanes), bf16), shape((8, width), f32)],
    )(trio, ctx, lse, resid, g, vo_hi, vo_lo, gain2, w_up)
    new_latents, c_part = call(mlp_rest_kernel, [shape((lanes, width), bf16), shape((wide, width), f32)])(
        trio, ctx, resid, d_resid, vector_rows, w_down, b_down
    )

    half = width // 2
    part = half // blocks
    quarter, tall, size = width // blocks, width // n_batch, width // blocks // n_batch
    cut = part == lanes and part % 128 == 0 and size % 16 == 0 and blocks == 4 and n_batch == 4
    tall = hidden // n_batch
    if cut:
        up = call(
            functools.partial(up_kernel, blocks),
            [shape((quarter, half), f32)]
            + [shape((blocks * quarter + wide, part), bf16)] * (blocks - 1)
            + [shape((2 * lanes, tall), bf16)] * n_batch,
        )(trio, comm.twin(trio_sent), back)
        up, act = list(up[:blocks]), list(up[blocks:])
        for _ in range(3, n_batch):
            g_all.append(comm.next_z(g_all[-1]))
        up[1:] = comm.to_chips(up[1:])
        act[1:] = comm.to_z(act[1:])
        up, (new_latents, c_part, *rest) = tie(up, [new_latents, c_part, *act, *g_all[3:]])
        act, g_all[3:] = rest[:n_batch], rest[n_batch:]
        sides, up = call(
            functools.partial(part_kernel, blocks), [shape(small, bf16), shape((quarter, half), f32)]
        )(back, *up)
        back_sides = [sides, comm.twin(sides)]
        g_mine, g_twin = call(halves_kernel, [shape((n_batch, lanes, half), bf16)] * 2)(*g_all)
        g_twin = comm.twin(g_twin)
    else:
        back_sides, _ = comm.spread(back, [])
    d_scores, d_ctx_all, dq_mine, dq_twin = call(
        functools.partial(back_kernel, rows),
        [
            shape((images, pix, every), bf16),
            shape((images, wide, every), bf16),
            shape(small, f32),
            shape(small, bf16),
        ],
        grid=(images,),
        ins=[one_of((pix, wide)), one_of((wide, pix)), one_of((pix, every)), one_of((1, every))]
        + [whole(small)] * 2,
        outs=[one_of((pix, every)), one_of((wide, every)), whole(small), whole(small)],
        scratch=[pltpu.VMEM((wide, every), bf16)],
    )(pix_x, pix_t, probs, top, *back_sides)

    pixel_grad = call(
        functools.partial(pixel_grad_kernel, feats), shape((feats, images, pix), f32)
    )(d_scores, probs, q_all, d_ctx_all)

    def place(masks, firsts, pieces, old=()):
        count = 2 * sum(v.shape[0] for v in pieces)
        hbm, vmem = pl.BlockSpec(memory_space=pltpu.HBM), pl.BlockSpec(memory_space=pltpu.VMEM)
        return list(
            pl.pallas_call(
                functools.partial(place_kernel, masks, firsts, len(old)),
                out_shape=[shape((width, width), f32)] * 2,
                in_specs=[vmem] * (2 * len(pieces)) + [hbm] * len(old),
                out_specs=[hbm] * 2,
                scratch_shapes=[pltpu.VMEM((count, size, width), f32), pltpu.SemaphoreType.DMA((count,))],
                input_output_aliases={2 * len(pieces) + i: i for i in range(len(old))},
                compiler_params=pltpu.CompilerParams(vmem_limit_bytes=VMEM_LIMIT),
            )(*pieces, *map(comm.twin, pieces), *old)
        )

    def folded(mine, twin):
        return call(
            functools.partial(fold_kernel, blocks),
            [shape(mine.shape[1:], f32)] + [shape(mine.shape[1:], bf16)] * (blocks - 1),
        )(mine, comm.twin(twin))

    if cut:
        first, down, *rest = call(
            functools.partial(fold_down_kernel, n_batch),
            [shape((wide, lanes), f32), shape((size, half), f32)]
            + [shape((wide + blocks * size, lanes), bf16)] * (blocks - 1),
            scratch=[pltpu.VMEM((tall, half), f32)],
        )(dq_mine, comm.twin(dq_twin), g_mine, g_twin, *act)
        up_keep, *up_send = call(
            split_kernel, [shape((size, half), f32)] + [shape((size, half), bf16)] * (n_batch - 1)
        )(up)
        up = [up_keep] + comm.to_z(up_send)
        dq = [first] + comm.to_chips(rest)
    else:
        first, *rest = folded(dq_mine, dq_twin)
        dq = [first] + comm.to_chips(rest)
    latent_grad, *both = call(
        functools.partial(latent_kernel, scale, blocks - 1, cut),
        [shape((lanes, width), f32)]
        + [shape((blocks, 2 * wide, part), f32), shape((blocks, 2 * wide, part), bf16)] * cut
        + [shape((2 * wide, width), f32)] * (not cut),
        scratch=[pltpu.VMEM((2 * wide, width), f32)] * cut + [pltpu.VMEM((wide, lanes), f32)],
    )(*dq, ctx, x, normed, gain1, w_key, w_query, d_resid, c_part)
    if cut:
        both, up = tie(both, up)
        first, *rest = folded(*both)
        up = call(add_kernel, shape((size, half), bf16))(*up)
        down = call(unfold_kernel, shape((size, half), bf16))(down, *dq[1:])
        own = call(stack_kernel, shape((2, size, half), bf16))(up, down)
        sums, (pixel_grad, *own) = tie([first] + comm.to_chips(rest), [pixel_grad, *comm.all_z(own)])
        own = call(stack_kernel, shape((n_batch, 2, size, half), bf16))(*own)
        sums = call(add_kernel, shape((2 * wide, part), bf16))(*sums)
        own = [own] + [comm.swap_chip(own, m) for m in (1, 2)]
        (sums,), own = tie([comm.sum_z(sums)], own)
        low, high = call(forward_kernel, [shape((n_batch // 2, 2, size, half), bf16)] * 2)(*own[1:])
        far = [comm.swap_chip(low, 2), comm.swap_chip(high, 1)]
        grads = place((0, 1, 2), (0, 0, 0), own)
        pieces, (*far, grads[0], grads[1]) = tie(comm.all_chips(sums), [*far, *grads])
        pieces = call(stack_kernel, shape((blocks, 2 * wide, part), bf16))(*pieces)
        pieces = [pieces, comm.twin(pieces)]
    else:
        pieces = [lax.psum(both[0], ("batch", "seq"))]
    steps = 4
    hbm, vmem = pl.BlockSpec(memory_space=pltpu.HBM), pl.BlockSpec(memory_space=pltpu.VMEM)
    *vectors, grad_query, grad_out, grad_key, grad_value = pl.pallas_call(
        functools.partial(final_kernel, scale, blocks if cut else 0),
        out_shape=[shape((1, width), f32)] * 6 + [shape((width, width), f32)] * 2 + [shape((feats, width), f32)] * 2,
        in_specs=[vmem] * (len(pieces) + 4),
        out_specs=[vmem] * 6 + [hbm] * 4,
        scratch_shapes=[
            pltpu.VMEM((2 * wide, width), bf16),
            pltpu.VMEM((2, steps, width // steps, width), f32),
            pltpu.VMEM((2, feats, width), f32),
            pltpu.SemaphoreType.DMA((2 * steps + 2,)),
        ],
        compiler_params=pltpu.CompilerParams(vmem_limit_bytes=24 << 20),
    )(*pieces, w_query, w_key, w_value, w_out)
    if cut:
        grads[:1], vectors[:1] = tie(grads[:1], vectors[:1])
        grad_up, grad_down = place((3, 3), (0, n_batch // 2), far, grads)
    vectors = [v.reshape(width) for v in vectors]
    if not cut:
        grad_up = lax.psum(dot(trio[0], trio[2], 0, 0), ("batch", "seq"))
        grad_down = lax.psum(dot(trio[1], g, 0, 0), ("batch", "seq"))
    dims = (images, rows, width)
    return (
        new_latents.reshape(dims),
        latent_grad.reshape(dims),
        pixel_grad.transpose(1, 2, 0),
        vectors[0],
        vectors[1],
        grad_query,
        grad_key,
        grad_value,
        grad_out,
        vectors[2],
        vectors[3],
        grad_up,
        vectors[4],
        grad_down,
        vectors[5],
    )


def solution(mesh):
    split = P("batch", "seq", None)
    placed = (split, split, P("batch", "seq")) + (P(),) * 12 + (split,)
    return jax.shard_map(
        functools.partial(shards, mesh.shape["seq"], mesh.shape["batch"]),
        mesh=mesh,
        in_specs=placed,
        out_specs=(split, split, split) + (P(),) * 12,
        check_vma=False,
    )
```
